32 devices in a mesh: dp: 16 (over z, x, core), tensor: 2 (over y).
Axes of the slice: x: 2, y: 2, z: 4, core: 2. Of those that a mesh axis runs over, the one named last changes fastest.
Arguments:
- x_in: float32 [16384, 768], P(('dp', 'tensor')), may hold values from -6 to 6
- lengths: int32 [16, 3], P('dp'), may hold values from 1 to 682, 1024 in all within a row
- token_ids: int32 [16384], P(('dp', 'tensor')), may hold values from 0 to 69
- ln1_gain: float32 [2, 768], replicated, may hold values from 0.1 to 1.9
- ln1_bias: float32 [2, 768], replicated, may hold values from -1.5 to 1.5
- w_qkv: bfloat16 [2, 768, 3, 768], P(None, None, None, 'tensor'), may hold values from -0.21875 to 0.21875
- b_qkv: float32 [2, 3, 768], P(None, None, 'tensor'), may hold values from -2.5 to 2.5
- w_out: bfloat16 [2, 768, 768], P(None, 'tensor'), may hold values from -2 to 2
- b_out: float32 [2, 768], replicated, may hold values from -2.5 to 2.5
- ln2_gain: float32 [2, 768], replicated, may hold values from 0.1 to 1.9
- ln2_bias: float32 [2, 768], replicated, may hold values from -1.5 to 1.5
- w_up: bfloat16 [2, 768, 3072], P(None, None, 'tensor'), may hold values from -0.21875 to 0.21875
- b_up: float32 [2, 3072], P(None, 'tensor'), may hold values from -2.5 to 2.5
- w_down: bfloat16 [2, 3072, 768], P(None, 'tensor'), may hold values from -0.109375 to 0.109375
- b_down: float32 [2, 768], replicated, may hold values from -2.5 to 2.5
- head: bfloat16 [768, 70], replicated, may hold values from -0.21875 to 0.21875
- class_bins: int32 [70], replicated, may hold values from 0 to 23
- cotangent: float32 [16384, 768], P(('dp', 'tensor')), may hold values from -6 to 6
Outputs:
- out_act: float32 [16384, 768], P(('dp', 'tensor'))
- grad_x: float32 [16384, 768], P(('dp', 'tensor'))
- grad_ln1_gain: float32 [2, 768], replicated
- grad_ln1_bias: float32 [2, 768], replicated
- grad_w_qkv: float32 [2, 768, 3, 768], P(None, 'dp', None, 'tensor')
- grad_b_qkv: float32 [2, 3, 768], P(None, None, 'tensor')
- grad_w_out: float32 [2, 768, 768], P(None, 'tensor', 'dp')
- grad_b_out: float32 [2, 768], replicated
- grad_ln2_gain: float32 [2, 768], replicated
- grad_ln2_bias: float32 [2, 768], replicated
- grad_w_up: float32 [2, 768, 3072], P(None, 'dp', 'tensor')
- grad_b_up: float32 [2, 3072], P(None, 'tensor')
- grad_w_down: float32 [2, 3072, 768], P(None, 'tensor', 'dp')
- grad_b_down: float32 [2, 768], replicated
- bin_density: float32 [24], replicated
- token_count: int32 [], replicated
The draws below stay inside these ranges and needn't reach their ends.
Inputs may be any that keep to these rules, and one draw needn't show every extreme that they name: `lengths`: each row sums to 1024, and its largest length is exactly 682. `token_ids`: ids 0 to 4 are special tokens, the others codons.
All inputs are finite; a program needn't handle non-finite values.
Results may differ from the reference program's by a relative error of at most 0.028.
Values may be sent and summed in bfloat16 or wider, within the bound.
No kernel may reach another device: no remote copies, remote signals or barrier semaphores. Data moves between devices by JAX's collectives and lax.ppermute only.
A program may use at most 192 MiB of HBM per device.

```python
import math
import jax
import jax.numpy as jnp
import numpy as np
from jax import lax

D = 768
HEADS = 12
HEAD_DIM = 64
FF = 3072
CLASSES = 70
LAYERS = 2
SEGS = 3
BINS = 24
GROUP = 1024
LONG = 682
TOKENS = 16384
N_DP = 16


def touch_ends(array, own_key, low, top_value):
    dims = array.shape
    place = [jax.random.randint(jax.random.fold_in(own_key, axis), (), 0, dims[axis]) for axis in range(len(dims))]
    array = array.at[tuple(place)].set(low)
    longest = dims.index(max(dims))
    place[longest] = (place[longest] + 1) % dims[longest]
    return array.at[tuple(place)].set(top_value)


def levels(rng, extent, pieces, least, largest):
    level = 1.0
    for dim, shards_of in pieces:
        draws = jax.random.uniform(jax.random.fold_in(jax.random.fold_in(rng, 6), dim), (shards_of,), jnp.float32, least / len(pieces), largest / len(pieces))
        level = level * jnp.repeat(jnp.exp(draws), extent[dim] // shards_of).reshape((-1,) + (1,) * (len(extent) - 1 - dim))
    return level


def split_up(count, total, reach, skew):
    portions = [(1 << 20) // math.isqrt(rank ** skew) + 1 for rank in range(2, count + 1)]
    surplus, given = total - reach - (count - 1), [1] * (count - 1)
    while surplus > 0:
        free = [i for i in range(count - 1) if given[i] < reach]
        whole, left = sum([portions[i] for i in free]), surplus
        for i in free:
            more = min(reach - given[i], max(1, left * portions[i] // whole), surplus)
            given[i] = given[i] + more
            surplus = surplus - more
    return np.array([reach] + given)


def ragged(rng, count, total, bound, slope):
    if count == 2:
        one = jax.random.randint(rng, (), max(1, total - bound), min(bound, total - 1) + 1)
        return jnp.stack([one, total - one])
    tallies = jnp.asarray(split_up(count, total, bound, slope), jnp.int32)
    twos = (count - 1) // 2
    giver, sink = tallies[1:1 + 2 * twos:2], tallies[2:2 + 2 * twos:2]
    room = jnp.minimum(giver - 1, bound - sink)
    shifted = jax.random.randint(jax.random.fold_in(rng, 1), (twos,), 0, 1 << 20) % (room + 1)
    tallies = tallies.at[1:1 + 2 * twos:2].set(giver - shifted).at[2:2 + 2 * twos:2].set(sink + shifted)
    return tallies[jax.random.permutation(jax.random.fold_in(rng, 2), count)]


def bell_draw(stream_key, shape, width, most, pieces=(), held_as=jnp.bfloat16):
    level = levels(stream_key, shape, pieces, -0.22, 0.18) if pieces else 1.0
    array = jax.random.normal(stream_key, shape, jnp.float32) * width * level
    return jnp.minimum(jnp.maximum(array, -most), most).astype(held_as)


def setup_inputs(seed: int = 0) -> dict:
    key_list = jax.random.split(jax.random.key(seed), 19)
    x_in = bell_draw(key_list[0], (TOKENS, D), 1.0, 6.0, ((0, 32),), jnp.float32)
    lengths = jax.vmap(lambda own: ragged(own, SEGS, GROUP, LONG, 2))(jax.random.split(key_list[1], N_DP)).reshape((N_DP, SEGS)).astype(jnp.int32)
    token_ids = touch_ends(jax.random.randint(key_list[2], (TOKENS,), 0, CLASSES), jax.random.fold_in(key_list[2], 1), 0, CLASSES - 1).astype(jnp.int32)
    ln1_gain = jnp.clip(1.0 + 0.18 * jax.random.normal(key_list[3], (LAYERS, D), jnp.float32), 0.1, 1.9)
    ln1_bias = bell_draw(key_list[4], (LAYERS, D), 0.3, 1.5, (), jnp.float32)
    w_qkv = bell_draw(key_list[5], (LAYERS, D, 3, D), D ** -0.5, 0.21875, ((3, 2),))
    b_qkv = bell_draw(key_list[6], (LAYERS, 3, D), 0.5, 2.5, ((2, 2),), jnp.float32)
    w_out = bell_draw(key_list[7], (LAYERS, D, D), 8 ** -0.5, 2.0, ((1, 2),))
    b_out = bell_draw(key_list[8], (LAYERS, D), 0.5, 2.5, (), jnp.float32)
    ln2_gain = jnp.clip(1.0 + 0.18 * jax.random.normal(key_list[9], (LAYERS, D), jnp.float32), 0.1, 1.9)
    ln2_bias = bell_draw(key_list[10], (LAYERS, D), 0.3, 1.5, (), jnp.float32)
    w_up = bell_draw(key_list[11], (LAYERS, D, FF), D ** -0.5, 0.21875, ((2, 2),))
    b_up = bell_draw(key_list[12], (LAYERS, FF), 0.5, 2.5, ((1, 2),), jnp.float32)
    w_down = bell_draw(key_list[13], (LAYERS, FF, D), FF ** -0.5, 0.109375, ((1, 2),))
    b_down = bell_draw(key_list[14], (LAYERS, D), 0.5, 2.5, (), jnp.float32)
    head = bell_draw(key_list[15], (D, CLASSES), D ** -0.5, 0.21875)
    class_bins = touch_ends(jax.random.randint(key_list[16], (CLASSES,), 0, BINS), jax.random.fold_in(key_list[16], 1), 0, BINS - 1).astype(jnp.int32)
    cotangent = bell_draw(key_list[17], (TOKENS, D), 1.0, 6.0, ((0, 32),), jnp.float32)
    return dict(x_in=x_in, lengths=lengths, token_ids=token_ids, ln1_gain=ln1_gain, ln1_bias=ln1_bias, w_qkv=w_qkv, b_qkv=b_qkv, w_out=w_out, b_out=b_out, ln2_gain=ln2_gain, ln2_bias=ln2_bias, w_up=w_up, b_up=b_up, w_down=w_down, b_down=b_down, head=head, class_bins=class_bins, cotangent=cotangent)


highest = lax.Precision.HIGHEST
eps = 1e-05
theta = 10000.0
special_ids = 5

@jax.custom_vjp
def low(v):
    return lax.optimization_barrier(v.astype(jnp.bfloat16)).astype(jnp.float32)

@jax.custom_vjp
def low_back(v):
    return v

def low_keep(v):
    return (low(v), None)

def low_pass(kept, grad):
    return (grad,)

def back_keep(v):
    return (v, None)

def back_low(kept, grad):
    return (low(grad),)
low.defvjp(low_keep, low_pass)
low_back.defvjp(back_keep, back_low)

def layer_norm(rows, gain, bias):
    centre = rows - lax.optimization_barrier(jnp.mean(rows, axis=-1, keepdims=True))
    spread = lax.optimization_barrier(jnp.mean(centre * centre, axis=-1, keepdims=True))
    return centre * lax.rsqrt(spread + eps) * gain + bias

def segment_info(seq_lengths, total):
    ends = jnp.cumsum(seq_lengths).astype(jnp.int32)
    places = jnp.arange(total, dtype=jnp.int32)
    labels = lax.optimization_barrier(jnp.sum((places[:, None] >= ends[None, :-1]).astype(jnp.int32), axis=1)).astype(jnp.int32)
    starts = (ends - seq_lengths).astype(jnp.int32)
    picks = labels[:, None] == jnp.arange(seq_lengths.shape[0], dtype=jnp.int32)[None, :]
    begin = lax.optimization_barrier(jnp.sum(jnp.where(picks, starts[None, :], 0), axis=1)).astype(jnp.int32)
    return (labels, (places - begin).astype(jnp.int32))

def rotary(features, places):
    half = features.shape[-1] // 2
    freqs = theta ** (-jnp.arange(half, dtype=jnp.float32) / half)
    angles = places.astype(jnp.float32)[:, None] * freqs[None, :]
    cosine = jnp.cos(angles)[:, None, :]
    sine = jnp.sin(angles)[:, None, :]
    first = features[..., :half]
    second = features[..., half:]
    return jnp.concatenate([first * cosine - second * sine, second * cosine + first * sine], axis=-1)

def attend(queries, keys, values, labels):
    total = queries.shape[0]
    block = min(512, total)

    def one_block(start):
        query_rows = lax.dynamic_slice_in_dim(queries, start, block, 0)
        label_rows = lax.dynamic_slice_in_dim(labels, start, block, 0)
        scores = low_back(jnp.einsum('qhe,khe->hqk', query_rows, keys, precision=highest))
        same = (label_rows[:, None] == labels[None, :])[None]
        scores = jnp.where(same, scores, -1e+30)
        probs = jax.nn.softmax(scores, axis=-1)
        return jnp.einsum('hqk,khe->qhe', low(probs), values, precision=highest)
    starts = jnp.arange(total // block, dtype=jnp.int32) * block
    result = lax.map(jax.checkpoint(one_block), starts)
    return result.reshape(total, queries.shape[1], queries.shape[2])

def layer(stream, weights, labels, places):
    ln1_gain, ln1_bias, w_qkv, b_qkv, w_out, b_out, ln2_gain, ln2_bias, w_up, b_up, w_down, b_down = weights
    total = stream.shape[0]
    normed = low(layer_norm(stream, ln1_gain, ln1_bias))
    mixed = low_back(jnp.dot(normed, w_qkv.reshape(D, 3 * D), precision=highest) + b_qkv.reshape(3 * D))
    mixed = mixed.reshape(total, 3, HEADS, HEAD_DIM)
    queries = low(rotary(mixed[:, 0], places) * HEAD_DIM ** (-0.5))
    keys = low(rotary(mixed[:, 1], places))
    values = low(mixed[:, 2])
    attended = low_back(low(attend(queries, keys, values, labels).reshape(total, D)))
    middle = stream + low_back(jnp.dot(attended, w_out, precision=highest)) + b_out
    normed_ffn = low(layer_norm(middle, ln2_gain, ln2_bias))
    hidden = low_back(jnp.dot(normed_ffn, w_up, precision=highest) + b_up)
    active = low(jax.nn.gelu(hidden, approximate=False))
    return middle + low_back(jnp.dot(active, w_down, precision=highest)) + b_down

def reference(x_in, lengths, token_ids, ln1_gain, ln1_bias, w_qkv, b_qkv, w_out, b_out, ln2_gain, ln2_bias, w_up, b_up, w_down, b_down, head, class_bins, cotangent):
    weights = tuple((w.astype(jnp.float32) for w in (ln1_gain, ln1_bias, w_qkv, b_qkv, w_out, b_out, ln2_gain, ln2_bias, w_up, b_up, w_down, b_down)))
    head_table = head.astype(jnp.float32)
    data_mask = (token_ids >= special_ids).astype(jnp.float32)
    bin_table = (class_bins[:, None] == jnp.arange(BINS, dtype=jnp.int32)[None, :]).astype(jnp.float32)

    def forward(params, inputs):

        def group(pair):
            stream, seq_lengths = pair
            labels, places = segment_info(seq_lengths, GROUP)
            for number in range(LAYERS):
                stream = layer(stream, tuple((w[number] for w in params)), labels, places)
            return stream
        result = lax.map(jax.checkpoint(group), (inputs.reshape(N_DP, GROUP, D), lengths))
        result = result.reshape(N_DP * GROUP, D)
        logits = jnp.dot(low(result), head_table, precision=highest)
        class_probs = jax.nn.softmax(logits, axis=-1)
        class_sums = lax.optimization_barrier(jnp.sum(class_probs * data_mask[:, None], axis=0))
        totals = jnp.dot(class_sums, bin_table, precision=highest)
        return (result, totals)
    out_act, pull, totals = jax.vjp(forward, weights, x_in.astype(jnp.float32), has_aux=True)
    grads, grad_x = pull(cotangent.astype(jnp.float32))
    count = jnp.sum(data_mask)
    bin_density = BINS * totals / jnp.maximum(count, 1.0)
    token_count = count.astype(jnp.int32)
    return (out_act, grad_x, grads[0], grads[1], grads[2], grads[3], grads[4], grads[5], grads[6], grads[7], grads[8], grads[9], grads[10], grads[11], bin_density, token_count)
```

```python
import functools

import jax
import jax.numpy as jnp
from jax import lax
from jax.experimental import pallas as pl
from jax.experimental.pallas import tpu as pltpu
from jax.sharding import PartitionSpec as P

HEAD_DIM = 64
HALF = HEAD_DIM // 2
BINS = 24
LANES = 128
PIECES = 4
VMEM_MIB = 44
COSTS = {}

eps = 1e-05
theta = 10000.0
special_ids = 5
far = -1e30

bf16 = jnp.bfloat16
f32 = jnp.float32
AXES = ("dp", "tensor")


def dot(a, b):
    return jnp.dot(a, b, preferred_element_type=f32)


def dot_nt(a, b):
    return lax.dot_general(a, b, (((1,), (1,)), ((), ())), preferred_element_type=f32)


def normalize(rows):
    centre = rows - jnp.mean(rows, axis=-1, keepdims=True)
    spread = jnp.mean(centre * centre, axis=-1, keepdims=True)
    scale = lax.rsqrt(spread + eps)
    return centre * scale, scale


def norm_backward(rows, gain, grad):
    unit, scale = normalize(rows)
    gained = grad * gain
    mean_grad = jnp.mean(gained, axis=-1, keepdims=True)
    mean_both = jnp.mean(gained * unit, axis=-1, keepdims=True)
    below = scale * (gained - mean_grad - unit * mean_both)
    return below, column_sum(grad * unit), column_sum(grad)


def column_sum(rows):
    return jnp.sum(rows, axis=0, keepdims=True)


def rotate(rows, cosine, sine, sign):
    lane = lax.broadcasted_iota(jnp.int32, cosine.shape, 1)
    low = lane % HEAD_DIM < HALF
    pieces = []
    for start in range(0, rows.shape[1], LANES):
        piece = rows[:, start : start + LANES]
        other = jnp.where(low, pltpu.roll(piece, LANES - HALF, 1), pltpu.roll(piece, HALF, 1))
        pieces.append(piece * cosine + sign * (other * sine))
    return jnp.concatenate(pieces, axis=1)


def gelu_pair(value):
    size = jnp.abs(value) * (2.0**-0.5)
    t = 1.0 / (1.0 + 0.3275911 * size)
    bell = jnp.exp(-0.5 * value * value)
    poly = t * (
        0.5 * 0.254829592
        + t
        * (
            0.5 * -0.284496736
            + t * (0.5 * 1.421413741 + t * (0.5 * -1.453152027 + t * (0.5 * 1.061405429)))
        )
    )
    tail = poly * bell
    share = jnp.where(value < 0, tail, 1.0 - tail)
    return value * share, share + value * bell * 0.3989422804014327


def three_parts(column):
    high = column.astype(bf16).astype(f32)
    rest = column - high
    middle = rest.astype(bf16).astype(f32)
    return high, middle, rest - middle


def spec(shape, index=None):
    zeros = (0,) * len(shape)
    return pl.BlockSpec(shape, index or (lambda i, *s: zeros))


def whole(array):
    return array, spec(array.shape)


def hot(array):
    return array, spec(array.shape), True


def cold(array):
    return pltpu.with_memory_space_constraint(array, pltpu.HBM)


def shaped(shape, dtype):
    return jax.ShapeDtypeStruct(shape, dtype)


def call(
    name, kernel, steps, operands, results, prefetch=(), scratch=(), alias=(), after=(), sides=()
):
    def side_spec(shape):
        lead = (0,) * (len(shape) - 1)
        return spec(
            tuple(shape[:-1]) + (shape[-1] // 3,), lambda i, *s: (*lead, jnp.minimum(i, 2))
        )

    own_in, own_out = len(operands), len(results)
    idle = [cold(array) for array, _ in alias] + [cold(array) for array in after]
    arrays = [entry[0] if len(entry) > 2 else cold(entry[0]) for entry in operands]
    in_specs = [entry[1] for entry in operands]
    out_specs = [entry[2] for entry in results]
    out_shape = [
        (shaped if len(entry) > 3 else pltpu.HBM)(entry[0], entry[1]) for entry in results
    ]
    for _, side_args, side_shapes in sides:
        in_specs += [side_spec(arg.shape) for arg in side_args]
        out_specs += [side_spec(getattr(shape, "shape", shape)) for shape in side_shapes]
        out_shape += [
            pltpu.HBM(shape.shape, shape.dtype)
            if hasattr(shape, "dtype")
            else pltpu.HBM(shape, bf16)
            for shape in side_shapes
        ]
        arrays += [cold(arg) for arg in side_args]
    ahead, count_in, count_out = len(prefetch), len(in_specs), len(out_specs)

    def body(*refs):
        early, refs = refs[:ahead], refs[ahead + len(idle) :]
        ins, outs, rest = (
            refs[:count_in], refs[count_in : count_in + count_out], refs[count_in + count_out :]
        )
        if kernel is not None:
            kernel(*early, *ins[:own_in], *outs[:own_out], *rest)

        def run_sides():
            at_in, at_out = own_in, own_out
            for side_kernel, side_args, side_shapes in sides:
                side_kernel(
                    *ins[at_in : at_in + len(side_args)], *outs[at_out : at_out + len(side_shapes)]
                )
                at_in, at_out = at_in + len(side_args), at_out + len(side_shapes)

        if sides and steps > 3:
            pl.when(pl.program_id(0) < 3)(run_sides)
        else:
            run_sides()

    made = pl.pallas_call(
        body,
        grid_spec=pltpu.PrefetchScalarGridSpec(
            num_scalar_prefetch=ahead,
            grid=(steps,),
            in_specs=[pl.BlockSpec(memory_space=pl.ANY)] * len(idle) + in_specs,
            out_specs=out_specs,
            scratch_shapes=list(scratch),
        ),
        out_shape=out_shape,
        name=name,
        input_output_aliases={
            ahead + place: result for place, (_, result) in enumerate(alias)
        },
        compiler_params=pltpu.CompilerParams(vmem_limit_bytes=VMEM_MIB << 20),
        cost_estimate=pl.CostEstimate(
            flops=int(COSTS.get(name, 6e10)), bytes_accessed=int(4e6), transcendentals=0
        ),
    )
    outs = made(*prefetch, *idle, *arrays)
    done, at = list(outs[:own_out]), own_out
    for _, _, side_shapes in sides:
        done.append(outs[at : at + len(side_shapes)])
        at += len(side_shapes)
    return done


def gate(array, after):
    anywhere = pl.BlockSpec(memory_space=pl.ANY)
    return pl.pallas_call(
        lambda *refs: None,
        in_specs=[anywhere] * (1 + len(after)),
        out_specs=anywhere,
        out_shape=pltpu.HBM(array.shape, array.dtype),
        input_output_aliases={0: 0},
        name="gate",
    )(cold(array), *[cold(other) for other in after])


def gather_rows(target, slots, pieces, lane=0):
    count, lanes = pieces[0].shape
    for place, piece in enumerate(pieces):
        start = pl.multiple_of(slots[place] * count, 16)
        target[pl.ds(start, count), lane : lane + lanes] = piece[...]


def qkv_kernel(number, base, members, first, distant, *refs):
    refs = list(refs)
    slots = refs.pop(0) if distant else None
    if first:
        x, gain, bias, turn = refs[:4]
        refs = refs[4:]
    else:
        normed = refs.pop(0)
    pieces, refs = (refs[:PIECES], refs[PIECES:]) if distant else (refs[:1], refs[1:])
    b, cosine, sine, *refs = refs
    if first:
        normed, n_t, *refs = refs
    queries = refs.pop(0) if 0 in members else None
    kv = refs.pop(0) if 1 in members else None
    step = pl.program_id(0)
    if first:

        @pl.when(step == 0)
        def _():
            unit, _ = normalize(x[...].astype(f32))
            normed[...] = (
                unit * gain[number : number + 1] + bias[number : number + 1]
            ).astype(bf16)
            n_t[...] = dot_nt(turn[...], normed[...]).astype(bf16)

    if distant:
        (matrix,) = refs
        gather_rows(matrix, slots, pieces)
        weight = matrix[...]
    else:
        weight = pieces[0][0, 0]
    mixed = dot(normed[...], weight) + b[0, number : number + 1]
    for member in members:

        @pl.when(step == member - base)
        def _(member=member):
            if member == 0:
                turned = rotate(mixed, cosine[...], sine[...], 1.0)
                queries[...] = (turned * HEAD_DIM**-0.5).astype(bf16)
            elif member == 1:
                kv[0] = rotate(mixed, cosine[...], sine[...], 1.0).astype(bf16)
            else:
                kv[0] = mixed.astype(bf16)


def qkv_call(number, members, rows_in, norm, weight, b, tables, prior=(), after=()):
    first, distant = norm is not None, isinstance(weight, tuple)
    rows, width = rows_in.shape
    part = b.shape[2]
    base = members[0]
    operands = [hot(rows_in)]
    if first:
        operands += [whole(array) for array in norm[:2]] + [hot(norm[2])]
    prefetch, scratch = (), ()
    if distant:
        slots, pieces = weight
        prefetch = (slots,)
        operands += [
            (piece, spec((width // PIECES, part), lambda i, *s: (i + base, 0))) for piece in pieces
        ]
        scratch = (pltpu.VMEM((width, part), bf16),)
    else:
        block = spec((1, 1, width, part), lambda i, *s: (number, i + base, 0, 0))
        operands.append((weight, block))
    operands.append((b, spec((1, b.shape[1], part), lambda i, *s: (i + base, 0, 0))))
    operands += [hot(table) for table in tables]
    half = 1 if distant else 0
    results = []
    if first:
        results += [
            ((rows, width), bf16, spec((rows, width)), True),
            ((width, rows), bf16, spec((width, rows))),
        ]
    alias = []
    if 0 in members:
        if prior:
            alias.append((prior[0], len(results)))
        results.append(
            ((rows, 2 * part), bf16, spec((rows, part), lambda i, *s: (0, half)))
        )
    if 1 in members:
        if prior:
            alias.append((prior[-1], len(results)))
        block = spec(
            (1, rows, part), lambda i, *s: (jnp.maximum(i + base - 1, 0), 0, half)
        )
        results.append(((2, rows, 2 * part), bf16, block))
    return call(
        "qkv",
        functools.partial(qkv_kernel, number, base, members, first, distant),
        len(members),
        operands,
        results,
        prefetch,
        scratch,
        alias,
        after,
    )


def head_lanes(shape, head):
    lane = lax.broadcasted_iota(jnp.int32, shape, 1)
    return (lane < HEAD_DIM) if head == 0 else (lane >= HEAD_DIM)


def attention_kernel(q, kv, kv_far, q_mark, k_mark, k_mark_far, out, logsum):
    rows = q.shape[0]
    queries = q[...]
    results, logs = [], []
    for head in range(2):
        mine = head_lanes((rows, LANES), head)
        marked = jnp.where(mine, queries, q_mark[...])
        scores, values = [], []
        for pair, mark in ((kv, k_mark), (kv_far, k_mark_far)):
            keys = jnp.where(mine, pair[0], mark[...])
            scores.append(dot_nt(marked, keys))
            values.append(jnp.where(mine, pair[1], jnp.ones_like(pair[1])))
        highest = jnp.maximum(
            jnp.max(scores[0], axis=-1, keepdims=True), jnp.max(scores[1], axis=-1, keepdims=True)
        )
        total = 0.0
        for score, value in zip(scores, values):
            total = total + dot(jnp.exp(score - highest).astype(bf16), value)
        column = HEAD_DIM if head == 0 else 0
        summed = total[:, column : column + 1]
        results.append(total / summed)
        logs.append(highest + jnp.log(summed))
    out[...] = jnp.where(head_lanes((rows, LANES), 0), results[0], results[1]).astype(bf16)
    logsum[...] = jnp.where(head_lanes((rows, LANES), 0), logs[1], logs[0])


def head_specs(rows):
    column = spec((rows, LANES), lambda i, *s: (0, i))
    both = spec((2, rows, LANES), lambda i, *s: (0, 0, i))
    return column, both


def attention_call(q, kv, kv_far, marks, after=(), sides=()):
    rows, width = q.shape
    column, both = head_specs(rows)
    return call(
        "attention",
        attention_kernel,
        width // LANES,
        [(q, column), (kv, both), (kv_far, both)] + [hot(mark) for mark in marks],
        [((rows, width), bf16, column), ((rows, width), f32, column)],
        after=after,
        sides=sides,
    )


def attention_back_kernel(
    q, kv, kv_far, q_mark, k_mark, k_mark_far, logsum, attended, grad, cosine, sine,
    grad_q, grad_kv, grad_kv_far,
):
    rows = q.shape[0]
    queries = q[...]
    grads = grad[...]
    lane = lax.broadcasted_iota(jnp.int32, (rows, LANES), 1) % HEAD_DIM
    logs = three_parts(logsum[...])
    log_mark = sum(
        jnp.where(lane == 3 + place, part, 0.0) for place, part in enumerate(logs)
    ).astype(bf16)
    product = attended[...].astype(f32) * grads.astype(f32)
    value_mark = jnp.where(lane < 3, -1.0, 0.0).astype(bf16)
    dots_t = []
    keys_t = [
        jnp.transpose(pair[0].astype(f32)).astype(bf16) for pair in (kv, kv_far)
    ]
    outs = ([], [])
    for head in range(2):
        mine = head_lanes((rows, LANES), head)
        centre = jnp.sum(jnp.where(mine, product, 0.0), axis=-1, keepdims=True)
        centre_mark = sum(
            jnp.where(lane == place, part, 0.0) for place, part in enumerate(three_parts(centre))
        ).astype(bf16)
        marked = jnp.where(mine, queries, q_mark[...] + log_mark)
        marked_grads = jnp.where(mine, grads, centre_mark)
        turned = 0.0
        for place, (pair, mark) in enumerate(((kv, k_mark), (kv_far, k_mark_far))):
            keys = jnp.where(mine, pair[0], mark[...])
            values = jnp.where(mine, pair[1], value_mark)
            probs = jnp.exp(dot_nt(keys, marked))
            grad_scores = (probs * dot_nt(values, marked_grads)).astype(bf16)
            grad_values = dot(probs.astype(bf16), grads)
            grad_keys = dot(grad_scores, queries)
            turned = turned + dot(
                keys_t[place][head * HEAD_DIM : (head + 1) * HEAD_DIM], grad_scores
            )
            outs[place].append((grad_keys, grad_values))
        dots_t.append(turned)
    grad_queries = jnp.transpose(jnp.concatenate(dots_t, axis=0)) * HEAD_DIM**-0.5
    grad_q[...] = rotate(grad_queries, cosine[...], sine[...], -1.0).astype(bf16)
    mine = head_lanes((rows, LANES), 0)
    for ref, (one, two) in zip((grad_kv, grad_kv_far), outs):
        for member in range(2):
            ref[member] = jnp.where(mine, one[member], two[member]).astype(ref.dtype)


def attention_back_call(q, kv, kv_far, marks, logsum, attended, grad, tables, after=(), sides=()):
    rows, width = q.shape
    column, both = head_specs(rows)
    return call(
        "attention_back",
        attention_back_kernel,
        width // LANES,
        [(q, column), (kv, both), (kv_far, both)]
        + [hot(mark) for mark in marks]
        + [(logsum, column), (attended, column), (grad, column, True)]
        + [hot(table) for table in tables],
        [
            ((rows, width), bf16, column, True),
            ((2, rows, width), f32, both, True),
            ((2, rows, width), bf16, both),
        ],
        after=after,
        sides=sides,
    )


def out_operands(pieces, part, width):
    low = part // PIECES
    lead = 3 * (width // PIECES) // low
    return [
        (piece, spec((low, part), lambda i, *s, side=side: (lead + side, 0)))
        for side in range(2)
        for piece in pieces
    ]


def gather_out(target, slots, pieces):
    part = target.shape[0]
    for side in range(2):
        gather_rows(target, slots, pieces[side * PIECES :][:PIECES], side * part)


def ffn_kernel(number, slots, *refs):
    x, att, wo_n = refs[:3]
    wo_pieces, refs = refs[3 : 3 + 2 * PIECES], refs[3 + 2 * PIECES :]
    (b_out, gain, bias, b_down, turn, w_up, b_up, w_down,
     middle, normed, n_t, active, slope, acc, wo_o) = refs
    row = slice(number, number + 1)

    @pl.when(pl.program_id(0) == 0)
    def _():
        part = wo_o.shape[0]
        gather_out(wo_o, slots, wo_pieces)
        mid = (
            x[...].astype(f32)
            + dot(att[:, :part], wo_n[0])
            + dot(att[:, part:], wo_o[...])
            + b_out[row]
        )
        middle[...] = mid
        unit, _ = normalize(mid)
        normed[...] = (unit * gain[row] + bias[row]).astype(bf16)
        n_t[...] = dot_nt(turn[...], normed[...]).astype(bf16)
        acc[...] = mid + b_down[row]

    hidden = dot(normed[...], w_up[0]) + b_up[row]
    value, back = gelu_pair(hidden)
    value = value.astype(bf16)
    active[...] = value
    slope[...] = back.astype(bf16)
    acc[...] += dot(value, w_down[0])


def ffn_call(number, x, att, w_out, heads_far, small, turn, w_up, b_up, w_down, after=()):
    rows, width = x.shape
    units, part = w_up.shape[2], w_out.shape[1]
    slots, pieces = heads_far
    b_out, gain, bias, b_down = small
    block = 2 * units // PIECES
    wide = spec((rows, block), lambda i, *s: (0, i))
    full = spec((rows, width))
    return call(
        "ffn",
        functools.partial(ffn_kernel, number),
        units // block,
        [
            whole(x),
            whole(att),
            (w_out, spec((1, part, width), lambda i, *s: (number, 0, 0))),
            *out_operands(pieces, part, width),
            *[whole(array) for array in (b_out, gain, bias, b_down)],
            hot(turn),
            (w_up, spec((1, width, block), lambda i, *s: (number, 0, i))),
            (b_up, spec((b_up.shape[0], block), lambda i, *s: (0, i))),
            (w_down, spec((1, block, width), lambda i, *s: (number, i, 0))),
        ],
        [
            ((rows, width), f32, full),
            ((rows, width), bf16, full, True),
            ((width, rows), bf16, spec((width, rows))),
            ((rows, units), bf16, wide),
            ((rows, units), bf16, wide),
            ((rows, width), f32, full, True),
        ],
        prefetch=(slots,),
        scratch=(pltpu.VMEM((part, width), bf16),),
        after=after,
    )


def far_ffn_operands(up_far, down_far, width, units):
    slots_u, ups = up_far
    slots_d, downs = down_far
    block = 2 * units // PIECES

    def at(i, slots):
        return slots[jnp.clip(i, 0, 1)] // 2

    ups = [
        (piece, spec((width // PIECES, block), lambda i, *s: (0, at(i, s[0])))) for piece in ups
    ]
    downs = [(piece, spec((units // PIECES, width))) for piece in downs]
    return ups, downs, at, (slots_d, slots_u)


def gather_down(target, step, slots, downs):
    for place in range(2):

        @pl.when(step == place)
        def _(place=place):
            for which in (place, place + 2):
                count = downs[which].shape[0]
                start = pl.multiple_of((slots[which] % 2) * count, 16)
                target[pl.ds(start, count), :] = downs[which][...]


def ffn_far_kernel(number, slots_d, slots_u, normed, acc_in, b_up, *refs):
    ups, downs = refs[:PIECES], refs[PIECES : 2 * PIECES]
    active, slope, acc, low, w_up, w_down = refs[2 * PIECES :]
    step = pl.program_id(0)

    @pl.when(step == 0)
    def _():
        acc[...] = acc_in[...]

    gather_rows(w_up, slots_u, ups)
    gather_down(w_down, step, slots_d, downs)
    hidden = dot(normed[...], w_up[...]) + b_up[number : number + 1]
    value, back = gelu_pair(hidden)
    value = value.astype(bf16)
    active[...] = value
    slope[...] = back.astype(bf16)
    acc[...] += dot(value, w_down[...])

    @pl.when(step == pl.num_programs(0) - 1)
    def _():
        low[...] = acc[...].astype(bf16)


def ffn_far_call(number, normed, acc, up_far, down_far, b_up, after=()):
    rows, width = normed.shape
    units = b_up.shape[1]
    block = 2 * units // PIECES
    ups, downs, at, prefetch = far_ffn_operands(up_far, down_far, width, units)
    wide = spec((rows, block), lambda i, *s: (0, at(i, s[0])))
    full = spec((rows, width))
    return call(
        "ffn_far",
        functools.partial(ffn_far_kernel, number),
        2,
        [
            hot(normed),
            hot(acc),
            (b_up, spec((b_up.shape[0], block), lambda i, *s: (0, at(i, s[0])))),
            *ups,
            *downs,
        ],
        [
            ((rows, units), bf16, wide),
            ((rows, units), bf16, wide),
            ((rows, width), f32, full),
            ((rows, width), bf16, full),
        ],
        prefetch=prefetch,
        scratch=(pltpu.VMEM((width, block), bf16), pltpu.VMEM((block, width), bf16)),
        after=after,
    )


def split_rows(product, keep, send, at):
    half = product.shape[0] // 2
    product = product.astype(bf16)
    keep[at] = product[:half]
    send[at] = product[half:]


def ffn_back_kernel(slots_d, slots_u, *refs):
    (g, n_t, g_t, active_n, slope_n, up_n, down_n, active_o, slope_o) = refs[:9]
    ups, downs = refs[9 : 9 + PIECES], refs[9 + PIECES : 9 + 2 * PIECES]
    acc, keep, send, b_up, up_o, down_o = refs[9 + 2 * PIECES :]
    step = pl.program_id(0)

    @pl.when(step == 0)
    def _():
        acc[...] = jnp.zeros_like(acc)

    def one(active, slope, w_up, w_down):
        grad_active = dot_nt(g[...], w_down)
        grad_hidden = (grad_active * slope[...].astype(f32)).astype(bf16)
        b_up[0] = column_sum(grad_hidden.astype(f32))
        acc[...] += dot_nt(grad_hidden, w_up)
        for which, product in enumerate(
            (dot(n_t[...], grad_hidden), dot(g_t[...], active[...]))
        ):
            block = product.shape[1] // 2
            for place in range(2):
                split_rows(
                    product[:, place * block : (place + 1) * block], keep, send, (0, which, place)
                )

    @pl.when(step < 2)
    def _():
        gather_rows(up_o, slots_u, ups)
        gather_down(down_o, step, slots_d, downs)
        one(active_o, slope_o, up_o[...], down_o[...])

    @pl.when(step >= 2)
    def _():
        one(active_n, slope_n, up_n[0], down_n[0])


def ffn_back_call(
    number, g, n_t, g_t, near, distant, w_up, w_down, up_far, down_far, after=(), sides=()
):
    rows, width = g.shape
    units = w_up.shape[2]
    block = 2 * units // PIECES
    ups, downs, at, prefetch = far_ffn_operands(up_far, down_far, width, units)

    def near_block(i):
        return jnp.maximum(i - 2, 0)

    def result_block(i, s):
        return jnp.where(i < 2, at(i, s[0]), near_block(i))

    def side(i):
        return jnp.where(i < 2, 1, 0)

    near_wide = spec((rows, block), lambda i, *s: (0, near_block(i)))
    far_wide = spec((rows, block), lambda i, *s: (0, at(i, s[0])))
    grads = spec(
        (1, 2, 2, width // 2, block // 2), lambda i, *s: (side(i), 0, result_block(i, s), 0, 0)
    )
    grads_shape = (2, 2, PIECES, width // 2, block // 2)
    return call(
        "ffn_back",
        ffn_back_kernel,
        4,
        [
            hot(g),
            whole(n_t),
            hot(g_t),
            *[(array, near_wide) for array in near],
            (w_up, spec((1, width, block), lambda i, *s: (number, 0, near_block(i)))),
            (w_down, spec((1, block, width), lambda i, *s: (number, near_block(i), 0))),
            *[(array, far_wide) for array in distant],
            *ups,
            *downs,
        ],
        [
            ((rows, width), f32, spec((rows, width)), True),
            (grads_shape, bf16, grads),
            (grads_shape, bf16, grads),
            ((2, 1, units), f32,
             spec((1, 1, block), lambda i, *s: (side(i), 0, result_block(i, s)))),
        ],
        prefetch=prefetch,
        scratch=(pltpu.VMEM((width, block), bf16), pltpu.VMEM((block, width), bf16)),
        after=after,
        sides=sides,
    )


def middle_back_kernel(number, slots, acc, middle, gain, g, wo_n, *refs):
    wo_pieces, refs = refs[: 2 * PIECES], refs[2 * PIECES :]
    turn, grad_middle, grad_att, low_t, smalls, wo_o, low = refs
    step = pl.program_id(0)
    part = wo_o.shape[0]

    @pl.when(step == 0)
    def _():
        below, d_gain, d_bias = norm_backward(middle[...], gain[number : number + 1], acc[...])
        total = below + g[...].astype(f32)
        grad_middle[...] = total
        low[...] = total.astype(bf16)
        smalls[0:1] = d_gain
        smalls[1:2] = d_bias
        smalls[2:3] = column_sum(total)

    @pl.when(step == 1)
    def _():
        gather_out(wo_o, slots, wo_pieces)
        grad_att[:, :part] = dot_nt(low[...], wo_n[0]).astype(bf16)
        grad_att[:, part:] = dot_nt(low[...], wo_o[...]).astype(bf16)

    @pl.when(step == 2)
    def _():
        low_t[...] = dot_nt(turn[...], low[...]).astype(bf16)


def middle_back_call(number, acc, middle, gain, g, w_out, heads_far, turn, after=(), sides=()):
    rows, width = acc.shape
    part = w_out.shape[1]
    slots, pieces = heads_far
    return call(
        "middle_back",
        functools.partial(middle_back_kernel, number),
        3,
        [
            hot(acc),
            *[whole(array) for array in (middle, gain, g)],
            (w_out, spec((1, part, width), lambda i, *s: (number, 0, 0))),
            *out_operands(pieces, part, width),
            hot(turn),
        ],
        [
            ((rows, width), f32, spec((rows, width)), True),
            ((rows, width), bf16, spec((rows, width)), True),
            ((width, rows), bf16, spec((width, rows)), True),
            ((3, width), f32, spec((3, width))),
        ],
        prefetch=(slots,),
        scratch=(pltpu.VMEM((part, width), bf16), pltpu.VMEM((rows, width), bf16)),
        after=after,
        sides=sides,
    )


def qkv_back_kernel(number, weight, rows_grad, *refs):
    refs = list(refs)
    slots = refs.pop(0) if rows_grad else None
    gq, kv, kv_far, cosine, sine = refs[:5]
    refs = refs[5:]
    if weight:
        n_t, gm_t, att, *refs = refs
    if rows_grad:
        w_n, *refs = refs
        pieces, refs = refs[:PIECES], refs[PIECES:]
        x, gain, g, turn, *refs = refs
    if weight:
        keep, send, b, *refs = refs
    if rows_grad:
        acc, low, low_t, smalls, matrix, *refs = refs
    (mixed,) = refs
    step = pl.program_id(0)
    part = gq.shape[1]

    def lanes(member):
        return slice(member * part, (member + 1) * part)

    mixed[:, lanes(0)] = gq[...]
    keys = rotate(kv[0] + kv_far[0].astype(f32), cosine[...], sine[...], -1.0)
    mixed[:, lanes(1)] = keys.astype(bf16)
    mixed[:, lanes(2)] = (kv[1] + kv_far[1].astype(f32)).astype(bf16)
    if weight:
        sums = column_sum(mixed[...].astype(f32))
        product = dot(n_t[...], mixed[...])
        for member in range(3):
            b[0, member] = sums[:, lanes(member)]
            split_rows(product[:, lanes(member)], keep, send, (0, member))
        split_rows(dot(gm_t[...], att[...]), keep, send, (0, 3))
    if rows_grad:

        @pl.when(step == 0)
        def _():
            for member in range(3):
                matrix[:, lanes(member)] = w_n[0, member]
            acc[...] = dot_nt(mixed[...], matrix[...])

        @pl.when(step == 1)
        def _():
            count = matrix.shape[0] // PIECES
            for place, piece in enumerate(pieces):
                start = pl.multiple_of(slots[place] * count, 16)
                for member in range(3):
                    matrix[pl.ds(start, count), lanes(member)] = piece[
                        member * count : (member + 1) * count
                    ]
            whole_grad = acc[...] + dot_nt(mixed[...], matrix[...])
            below, d_gain, d_bias = norm_backward(
                x[...].astype(f32), gain[number : number + 1], whole_grad
            )
            total = below + g[...]
            acc[...] = total
            low[...] = total.astype(bf16)
            low_t[...] = dot_nt(turn[...], low[...]).astype(bf16)
            smalls[0:1] = d_gain
            smalls[1:2] = d_bias
            smalls[2:3] = column_sum(total)


def qkv_back_call(
    number, gq, kv, kv_far, tables, sources=None, weights=None, ending=None, after=()
):
    rows = gq.shape[0]
    part = gq.shape[1] // 2
    width = 2 * part
    column = spec((rows, part), lambda i, *s: (0, i))
    both = spec((2, rows, part), lambda i, *s: (0, 0, i))
    operands = [(gq, column, True), (kv, both, True), (kv_far, both, True), *[hot(table) for table in tables]]
    results, prefetch, scratch = [], (), []
    if sources is not None:
        n_t, gm_t, att = sources
        operands += [whole(n_t), hot(gm_t), (att, column)]
        grads = spec((1, 4, width // 2, part), lambda i, *s: (i, 0, 0, 0))
        results += [((2, 4, width // 2, part), bf16, grads)] * 2
        results.append(
            ((2, 3, 1, part), f32, spec((1, 3, 1, part), lambda i, *s: (i, 0, 0, 0)))
        )
    if weights is not None:
        w_n, (slots, pieces) = weights
        prefetch = (slots,)
        operands.append((w_n, spec((1, 3, width, part), lambda i, *s: (number, 0, 0, 0))))
        operands += [whole(piece) for piece in pieces]
        x, gain, g, turn = ending
        operands += [whole(x), whole(gain), hot(g), hot(turn)]
        results += [
            ((rows, width), f32, spec((rows, width))),
            ((rows, width), bf16, spec((rows, width)), True),
            ((width, rows), bf16, spec((width, rows)), True),
            ((3, width), f32, spec((3, width))),
        ]
        scratch.append(pltpu.VMEM((width, 3 * part), bf16))
    scratch.append(pltpu.VMEM((rows, 3 * part), bf16))
    return call(
        "qkv_back",
        functools.partial(qkv_back_kernel, number, sources is not None, weights is not None),
        2,
        operands,
        results,
        prefetch=prefetch,
        scratch=scratch,
        after=after,
    )


def pack_call(number, slots, groups, after=()):
    operands, results, entries = [], [], []
    for which, matrices in groups:
        rows, places = 0, []
        lanes = matrices[0].shape[-1]
        for matrix in matrices:
            lead = matrix.shape[1] if matrix.ndim == 4 else 1
            chunk, sides = matrix.shape[-2] // PIECES, matrix.shape[-1] // lanes
            middle = (lead,) if matrix.ndim == 4 else ()
            zeros = (0,) * len(middle)
            operands.append((
                matrix,
                spec(
                    (1, *middle, chunk, matrix.shape[-1]),
                    lambda i, *s, which=which, zeros=zeros: (number, *zeros, s[which][0], 0),
                ),
            ))
            places.append((rows, lead, chunk, sides))
            rows += lead * chunk * sides
        results.append(((rows, lanes), bf16, spec((rows, lanes))))
        entries.append((places, lanes))

    def kernel(*refs):
        refs = refs[len(slots) :]
        outs = refs[len(operands) :]
        at = 0
        for out, (places, lanes) in zip(outs, entries):
            for row, lead, chunk, sides in places:
                source = refs[at]
                at += 1
                for member in range(lead):
                    for side in range(sides):
                        cut = slice(side * lanes, (side + 1) * lanes)
                        start = row + (member * sides + side) * chunk
                        if len(source.shape) == 4:
                            piece = source[0, member, :, cut]
                        else:
                            piece = source[0, :, cut]
                        out[start : start + chunk] = piece

    return call("pack", kernel, 1, operands, results, prefetch=slots, after=after)


def plus(a, b):
    return (a.astype(f32) + b.astype(f32)).astype(bf16)


def join_ffn_kernel(keep, got, a_keep, a_send, b_keep, b_send):
    half = b_keep.shape[2]
    for place in range(PIECES):
        a_keep[place] = plus(keep[0, 0, place], got[0, 0, place])
        a_send[place] = plus(keep[1, 0, place], got[1, 0, place])
        for side in range(2):
            b_keep[side, place] = plus(keep[side, 1, place, :half], got[side, 1, place, :half])
            b_send[side, place] = plus(keep[side, 1, place, half:], got[side, 1, place, half:])


def join_attention_kernel(keep, got, a_keep, a_send, b_keep, b_send):
    half = b_keep.shape[2]
    for member in range(2):
        a_keep[member] = plus(keep[0, member], got[0, member])
        a_send[member] = plus(keep[1, member], got[1, member])
        for side in range(2):
            kept, came = keep.at[side, 2 + member], got.at[side, 2 + member]
            b_keep[side, member] = plus(kept[:half], came[:half])
            b_send[side, member] = plus(kept[half:], came[half:])


def join_line_kernel(keep, got, next_keep, next_send):
    half, quarter = keep.shape[2] // 2, next_keep.shape[2]
    for side in range(2):
        for member in range(4):
            for x in range(2):
                for start, ref in ((x * half, next_keep), (x * half + quarter, next_send)):
                    cut = slice(start, start + quarter)
                    ref[4 * side + member, x] = plus(
                        keep[side, member, cut], got[side, member, cut]
                    )


def cut_kernel(keep, got, next_keep, next_send):
    for member in range(keep.shape[0]):
        next_keep[member] = plus(keep[member, 0], got[member, 0])
        next_send[member] = plus(keep[member, 1], got[member, 1])


def turn_kernel(a_keep, a_got, b_keep, b_got, a_next, a_send, b_next, b_send):
    half = a_next.shape[1]
    for member in range(a_keep.shape[0]):
        a_next[member] = plus(a_keep[member, :half], a_got[member, :half])
        a_send[member] = plus(a_keep[member, half:], a_got[member, half:])
    for member in range(b_keep.shape[1]):
        b_next[member] = plus(b_keep[0, member], b_got[0, member])
        b_send[member] = plus(b_keep[1, member], b_got[1, member])


def merge_kernel(*refs):
    keep, send = refs[-2:]
    half = keep.shape[1]
    place = 0
    for kept, got in zip(refs[:-2:2], refs[1:-2:2]):
        for member in range(kept.shape[0]):
            keep[place] = plus(kept[member, :half], got[member, :half])
            send[place] = plus(kept[member, half:], got[member, half:])
            place += 1


def part_kernel(first, keep, got, near, distant):
    for place in range(4):
        near[place] = plus(keep[first + place], got[first + place])
        distant[place] = plus(keep[first + 4 + place], got[first + 4 + place])


def add_kernel(a, b, out):
    out[...] = a[...] + b[...]


def sums_call(name, *sides, after=()):
    return call(name, None, 3, [], [], after=after, sides=sides)


def emit_call(ffn, attention):
    depth = len(ffn)
    terms = [array for _, arrays in ffn + attention for array in arrays]
    chunk, part = terms[0].shape[1:]
    shapes = [
        (depth, chunk, PIECES * part), (depth, chunk, PIECES * part),
        (depth, 3, chunk, part), (depth, chunk, part),
    ]

    def kernel(*refs):
        up, down, qkv, out = refs[len(terms) :]
        at = 0
        for number, (first, arrays) in enumerate(ffn):
            here = refs[at : at + len(arrays)]
            at += len(arrays)
            for place in range(2 * PIECES):
                total = sum(term[first + place].astype(f32) for term in here)
                start = place % PIECES * part
                (up, down)[place // PIECES][number, :, start : start + part] = total
        for number, (first, arrays) in enumerate(attention):
            here = refs[at : at + len(arrays)]
            at += len(arrays)
            for member in range(4):
                total = sum(term[first + member].astype(f32) for term in here)
                if member < 3:
                    qkv[number, member] = total
                else:
                    out[number] = total

    return call(
        "emit", kernel, 1, [whole(term) for term in terms],
        [(shape, f32, spec(shape)) for shape in shapes],
    )


def widen_call(arrays, after=()):
    def kernel(*refs):
        for source, out in zip(refs[: len(arrays)], refs[len(arrays) :]):
            out[...] = source[...].astype(f32)

    rows, width = arrays[0].shape
    block = spec((rows // 4, width), lambda i, *s: (i, 0))
    return call(
        "widen", kernel, 4, [(array, block) for array in arrays],
        [((rows, width), f32, block) for _ in arrays], after=after,
    )


def share_call(low, head, ids, class_bins, after):
    high = lax.Precision.HIGHEST

    def kernel(low, head, ids, class_bins, out):
        logits = dot_nt(low[...], head[...])
        expos = jnp.exp(logits - jnp.max(logits, axis=-1, keepdims=True))
        shares = expos / jnp.sum(expos, axis=-1, keepdims=True)
        mask = (ids[...] >= special_ids).astype(f32)
        sums = jnp.dot(mask, shares, precision=high, preferred_element_type=f32)
        bins = lax.broadcasted_iota(jnp.int32, (LANES, class_bins.shape[1]), 0)
        table = (bins == class_bins[...]).astype(f32)
        totals = lax.dot_general(
            jnp.broadcast_to(sums, (8, sums.shape[1])), table, (((1,), (1,)), ((), ())),
            precision=high, preferred_element_type=f32,
        )[0:1]
        lane = lax.broadcasted_iota(jnp.int32, (1, LANES), 1)
        out[...] = jnp.where(lane == BINS, jnp.sum(mask), jnp.where(lane < BINS, totals, 0.0))

    args = (low, head, ids, class_bins)
    return call(
        "share", kernel, 1, [whole(array) for array in args],
        [((1, LANES), f32, spec((1, LANES)))], after=(after,),
    )[0]


def pack_small(layers, bin_row, width):
    count = len(layers)
    part, units = layers[0][3].shape[3], layers[0][4].shape[2]
    folds = units // width
    shared = 6 * count + 1
    total = shared + count * (3 + folds)
    args = [array for layer in layers for array in layer] + [bin_row]

    def kernel(*refs):
        own, other = refs[-2:]
        own[...] = jnp.zeros_like(own)
        for number in range(count):
            one, two, down, _, _ = refs[5 * number : 5 * number + 5]
            own[6 * number : 6 * number + 2] = one[0:2]
            own[6 * number + 2 : 6 * number + 5] = two[...]
            own[6 * number + 5 : 6 * number + 6] = down[down.shape[0] - 1 :]
        bins = refs[5 * count]
        own[6 * count : 6 * count + 1, : bins.shape[1]] = bins[...]
        other[...] = own[...]
        for number in range(count):
            qkv, up = refs[5 * number + 3 : 5 * number + 5]
            start = shared + number * (3 + folds)
            for side, out in enumerate((own, other)):
                for member in range(3):
                    out[start + member : start + member + 1, :part] = qkv[side, member]
                for fold in range(folds):
                    row = start + 3 + fold
                    out[row : row + 1] = up[side, :, fold * width : (fold + 1) * width]

    result = ((total, width), f32, spec((total, width)))
    return call("pack_small", kernel, 1, [whole(array) for array in args], [result, result])


def unpack_small(terms, count, part, units):
    width = terms[0].shape[1]
    folds = units // width
    shared = 6 * count + 1

    def kernel(one, two, *outs):
        sums = one[...] + two[...]
        qkv, up, bins, tokens = outs[6:]
        for number in range(count):
            for member in range(6):
                row = 6 * number + member
                outs[member][number : number + 1] = sums[row : row + 1]
            start = shared + number * (3 + folds)
            for member in range(3):
                row = start + member
                qkv[member, number : number + 1] = sums[row : row + 1, :part]
            for fold in range(folds):
                row = start + 3 + fold
                up[number : number + 1, fold * width : (fold + 1) * width] = sums[row : row + 1]
        row = sums[6 * count : 6 * count + 1, :LANES]
        tally = row[:, BINS : BINS + 1]
        bins[...] = BINS * row / jnp.maximum(tally, 1.0)
        tokens[...] = jnp.broadcast_to(tally, tokens.shape).astype(jnp.int32)

    shapes = [((count, width), f32)] * 6 + [
        ((3, count, part), f32), ((count, units), f32), ((1, LANES), f32), ((1, LANES), jnp.int32)
    ]
    outs = call(
        "unpack_small", kernel, 1, [whole(term) for term in terms],
        [(shape, dtype, spec(shape)) for shape, dtype in shapes],
    )
    return outs[:6], outs[6], outs[7], outs[8], outs[9]


def segment_info(seq_lengths, total):
    ends = jnp.cumsum(seq_lengths)
    places = jnp.arange(total, dtype=jnp.int32)
    labels = jnp.sum((places[:, None] >= ends[None, :-1]).astype(jnp.int32), axis=1)
    starts = ends - seq_lengths
    picks = labels[:, None] == jnp.arange(seq_lengths.shape[0], dtype=jnp.int32)[None, :]
    begin = jnp.sum(jnp.where(picks, starts[None, :], 0), axis=1)
    return (labels, places - begin)


def moves(dp_size, tensor_size):
    def flat(dp, tensor):
        return dp * tensor_size + tensor

    every = [(dp, tensor) for dp in range(dp_size) for tensor in range(tensor_size)]

    def by(target):
        return [(flat(*where), flat(*target(*where))) for where in every]

    return {
        "swap": by(lambda dp, tensor: (dp - dp % 2 + tensor, dp % 2)),
        "y": by(lambda dp, tensor: (dp, 1 - tensor)),
        "bits": [
            by(lambda dp, tensor, bit=bit: (dp ^ bit, tensor))
            for bit in (1 << place for place in range(dp_size.bit_length() - 1))
        ],
    }


def per_device(
    x_in,
    lengths,
    token_ids,
    ln1_gain,
    ln1_bias,
    w_qkv,
    b_qkv,
    w_out,
    b_out,
    ln2_gain,
    ln2_bias,
    w_up,
    b_up,
    w_down,
    b_down,
    head,
    class_bins,
    cotangent,
):
    rows, width = x_in.shape
    dp_size = lax.axis_size("dp")
    tensor_size = lax.axis_size("tensor")
    depth = w_qkv.shape[0]
    part = w_qkv.shape[3]
    units = w_up.shape[2]
    total = rows * tensor_size
    dp = lax.axis_index("dp")
    core = dp % 2
    bits = dp_size.bit_length() - 1
    move = moves(dp_size, tensor_size)

    def send(array, name):
        return lax.ppermute(array, AXES, move["bits"][name] if isinstance(name, int) else move[name])

    numbers = send(jnp.concatenate([lengths[0], token_ids]), "swap")
    seq_lengths, ids = numbers[: lengths.shape[1]], numbers[lengths.shape[1] :]
    small_biases = jnp.concatenate([b_qkv.reshape(depth, -1), b_up], axis=1)
    far_biases = send(small_biases, "y")
    w_qkv = jnp.transpose(w_qkv, (0, 2, 1, 3))
    b_qkv = jnp.transpose(b_qkv, (1, 0, 2))
    far_b_qkv = jnp.transpose(far_biases[:, : 3 * part].reshape(depth, 3, part), (1, 0, 2))
    far_b_up = far_biases[:, 3 * part :]

    z_bit = min(2, bits - 1)

    def slots_of(bit):
        own = ((dp >> bit) % 2) * 2 + core
        return jnp.stack([own, own ^ 2, own ^ 1, own ^ 3]).astype(jnp.int32)

    all_slots = (slots_of(1), slots_of(z_bit))

    class Bundle:
        def __init__(self, way, packed):
            self.way, self.packed = way, packed

        def begin(self, *tokens):
            packed = gate(self.packed, tokens) if tokens else self.packed
            self.got = send(packed, "y")
            return packed

        def hop(self, *tokens):
            if tokens:
                self.got = gate(self.got, tokens)
            self.beside = send(self.got, (1, z_bit)[self.way])
            self.across = send(self.got, 0)
            return self.got

        def end(self, *tokens):
            beside = gate(self.beside, tokens)
            pieces = [self.got, beside, self.across, send(beside, 0)]
            self.far = (all_slots[self.way], pieces)
            return beside

    (packed,) = pack_call(0, all_slots, [(0, (w_qkv, w_out))])
    heads = [Bundle(0, packed)]
    ups, downs = [], []
    heads[0].begin()
    heads[0].hop()
    x_low = gate(x_in.astype(bf16), (packed,))
    stream = send(x_low, "swap")
    for number in range(depth):
        groups = [(0, (w_up,)), (1, (w_down,))]
        if number:
            groups.append((1, (w_qkv, w_out)))
        arrays = pack_call(number, all_slots, groups, (packed, x_low))
        ups.append(Bundle(0, arrays[0]))
        downs.append(Bundle(1, arrays[1]))
        if number:
            heads.append(Bundle(1, arrays[2]))
    ups[0].begin(heads[0].got)
    cotangent_low = cotangent.astype(bf16)

    labels, places = segment_info(seq_lengths, total)
    labels_here = lax.dynamic_slice_in_dim(labels, core * rows, rows, 0)
    labels_far = lax.dynamic_slice_in_dim(labels, (1 - core) * rows, rows, 0)
    places_here = lax.dynamic_slice_in_dim(places, core * rows, rows, 0)
    lane = jnp.arange(LANES, dtype=jnp.int32)[None, :]
    freqs = theta ** (-(lane % HALF).astype(f32) / HALF)
    angles = places_here.astype(f32)[:, None] * freqs
    sine = jnp.sin(angles)
    tables = (jnp.cos(angles), jnp.where(lane % HEAD_DIM < HALF, -sine, sine))
    place = lane % HEAD_DIM
    q_mark = jnp.where(labels_here[:, None] == place, far, 0.0).astype(bf16)

    def key_mark(own):
        other = (own[:, None] != place) & (place < 3)
        return jnp.where(other, 1.0, jnp.where((place >= 3) & (place < 6), -1.0, 0.0)).astype(bf16)

    marks = (q_mark, key_mark(labels_here), key_mark(labels_far))
    chunk = width // dp_size
    order = jnp.arange(width, dtype=jnp.int32)
    block, inside = order // chunk, order % chunk
    home = sum(
        (((block >> (bits - 1 - place)) & 1) << place) for place in range(bits)
    )
    order = (home ^ dp) * chunk + inside
    turn = (order[:, None] == jnp.arange(width, dtype=jnp.int32)[None, :]).astype(bf16)

    def turned(array):
        return lax.dot_general(turn, array, (((1,), (1,)), ((), ())), preferred_element_type=bf16)

    saved = []
    wait = ()
    for number in range(depth):
        more = number + 1 < depth
        normed_attn, n_t_attn, q, kv = qkv_call(
            number, (0, 1, 2), stream, (ln1_gain, ln1_bias, turn), w_qkv, b_qkv, tables,
            after=wait,
        )
        if number == 0:
            heads[0].end(kv)
        qkv_far = heads[number].far
        (kv,) = qkv_call(
            number, (1, 2), normed_attn, None, qkv_far, far_b_qkv, tables, (kv,)
        )
        kv_far = send(kv, 0)
        if number == 0:
            wait = (ups[0].hop(kv), downs[0].begin(ups[0].got, kv))
        else:
            wait = (ups[number].end(kv), downs[number].hop(kv))
        if not more:
            low = gate(cotangent_low, (downs[number].got, kv))
            grad_stream = send(low, "swap")
            wait += (low,)
        (q,) = qkv_call(
            number, (0,), normed_attn, None, qkv_far, far_b_qkv, tables, (q,), (kv, *wait)
        )
        att, logsum = attention_call(q, kv, kv_far, marks)
        if number == 0:
            wait = (ups[0].end(att), downs[0].hop(att))
        else:
            wait = (downs[number].end(att),)
        if more:
            wait += (heads[number + 1].begin(downs[number].got, att),)
        middle, normed_ffn, n_t_ffn, active, slope, acc = ffn_call(
            number, stream, att, w_out, qkv_far, (b_out, ln2_gain, ln2_bias, b_down),
            turn, w_up, b_up, w_down, wait,
        )
        wait = (downs[0].end(acc),) if number == 0 else ()
        if more:
            wait += (heads[number + 1].hop(acc), ups[number + 1].begin(heads[number + 1].got, acc))
        up_far, down_far = ups[number].far, downs[number].far
        active_o, slope_o, below, low = ffn_far_call(
            number, normed_ffn, acc, up_far, down_far, far_b_up, wait
        )
        if more:
            wait = (
                heads[number + 1].end(low),
                ups[number + 1].hop(low),
                downs[number + 1].begin(ups[number + 1].got, low),
            )
        saved.append(
            (stream, n_t_attn, (q, kv, kv_far), logsum, att, middle, n_t_ffn,
             (active, slope), (active_o, slope_o))
        )
        stream = below
    out_low = send(low, "swap")
    half = width // 2
    quarter, eighth = half // 2, half // 4

    def pairs(*steps):
        return tuple(array for keep, sent, way in steps for array in (keep, send(sent, way)))

    def join_ffn(keep, got):
        shapes = ((PIECES, half, part),) * 2 + ((2, PIECES, quarter, part),) * 2
        return join_ffn_kernel, (keep, got), shapes

    def join_attention(*arrays):
        shapes = ((2, half, part),) * 2 + ((2, 2, quarter, part),) * 2
        return join_attention_kernel, arrays, shapes

    def join_line(*arrays):
        return join_line_kernel, arrays, ((8, 2, eighth, part),) * 2

    def cut(keep, sent, way):
        members, _, deep, cols = keep.shape
        return cut_kernel, pairs((keep, sent, way)), ((members, deep, cols),) * 2

    def turn_ways(joined):
        a_keep, a_send, b_keep, b_send = joined
        members, deep, cols = a_keep.shape
        shape_a, shape_b = (members, deep // 2, cols), b_keep.shape[1:]
        arrays = pairs((a_keep, a_send, "y"), (b_keep, b_send, 1))
        return turn_kernel, arrays, (shape_a, shape_a, shape_b, shape_b)

    def merge(*steps):
        members = sum(keep.shape[0] for keep, _, _ in steps)
        _, deep, cols = steps[0][0].shape
        return merge_kernel, pairs(*steps), ((members, deep // 2, cols),) * 2

    def merge_ways(turned):
        a_keep, a_send, b_keep, b_send = turned
        return merge((a_keep, a_send, 1), (b_keep, b_send, "y"))

    def part_sides(first, keep, sent):
        return (
            functools.partial(part_kernel, first), pairs((keep, sent, 3)),
            ((4,) + keep.shape[1:],) * 2,
        )

    def add_small(array, other, way):
        return add_kernel, (array, send(other, way)), (shaped(array.shape, f32),)

    def plain_sum(keep, got):
        total = plus(keep, got)
        total = plus(total[0], send(total[1], "y"))
        for bit in range(1, bits):
            rows_left = total.shape[-2] // 2
            total = plus(total[..., :rows_left, :], send(total[..., rows_left:, :], bit))
        return total.astype(f32)

    placed = bits == 4 and depth == 2
    pieces = [None] * depth
    plain = [None] * depth
    grad_low = grad_stream
    g_t = turned(grad_low)
    grad_b_down = column_sum(grad_stream.astype(f32))
    for number in reversed(range(depth)):
        stream, n_t_attn, keyed, logsum, att, middle, n_t_ffn, near, distant = saved[number]
        top, last = number == depth - 1, number == 0
        acc, ffn_k, ffn_s, d_b_up = ffn_back_call(
            number, grad_low, n_t_ffn, g_t, near, distant, w_up, w_down,
            ups[number].far, downs[number].far,
        )
        ffn_g = send(ffn_s, 0)
        sides = []
        if placed and not top:
            sides = [turn_ways(joined_ffn), join_line(qkv_k, qkv_g)]
        after = ()
        if last:
            bin_row = share_call(low, jnp.transpose(head), ids[None], class_bins[None], ffn_k)
            after = (bin_row,)
        grad_middle, grad_att, gm_t, smalls_two, *more = middle_back_call(
            number, acc, middle, ln2_gain, grad_stream, w_out, heads[number].far, turn,
            sides=sides, after=after,
        )
        if more:
            turned_ffn, lined = more
        after = ()
        if placed and last:
            (joined_low,) = sums_call("join_ffn", join_ffn(ffn_k, ffn_g), after=(grad_att,))
            after = joined_low[1:2]
        gq, gkv, gkv_s = attention_back_call(
            *keyed, marks, logsum, att, grad_att, tables, after=after
        )
        gkv_g = send(gkv_s, 0)
        after = ()
        if placed and not last:
            (joined_ffn,) = sums_call("join_ffn", join_ffn(ffn_k, ffn_g), after=(gkv_s,))
            after = joined_ffn[1:2]
        elif placed:
            merged_ffn, cut_line, turned_low = sums_call(
                "merge_above", merge_ways(turned_ffn), cut(*lined, z_bit), turn_ways(joined_low),
                after=(gkv_s,),
            )
            after = merged_ffn[1:2]
        weights, ending = (w_qkv, heads[number].far), (stream, ln1_gain, grad_middle, turn)
        if placed and last:
            qkv_k, qkv_s, d_b_qkv = qkv_back_call(
                number, gq, gkv, gkv_g, tables, (n_t_attn, gm_t, att), after=after
            )
            qkv_g = send(qkv_s, 0)
            grad_stream, grad_low, g_t, smalls_one = qkv_back_call(
                number, gq, gkv, gkv_g, tables, None, weights, ending, after=(qkv_s,)
            )
        else:
            qkv_k, qkv_s, d_b_qkv, grad_stream, grad_low, g_t, smalls_one = qkv_back_call(
                number, gq, gkv, gkv_g, tables, (n_t_attn, gm_t, att), weights, ending, after=after
            )
            qkv_g = send(qkv_s, 0)
        if not placed:
            plain[number] = (plain_sum(ffn_k, ffn_g), plain_sum(qkv_k, qkv_g))
        pieces[number] = (smalls_one, smalls_two, grad_b_down, d_b_qkv, d_b_up)
        grad_b_down = smalls_one
    grad_x_low = send(grad_low, "swap")
    own, other = pack_small(pieces, bin_row, width)
    if placed:
        joined_att, merged_low, ended_above = sums_call(
            "tail_one", join_attention(qkv_k, qkv_g), merge_ways(turned_low),
            merge((*merged_ffn, z_bit), (*cut_line, 1)), after=(own,),
        )
        turned_att, ended_low, (sums,) = sums_call(
            "tail_two", turn_ways(joined_att), merge((*merged_low, z_bit)),
            add_small(own, other, "y"),
        )
        merged_att, (near_1, far_1), (sums,) = sums_call(
            "tail_three", merge_ways(turned_att), part_sides(8, *ended_above),
            add_small(sums, sums, 0),
        )
        ended_att, (sums,) = sums_call(
            "tail_four", merge((*merged_att, z_bit)), add_small(sums, sums, 1)
        )
        ((sums,),) = sums_call("tail_five", add_small(sums, sums, 2), after=ended_att[1:2])
        out_act, grad_x = widen_call((out_low, grad_x_low), (sums,))
        ended_ffn = [(0, pairs((*ended_low, 3))), (0, pairs((*ended_above, 3)))]
        ended_attention = [(0, pairs((*ended_att, 3))), (0, pairs((near_1, far_1, "y")))]
        grad_w_up, grad_w_down, grad_w_qkv, grad_w_out = emit_call(ended_ffn, ended_attention)
        terms = (sums, send(sums, 3))
    else:
        grad_w_up, grad_w_down = (
            jnp.stack([
                jnp.concatenate([ffn[which, place] for place in range(PIECES)], axis=-1)
                for ffn, _ in plain
            ])
            for which in range(2)
        )
        grad_w_qkv = jnp.stack([entry[1][:3] for entry in plain])
        grad_w_out = jnp.stack([entry[1][3] for entry in plain])
        out_act, grad_x = widen_call((out_low, grad_x_low))
        sums = own + send(other, "y")
        for bit in range(bits - 1):
            sums = sums + send(sums, bit)
        terms = (sums, send(sums, bits - 1))
    replicated, sharded_qkv, sharded_up, bin_density, count = unpack_small(
        terms, depth, part, units
    )

    return (
        out_act,
        grad_x,
        replicated[0],
        replicated[1],
        jnp.transpose(grad_w_qkv, (0, 2, 1, 3)),
        jnp.transpose(sharded_qkv, (1, 0, 2)),
        jnp.transpose(grad_w_out, (0, 2, 1)),
        replicated[4],
        replicated[2],
        replicated[3],
        grad_w_up,
        sharded_up,
        jnp.transpose(grad_w_down, (0, 2, 1)),
        replicated[5],
        bin_density[0, :BINS],
        count[0, 0],
    )


def solution(mesh):
    placed = (
        P(("dp", "tensor"), None),
        P("dp", None),
        P(("dp", "tensor")),
        P(),
        P(),
        P(None, None, None, "tensor"),
        P(None, None, "tensor"),
        P(None, "tensor", None),
        P(),
        P(),
        P(),
        P(None, None, "tensor"),
        P(None, "tensor"),
        P(None, "tensor", None),
        P(),
        P(),
        P(),
        P(("dp", "tensor"), None),
    )
    return jax.shard_map(
        per_device,
        mesh=mesh,
        in_specs=placed,
        out_specs=(
            P(("dp", "tensor"), None),
            P(("dp", "tensor"), None),
            P(),
            P(),
            P(None, "dp", None, "tensor"),
            P(None, None, "tensor"),
            P(None, "tensor", "dp"),
            P(),
            P(),
            P(),
            P(None, "dp", "tensor"),
            P(None, "tensor"),
            P(None, "tensor", "dp"),
            P(),
            P(),
            P(),
        ),
        check_vma=False,
    )
```

```python
import functools

import jax
import jax.numpy as jnp
from jax import lax
from jax.experimental import pallas as pl
from jax.experimental.pallas import tpu as pltpu
from jax.sharding import PartitionSpec as P

HEAD_DIM = 64
HALF = HEAD_DIM // 2
BINS = 24
LANES = 128
PIECES = 4
VMEM_MIB = {}
COSTS = {}

eps = 1e-05
theta = 10000.0
special_ids = 5
far = -1e30

bf16 = jnp.bfloat16
f32 = jnp.float32
AXES = ("dp", "tensor")


def dot(a, b):
    return jnp.dot(a, b, preferred_element_type=f32)


def dot_nt(a, b):
    return lax.dot_general(a, b, (((1,), (1,)), ((), ())), preferred_element_type=f32)


def normalize(rows):
    centre = rows - jnp.mean(rows, axis=-1, keepdims=True)
    spread = jnp.mean(centre * centre, axis=-1, keepdims=True)
    scale = lax.rsqrt(spread + eps)
    return centre * scale, scale


def norm_backward(rows, gain, grad):
    unit, scale = normalize(rows)
    gained = grad * gain
    mean_grad = jnp.mean(gained, axis=-1, keepdims=True)
    mean_both = jnp.mean(gained * unit, axis=-1, keepdims=True)
    below = scale * (gained - mean_grad - unit * mean_both)
    return below, column_sum(grad * unit), column_sum(grad)


def column_sum(rows):
    return jnp.sum(rows, axis=0, keepdims=True)


def rotate(rows, cosine, sine, sign):
    lane = lax.broadcasted_iota(jnp.int32, cosine.shape, 1)
    low = lane % HEAD_DIM < HALF
    pieces = []
    for start in range(0, rows.shape[1], LANES):
        piece = rows[:, start : start + LANES]
        other = jnp.where(low, pltpu.roll(piece, LANES - HALF, 1), pltpu.roll(piece, HALF, 1))
        pieces.append(piece * cosine + sign * (other * sine))
    return jnp.concatenate(pieces, axis=1)


def gelu_pair(value):
    size = jnp.abs(value) * (2.0**-0.5)
    t = 1.0 / (1.0 + 0.3275911 * size)
    bell = jnp.exp(-0.5 * value * value)
    poly = t * (
        0.5 * 0.254829592
        + t
        * (
            0.5 * -0.284496736
            + t * (0.5 * 1.421413741 + t * (0.5 * -1.453152027 + t * (0.5 * 1.061405429)))
        )
    )
    tail = poly * bell
    share = jnp.where(value < 0, tail, 1.0 - tail)
    return value * share, share + value * bell * 0.3989422804014327


def three_parts(column):
    high = column.astype(bf16).astype(f32)
    rest = column - high
    middle = rest.astype(bf16).astype(f32)
    return high, middle, rest - middle


def spec(shape, index=None):
    zeros = (0,) * len(shape)
    return pl.BlockSpec(shape, index or (lambda i, *s: zeros))


def whole(array):
    return array, spec(array.shape)


def hot(array):
    return array, spec(array.shape), True


def cold(array):
    return pltpu.with_memory_space_constraint(array, pltpu.HBM)


def shaped(shape, dtype):
    return jax.ShapeDtypeStruct(shape, dtype)


def call(
    name, kernel, steps, operands, results, prefetch=(), scratch=(), alias=(), after=(), sides=()
):
    def side_spec(shape):
        lead = (0,) * (len(shape) - 1)
        return spec(
            tuple(shape[:-1]) + (shape[-1] // 3,), lambda i, *s: (*lead, jnp.minimum(i, 2))
        )

    own_in, own_out = len(operands), len(results)
    idle = [array for array, _ in alias] + list(after)
    arrays = [entry[0] if len(entry) > 2 else cold(entry[0]) for entry in operands]
    in_specs = [entry[1] for entry in operands]
    out_specs = [entry[2] for entry in results]
    out_shape = [
        (shaped if len(entry) > 3 else pltpu.HBM)(entry[0], entry[1]) for entry in results
    ]
    for _, side_args, side_shapes in sides:
        in_specs += [side_spec(arg.shape) for arg in side_args]
        out_specs += [side_spec(getattr(shape, "shape", shape)) for shape in side_shapes]
        out_shape += [
            shape if hasattr(shape, "dtype") else shaped(shape, bf16) for shape in side_shapes
        ]
        arrays += side_args
    ahead, count_in, count_out = len(prefetch), len(in_specs), len(out_specs)

    def body(*refs):
        early, refs = refs[:ahead], refs[ahead + len(idle) :]
        ins, outs, rest = (
            refs[:count_in], refs[count_in : count_in + count_out], refs[count_in + count_out :]
        )
        if kernel is not None:
            kernel(*early, *ins[:own_in], *outs[:own_out], *rest)

        def run_sides():
            at_in, at_out = own_in, own_out
            for side_kernel, side_args, side_shapes in sides:
                side_kernel(
                    *ins[at_in : at_in + len(side_args)], *outs[at_out : at_out + len(side_shapes)]
                )
                at_in, at_out = at_in + len(side_args), at_out + len(side_shapes)

        if sides and steps > 3:
            pl.when(pl.program_id(0) < 3)(run_sides)
        else:
            run_sides()

    made = pl.pallas_call(
        body,
        grid_spec=pltpu.PrefetchScalarGridSpec(
            num_scalar_prefetch=ahead,
            grid=(steps,),
            in_specs=[pl.BlockSpec(memory_space=pl.ANY)] * len(idle) + in_specs,
            out_specs=out_specs,
            scratch_shapes=list(scratch),
        ),
        out_shape=out_shape,
        name=name,
        input_output_aliases={
            ahead + place: result for place, (_, result) in enumerate(alias)
        },
        compiler_params=pltpu.CompilerParams(vmem_limit_bytes=VMEM_MIB.get(name, 44) << 20),
        cost_estimate=pl.CostEstimate(
            flops=int(COSTS.get(name, 6e10)), bytes_accessed=int(4e6), transcendentals=0
        ),
    )
    outs = made(*prefetch, *idle, *arrays)
    done, at = list(outs[:own_out]), own_out
    for _, _, side_shapes in sides:
        done.append(outs[at : at + len(side_shapes)])
        at += len(side_shapes)
    return done


def gate(array, after):
    return lax.optimization_barrier((array, *after))[0]


def gather_rows(target, slots, pieces, lane=0):
    count, lanes = pieces[0].shape
    for place, piece in enumerate(pieces):
        start = pl.multiple_of(slots[place] * count, 16)
        target[pl.ds(start, count), lane : lane + lanes] = piece[...]


def qkv_kernel(number, base, members, first, distant, *refs):
    refs = list(refs)
    slots = refs.pop(0) if distant else None
    if first:
        x, gain, bias, turn = refs[:4]
        refs = refs[4:]
    else:
        normed = refs.pop(0)
    pieces, refs = (refs[:PIECES], refs[PIECES:]) if distant else (refs[:1], refs[1:])
    b, cosine, sine, *refs = refs
    if first:
        normed, n_t, *refs = refs
    queries = refs.pop(0) if 0 in members else None
    kv = refs.pop(0) if 1 in members else None
    step = pl.program_id(0)
    if first:

        @pl.when(step == 0)
        def _():
            unit, _ = normalize(x[...].astype(f32))
            normed[...] = (
                unit * gain[number : number + 1] + bias[number : number + 1]
            ).astype(bf16)
            n_t[...] = dot_nt(turn[...], normed[...]).astype(bf16)

    if distant:
        (matrix,) = refs
        gather_rows(matrix, slots, pieces)
        weight = matrix[...]
    else:
        weight = pieces[0][0, 0]
    mixed = dot(normed[...], weight) + b[0, number : number + 1]
    for member in members:

        @pl.when(step == member - base)
        def _(member=member):
            if member == 0:
                turned = rotate(mixed, cosine[...], sine[...], 1.0)
                queries[...] = (turned * HEAD_DIM**-0.5).astype(bf16)
            elif member == 1:
                kv[0] = rotate(mixed, cosine[...], sine[...], 1.0).astype(bf16)
            else:
                kv[0] = mixed.astype(bf16)


def qkv_call(number, members, rows_in, norm, weight, b, tables, prior=(), after=()):
    first, distant = norm is not None, isinstance(weight, tuple)
    rows, width = rows_in.shape
    part = b.shape[2]
    base = members[0]
    operands = [hot(rows_in)]
    if first:
        operands += [whole(array) for array in norm[:2]] + [hot(norm[2])]
    prefetch, scratch = (), ()
    if distant:
        slots, pieces, lead = weight
        prefetch = (slots,)
        operands += [
            (piece, spec((width // PIECES, part), lambda i, *s: (i + lead, 0)), True)
            for piece in pieces
        ]
        scratch = (pltpu.VMEM((width, part), bf16),)
    else:
        block = spec((1, 1, width, part), lambda i, *s: (number, i + base, 0, 0))
        operands.append((weight, block))
    operands.append((b, spec((1, b.shape[1], part), lambda i, *s: (i + base, 0, 0))))
    operands += [hot(table) for table in tables]
    half = 1 if distant else 0
    results = []
    if first:
        results += [
            ((rows, width), bf16, spec((rows, width)), True),
            ((width, rows), bf16, spec((width, rows))),
        ]
    alias = []
    if 0 in members:
        if prior:
            alias.append((prior[0], len(results)))
        results.append(
            ((rows, 2 * part), bf16, spec((rows, part), lambda i, *s: (0, half)), True)
        )
    if 1 in members:
        if prior:
            alias.append((prior[-1], len(results)))
        block = spec(
            (1, rows, part), lambda i, *s: (jnp.maximum(i + base - 1, 0), 0, half)
        )
        results.append(((2, rows, 2 * part), bf16, block, True))
    return call(
        "qkv",
        functools.partial(qkv_kernel, number, base, members, first, distant),
        len(members),
        operands,
        results,
        prefetch,
        scratch,
        alias,
        after,
    )


def head_lanes(shape, head):
    lane = lax.broadcasted_iota(jnp.int32, shape, 1)
    return (lane < HEAD_DIM) if head == 0 else (lane >= HEAD_DIM)


def attention_kernel(q, kv, kv_far, q_mark, k_mark, k_mark_far, out, logsum):
    rows = q.shape[0]
    queries = q[...]
    scores, values = [], []
    for head in range(2):
        mine = head_lanes((rows, LANES), head)
        marked = jnp.where(mine, queries, q_mark[...])
        for pair, mark in ((kv, k_mark), (kv_far, k_mark_far)):
            scores.append(dot_nt(marked, jnp.where(mine, pair[0], mark[...])))
            values.append(jnp.where(mine, pair[1], jnp.ones_like(pair[1])))
    highest, expos = [], []
    for head in range(2):
        near, distant = scores[2 * head : 2 * head + 2]
        highest.append(
            jnp.maximum(
                jnp.max(near, axis=-1, keepdims=True), jnp.max(distant, axis=-1, keepdims=True)
            )
        )
        expos += [jnp.exp(score - highest[head]).astype(bf16) for score in (near, distant)]
    results, logs = [], []
    for head in range(2):
        total = dot(expos[2 * head], values[2 * head])
        total = total + dot(expos[2 * head + 1], values[2 * head + 1])
        column = HEAD_DIM if head == 0 else 0
        summed = total[:, column : column + 1]
        results.append(total / summed)
        logs.append(highest[head] + jnp.log(summed))
    out[...] = jnp.where(head_lanes((rows, LANES), 0), results[0], results[1]).astype(bf16)
    logsum[...] = jnp.where(head_lanes((rows, LANES), 0), logs[1], logs[0])


def head_specs(rows):
    column = spec((rows, LANES), lambda i, *s: (0, i))
    both = spec((2, rows, LANES), lambda i, *s: (0, 0, i))
    return column, both


def attention_call(q, kv, kv_far, marks, after=(), sides=()):
    rows, width = q.shape
    column, both = head_specs(rows)
    return call(
        "attention",
        attention_kernel,
        width // LANES,
        [(q, column, True), (kv, both, True), (kv_far, both, True)] + [hot(mark) for mark in marks],
        [((rows, width), bf16, column), ((rows, width), f32, column)],
        after=after,
        sides=sides,
    )


def attention_back_kernel(
    q, kv, kv_far, q_mark, k_mark, k_mark_far, logsum, attended, grad, cosine, sine,
    grad_q, grad_kv, grad_kv_far,
):
    rows = q.shape[0]
    queries = q[...]
    grads = grad[...]
    lane = lax.broadcasted_iota(jnp.int32, (rows, LANES), 1) % HEAD_DIM
    logs = three_parts(logsum[...])
    log_mark = sum(
        jnp.where(lane == 3 + place, part, 0.0) for place, part in enumerate(logs)
    ).astype(bf16)
    product = attended[...].astype(f32) * grads.astype(f32)
    value_mark = jnp.where(lane < 3, -1.0, 0.0).astype(bf16)
    dots_t = []
    keys_t = [
        jnp.transpose(pair[0].astype(f32)).astype(bf16) for pair in (kv, kv_far)
    ]
    outs = ([], [])
    for head in range(2):
        mine = head_lanes((rows, LANES), head)
        centre = jnp.sum(jnp.where(mine, product, 0.0), axis=-1, keepdims=True)
        centre_mark = sum(
            jnp.where(lane == place, part, 0.0) for place, part in enumerate(three_parts(centre))
        ).astype(bf16)
        marked = jnp.where(mine, queries, q_mark[...] + log_mark)
        marked_grads = jnp.where(mine, grads, centre_mark)
        turned = 0.0
        for place, (pair, mark) in enumerate(((kv, k_mark), (kv_far, k_mark_far))):
            keys = jnp.where(mine, pair[0], mark[...])
            values = jnp.where(mine, pair[1], value_mark)
            probs = jnp.exp(dot_nt(keys, marked))
            grad_scores = (probs * dot_nt(values, marked_grads)).astype(bf16)
            grad_values = dot(probs.astype(bf16), grads)
            grad_keys = dot(grad_scores, queries)
            turned = turned + dot(
                keys_t[place][head * HEAD_DIM : (head + 1) * HEAD_DIM], grad_scores
            )
            outs[place].append((grad_keys, grad_values))
        dots_t.append(turned)
    grad_queries = jnp.transpose(jnp.concatenate(dots_t, axis=0)) * HEAD_DIM**-0.5
    grad_q[...] = rotate(grad_queries, cosine[...], sine[...], -1.0).astype(bf16)
    mine = head_lanes((rows, LANES), 0)
    for ref, (one, two) in zip((grad_kv, grad_kv_far), outs):
        for member in range(2):
            ref[member] = jnp.where(mine, one[member], two[member]).astype(ref.dtype)


def attention_back_call(q, kv, kv_far, marks, logsum, attended, grad, tables, after=(), sides=()):
    rows, width = q.shape
    column, both = head_specs(rows)
    return call(
        "attention_back",
        attention_back_kernel,
        width // LANES,
        [(q, column), (kv, both), (kv_far, both)]
        + [hot(mark) for mark in marks]
        + [(logsum, column), (attended, column), (grad, column, True)]
        + [hot(table) for table in tables],
        [
            ((rows, width), bf16, column, True),
            ((2, rows, width), bf16, both, True),
            ((2, rows, width), bf16, both, True),
        ],
        after=after,
        sides=sides,
    )


def out_operands(pieces, part, row):
    low = part // PIECES
    return [
        (piece, spec((low, part), lambda i, *s, side=side: (row // low + side, 0)), True)
        for side in range(2)
        for piece in pieces
    ]


def gather_out(target, slots, pieces):
    part = target.shape[0]
    for side in range(2):
        gather_rows(target, slots, pieces[side * PIECES :][:PIECES], side * part)


def ffn_kernel(number, slots, *refs):
    x, att, wo_n = refs[:3]
    wo_pieces, refs = refs[3 : 3 + 2 * PIECES], refs[3 + 2 * PIECES :]
    (b_out, gain, bias, b_down, turn, w_up, b_up, w_down,
     middle, normed, n_t, active, slope, acc, wo_o) = refs
    row = slice(number, number + 1)

    @pl.when(pl.program_id(0) == 0)
    def _():
        part = wo_o.shape[0]
        gather_out(wo_o, slots, wo_pieces)
        mid = (
            x[...].astype(f32)
            + dot(att[:, :part], wo_n[0])
            + dot(att[:, part:], wo_o[...])
            + b_out[row]
        )
        middle[...] = mid
        unit, _ = normalize(mid)
        normed[...] = (unit * gain[row] + bias[row]).astype(bf16)
        n_t[...] = dot_nt(turn[...], normed[...]).astype(bf16)
        acc[...] = mid + b_down[row]

    hidden = dot(normed[...], w_up[0]) + b_up[row]
    value, back = gelu_pair(hidden)
    value = value.astype(bf16)
    active[...] = value
    slope[...] = back.astype(bf16)
    acc[...] += dot(value, w_down[0])


def ffn_call(number, x, att, w_out, heads_far, small, turn, w_up, b_up, w_down, after=()):
    rows, width = x.shape
    units, part = w_up.shape[2], w_out.shape[1]
    slots, pieces, row = heads_far
    b_out, gain, bias, b_down = small
    block = 2 * units // PIECES
    wide = spec((rows, block), lambda i, *s: (0, i))
    full = spec((rows, width))
    return call(
        "ffn",
        functools.partial(ffn_kernel, number),
        units // block,
        [
            whole(x),
            whole(att),
            (w_out, spec((1, part, width), lambda i, *s: (number, 0, 0))),
            *out_operands(pieces, part, row),
            *[whole(array) for array in (b_out, gain, bias, b_down)],
            hot(turn),
            (w_up, spec((1, width, block), lambda i, *s: (number, 0, i))),
            (b_up, spec((b_up.shape[0], block), lambda i, *s: (0, i))),
            (w_down, spec((1, block, width), lambda i, *s: (number, i, 0))),
        ],
        [
            ((rows, width), f32, full),
            ((rows, width), bf16, full, True),
            ((width, rows), bf16, spec((width, rows))),
            ((rows, units), bf16, wide),
            ((rows, units), bf16, wide),
            ((rows, width), f32, full, True),
        ],
        prefetch=(slots,),
        scratch=(pltpu.VMEM((part, width), bf16),),
        after=after,
    )


def far_ffn_operands(up_far, down_far, width, units):
    slots_u, ups = up_far
    slots_d, downs = down_far
    block = 2 * units // PIECES

    def at(i, slots):
        return slots[jnp.clip(i, 0, 1)] // 2

    ups = [
        (piece, spec((width // PIECES, block), lambda i, *s: (0, at(i, s[0]))), True)
        for piece in ups
    ]
    downs = [(piece, spec((units // PIECES, width)), True) for piece in downs]
    return ups, downs, at, (slots_d, slots_u)


def gather_down(target, step, slots, downs):
    for place in range(2):

        @pl.when(step == place)
        def _(place=place):
            for which in (place, place + 2):
                count = downs[which].shape[0]
                start = pl.multiple_of((slots[which] % 2) * count, 16)
                target[pl.ds(start, count), :] = downs[which][...]


def ffn_far_kernel(number, slots_d, slots_u, normed, acc_in, b_up, *refs):
    ups, downs = refs[:PIECES], refs[PIECES : 2 * PIECES]
    active, slope, acc, low, w_up, w_down = refs[2 * PIECES :]
    step = pl.program_id(0)

    @pl.when(step == 0)
    def _():
        acc[...] = acc_in[...]

    gather_rows(w_up, slots_u, ups)
    gather_down(w_down, step, slots_d, downs)
    hidden = dot(normed[...], w_up[...]) + b_up[number : number + 1]
    value, back = gelu_pair(hidden)
    value = value.astype(bf16)
    active[...] = value
    slope[...] = back.astype(bf16)
    acc[...] += dot(value, w_down[...])

    @pl.when(step == pl.num_programs(0) - 1)
    def _():
        low[...] = acc[...].astype(bf16)


def ffn_far_call(number, normed, acc, up_far, down_far, b_up, after=()):
    rows, width = normed.shape
    units = b_up.shape[1]
    block = 2 * units // PIECES
    ups, downs, at, prefetch = far_ffn_operands(up_far, down_far, width, units)
    wide = spec((rows, block), lambda i, *s: (0, at(i, s[0])))
    full = spec((rows, width))
    return call(
        "ffn_far",
        functools.partial(ffn_far_kernel, number),
        2,
        [
            hot(normed),
            hot(acc),
            (b_up, spec((b_up.shape[0], block), lambda i, *s: (0, at(i, s[0])))),
            *ups,
            *downs,
        ],
        [
            ((rows, units), bf16, wide),
            ((rows, units), bf16, wide),
            ((rows, width), f32, full),
            ((rows, width), bf16, full),
        ],
        prefetch=prefetch,
        scratch=(pltpu.VMEM((width, block), bf16), pltpu.VMEM((block, width), bf16)),
        after=after,
    )


def split_rows(product, keep, send, at):
    half = product.shape[0] // 2
    product = product.astype(bf16)
    keep[at] = product[:half]
    send[at] = product[half:]


def ffn_back_kernel(slots_d, slots_u, *refs):
    (g, n_t, g_t, active_n, slope_n, up_n, down_n, active_o, slope_o) = refs[:9]
    ups, downs = refs[9 : 9 + PIECES], refs[9 + PIECES : 9 + 2 * PIECES]
    acc, keep, send, b_up, up_o, down_o = refs[9 + 2 * PIECES :]
    step = pl.program_id(0)

    @pl.when(step == 0)
    def _():
        acc[...] = jnp.zeros_like(acc)

    def one(active, slope, w_up, w_down):
        grad_active = dot_nt(g[...], w_down)
        grad_hidden = (grad_active * slope[...].astype(f32)).astype(bf16)
        b_up[0] = column_sum(grad_hidden.astype(f32))
        acc[...] += dot_nt(grad_hidden, w_up)
        for which, product in enumerate(
            (dot(n_t[...], grad_hidden), dot(g_t[...], active[...]))
        ):
            block = product.shape[1] // 2
            for place in range(2):
                split_rows(
                    product[:, place * block : (place + 1) * block], keep, send, (0, which, place)
                )

    @pl.when(step < 2)
    def _():
        gather_rows(up_o, slots_u, ups)
        gather_down(down_o, step, slots_d, downs)
        one(active_o, slope_o, up_o[...], down_o[...])

    @pl.when(step >= 2)
    def _():
        one(active_n, slope_n, up_n[0], down_n[0])


def ffn_back_call(
    number, g, n_t, g_t, near, distant, w_up, w_down, up_far, down_far, after=(), sides=()
):
    rows, width = g.shape
    units = w_up.shape[2]
    block = 2 * units // PIECES
    ups, downs, at, prefetch = far_ffn_operands(up_far, down_far, width, units)

    def near_block(i):
        return jnp.maximum(i - 2, 0)

    def result_block(i, s):
        return jnp.where(i < 2, at(i, s[0]), near_block(i))

    def side(i):
        return jnp.where(i < 2, 1, 0)

    near_wide = spec((rows, block), lambda i, *s: (0, near_block(i)))
    far_wide = spec((rows, block), lambda i, *s: (0, at(i, s[0])))
    grads = spec(
        (1, 2, 2, width // 2, block // 2), lambda i, *s: (side(i), 0, result_block(i, s), 0, 0)
    )
    grads_shape = (2, 2, PIECES, width // 2, block // 2)
    return call(
        "ffn_back",
        ffn_back_kernel,
        4,
        [
            hot(g),
            whole(n_t),
            hot(g_t),
            *[(array, near_wide) for array in near],
            (w_up, spec((1, width, block), lambda i, *s: (number, 0, near_block(i)))),
            (w_down, spec((1, block, width), lambda i, *s: (number, near_block(i), 0))),
            *[(array, far_wide) for array in distant],
            *ups,
            *downs,
        ],
        [
            ((rows, width), f32, spec((rows, width)), True),
            (grads_shape, bf16, grads),
            (grads_shape, bf16, grads),
            ((2, 1, units), f32,
             spec((1, 1, block), lambda i, *s: (side(i), 0, result_block(i, s)))),
        ],
        prefetch=prefetch,
        scratch=(pltpu.VMEM((width, block), bf16), pltpu.VMEM((block, width), bf16)),
        after=after,
        sides=sides,
    )


def middle_back_kernel(number, slots, acc, middle, gain, g, wo_n, *refs):
    wo_pieces, refs = refs[: 2 * PIECES], refs[2 * PIECES :]
    turn, grad_middle, grad_att, low_t, smalls, wo_o, low = refs
    step = pl.program_id(0)
    part = wo_o.shape[0]

    @pl.when(step == 0)
    def _():
        below, d_gain, d_bias = norm_backward(middle[...], gain[number : number + 1], acc[...])
        total = below + g[...].astype(f32)
        grad_middle[...] = total
        low[...] = total.astype(bf16)
        smalls[0:1] = d_gain
        smalls[1:2] = d_bias
        smalls[2:3] = column_sum(total)

    @pl.when(step == 1)
    def _():
        gather_out(wo_o, slots, wo_pieces)
        grad_att[:, :part] = dot_nt(low[...], wo_n[0]).astype(bf16)
        grad_att[:, part:] = dot_nt(low[...], wo_o[...]).astype(bf16)

    @pl.when(step == 2)
    def _():
        low_t[...] = dot_nt(turn[...], low[...]).astype(bf16)


def middle_back_call(number, acc, middle, gain, g, w_out, heads_far, turn, after=(), sides=()):
    rows, width = acc.shape
    part = w_out.shape[1]
    slots, pieces, row = heads_far
    return call(
        "middle_back",
        functools.partial(middle_back_kernel, number),
        3,
        [
            hot(acc),
            *[whole(array) for array in (middle, gain, g)],
            (w_out, spec((1, part, width), lambda i, *s: (number, 0, 0))),
            *out_operands(pieces, part, row),
            hot(turn),
        ],
        [
            ((rows, width), f32, spec((rows, width)), True),
            ((rows, width), bf16, spec((rows, width)), True),
            ((width, rows), bf16, spec((width, rows)), True),
            ((3, width), f32, spec((3, width))),
        ],
        prefetch=(slots,),
        scratch=(pltpu.VMEM((part, width), bf16), pltpu.VMEM((rows, width), bf16)),
        after=after,
        sides=sides,
    )


def qkv_back_kernel(number, weight, rows_grad, *refs):
    refs = list(refs)
    slots = (refs.pop(0), refs.pop(0)) if rows_grad else None
    gq, kv, kv_far, cosine, sine = refs[:5]
    refs = refs[5:]
    if weight:
        n_t, gm_t, att, *refs = refs
    if rows_grad:
        w_n, *refs = refs
        pieces, refs = refs[: 3 * PIECES], refs[3 * PIECES :]
        x, gain, g, turn, *refs = refs
    if weight:
        keep, send, b, *refs = refs
    if rows_grad:
        acc, low, low_t, smalls, matrix, *refs = refs
    (mixed,) = refs
    step = pl.program_id(0)
    part = gq.shape[1]

    def lanes(member):
        return slice(member * part, (member + 1) * part)

    mixed[:, lanes(0)] = gq[...]
    keys = rotate(
        kv[0].astype(f32) + kv_far[0].astype(f32), cosine[...], sine[...], -1.0
    )
    mixed[:, lanes(1)] = keys.astype(bf16)
    mixed[:, lanes(2)] = plus(kv[1], kv_far[1])
    if weight:
        sums = column_sum(mixed[...].astype(f32))
        product = dot(n_t[...], mixed[...])
        for member in range(3):
            b[0, member] = sums[:, lanes(member)]
            split_rows(product[:, lanes(member)], keep, send, (0, member))
        split_rows(dot(gm_t[...], att[...]), keep, send, (0, 3))
    if rows_grad:

        @pl.when(step == 0)
        def _():
            for member in range(3):
                matrix[:, lanes(member)] = w_n[0, member]
            acc[...] = dot_nt(mixed[...], matrix[...])

        @pl.when(step == 1)
        def _():
            for member in range(3):
                gather_rows(
                    matrix, slots[min(member, 1)], pieces[member * PIECES :][:PIECES],
                    member * part,
                )
            whole_grad = acc[...] + dot_nt(mixed[...], matrix[...])
            below, d_gain, d_bias = norm_backward(
                x[...].astype(f32), gain[number : number + 1], whole_grad
            )
            total = below + g[...]
            acc[...] = total
            low[...] = total.astype(bf16)
            low_t[...] = dot_nt(turn[...], low[...]).astype(bf16)
            smalls[0:1] = d_gain
            smalls[1:2] = d_bias
            smalls[2:3] = column_sum(total)


def qkv_back_call(
    number, gq, kv, kv_far, tables, sources=None, weights=None, ending=None, after=()
):
    rows = gq.shape[0]
    part = gq.shape[1] // 2
    width = 2 * part
    column = spec((rows, part), lambda i, *s: (0, i))
    both = spec((2, rows, part), lambda i, *s: (0, 0, i))
    operands = [(gq, column, True), (kv, both, True), (kv_far, both, True), *[hot(table) for table in tables]]
    results, prefetch, scratch = [], (), []
    if sources is not None:
        n_t, gm_t, att = sources
        operands += [whole(n_t), hot(gm_t), (att, column)]
        grads = spec((1, 4, width // 2, part), lambda i, *s: (i, 0, 0, 0))
        results += [((2, 4, width // 2, part), bf16, grads)] * 2
        results.append(
            ((2, 3, 1, part), f32, spec((1, 3, 1, part), lambda i, *s: (i, 0, 0, 0)))
        )
    if weights is not None:
        w_n, members = weights
        prefetch = (members[0][0], members[1][0])
        operands.append((w_n, spec((1, 3, width, part), lambda i, *s: (number, 0, 0, 0))))
        operands += [
            (piece, spec((width // PIECES, part), lambda i, *s, lead=lead: (lead, 0)), True)
            for _, pieces, lead in members
            for piece in pieces
        ]
        x, gain, g, turn = ending
        operands += [whole(x), whole(gain), hot(g), hot(turn)]
        results += [
            ((rows, width), f32, spec((rows, width))),
            ((rows, width), bf16, spec((rows, width)), True),
            ((width, rows), bf16, spec((width, rows)), True),
            ((3, width), f32, spec((3, width))),
        ]
        scratch.append(pltpu.VMEM((width, 3 * part), bf16))
    scratch.append(pltpu.VMEM((rows, 3 * part), bf16))
    return call(
        "qkv_back",
        functools.partial(qkv_back_kernel, number, sources is not None, weights is not None),
        2,
        operands,
        results,
        prefetch=prefetch,
        scratch=scratch,
        after=after,
    )


def pack_call(number, slots, groups, after=()):
    operands, results, entries = [], [], []
    for which, matrices in groups:
        rows, places = 0, []
        matrices = [entry if isinstance(entry, tuple) else (entry, (0,)) for entry in matrices]
        lanes = matrices[0][0].shape[-1]
        for matrix, members in matrices:
            chunk, sides = matrix.shape[-2] // PIECES, matrix.shape[-1] // lanes
            middle = matrix.shape[1:-2]
            zeros = (0,) * len(middle)
            operands.append((
                matrix,
                spec(
                    (1, *middle, chunk, matrix.shape[-1]),
                    lambda i, *s, which=which, zeros=zeros: (number, *zeros, s[which][0], 0),
                ),
            ))
            places.append((rows, members, chunk, sides))
            rows += len(members) * chunk * sides
        results.append(((rows, lanes), bf16, spec((rows, lanes))))
        entries.append((places, lanes))

    def kernel(*refs):
        refs = refs[len(slots) :]
        outs = refs[len(operands) :]
        at = 0
        for out, (places, lanes) in zip(outs, entries):
            for row, members, chunk, sides in places:
                source = refs[at]
                at += 1
                for place, member in enumerate(members):
                    for side in range(sides):
                        cut = slice(side * lanes, (side + 1) * lanes)
                        start = row + (place * sides + side) * chunk
                        if len(source.shape) == 4:
                            piece = source[0, member, :, cut]
                        else:
                            piece = source[0, :, cut]
                        out[start : start + chunk] = piece

    return call("pack", kernel, 1, operands, results, prefetch=slots, after=after)


def plus(a, b):
    return (a.astype(f32) + b.astype(f32)).astype(bf16)


def join_ffn_kernel(keep, got, a_keep, a_send, b_keep, b_send):
    half = b_keep.shape[2]
    for place in range(a_keep.shape[0]):
        a_keep[place] = plus(keep[0, 0, place], got[0, 0, place])
        a_send[place] = plus(keep[1, 0, place], got[1, 0, place])
        for side in range(2):
            b_keep[side, place] = plus(keep[side, 1, place, :half], got[side, 1, place, :half])
            b_send[side, place] = plus(keep[side, 1, place, half:], got[side, 1, place, half:])


def join_ffn_call(keep, got, after=()):
    deep, cols = keep.shape[3:]
    source = spec((2, 2, 1, deep, cols), lambda i, *s: (0, 0, i, 0, 0))
    one = ((PIECES, deep, cols), bf16, spec((1, deep, cols), lambda i, *s: (i, 0, 0)), True)
    two = (
        (2, PIECES, deep // 2, cols), bf16,
        spec((2, 1, deep // 2, cols), lambda i, *s: (0, i, 0, 0)),
        True,
    )
    return call(
        "join_ffn", join_ffn_kernel, PIECES, [(keep, source), (got, source, True)],
        [one, one, two, two], after=after,
    )


def join_attention_kernel(keep, got, a_keep, a_send, b_keep, b_send):
    half = b_keep.shape[2]
    for member in range(2):
        a_keep[member] = plus(keep[0, member], got[0, member])
        a_send[member] = plus(keep[1, member], got[1, member])
        for side in range(2):
            kept, came = keep.at[side, 2 + member], got.at[side, 2 + member]
            b_keep[side, member] = plus(kept[:half], came[:half])
            b_send[side, member] = plus(kept[half:], came[half:])


def join_line_kernel(keep, got, next_keep, next_send):
    half, quarter = keep.shape[2] // 2, next_keep.shape[2]
    for side in range(2):
        for member in range(4):
            for x in range(2):
                for start, ref in ((x * half, next_keep), (x * half + quarter, next_send)):
                    cut = slice(start, start + quarter)
                    ref[4 * side + member, x] = plus(
                        keep[side, member, cut], got[side, member, cut]
                    )


def cut_kernel(keep, got, next_keep, next_send):
    for member in range(keep.shape[0]):
        next_keep[member] = plus(keep[member, 0], got[member, 0])
        next_send[member] = plus(keep[member, 1], got[member, 1])


def inner_kernel(keep, got, next_keep, next_send):
    half = next_keep.shape[2]
    for member in range(keep.shape[0]):
        for x in range(2):
            next_keep[member, x] = plus(keep[member, x, :half], got[member, x, :half])
            next_send[member, x] = plus(keep[member, x, half:], got[member, x, half:])


def sum_kernel(keep, got, out):
    for member in range(keep.shape[0]):
        out[member] = plus(keep[member], got[member])


def turn_kernel(a_keep, a_got, b_keep, b_got, a_next, a_send, b_next, b_send):
    half = a_next.shape[1]
    for member in range(a_keep.shape[0]):
        a_next[member] = plus(a_keep[member, :half], a_got[member, :half])
        a_send[member] = plus(a_keep[member, half:], a_got[member, half:])
    for member in range(b_keep.shape[1]):
        b_next[member] = plus(b_keep[0, member], b_got[0, member])
        b_send[member] = plus(b_keep[1, member], b_got[1, member])


def merge_kernel(*refs):
    keep, send = refs[-2:]
    half = keep.shape[1]
    place = 0
    for kept, got in zip(refs[:-2:2], refs[1:-2:2]):
        for member in range(kept.shape[0]):
            keep[place] = plus(kept[member, :half], got[member, :half])
            send[place] = plus(kept[member, half:], got[member, half:])
            place += 1


def part_kernel(first, keep, got, near, distant):
    for place in range(4):
        near[place] = plus(keep[first + place], got[first + place])
        distant[place] = plus(keep[first + 4 + place], got[first + 4 + place])


def add_kernel(a, b, out):
    out[...] = a[...] + b[...]


def sums_call(name, *sides, after=()):
    return call(name, None, 3, [], [], after=after, sides=sides)


def emit_call(ffn, attention):
    depth = len(ffn)
    terms = [array for _, arrays in ffn + attention for array in arrays]
    chunk, part = terms[0].shape[1:]
    shapes = [
        (depth, chunk, PIECES * part), (depth, chunk, PIECES * part),
        (depth, 3, chunk, part), (depth, chunk, part),
    ]

    def kernel(*refs):
        up, down, qkv, out = refs[len(terms) :]
        at = 0
        for number, (first, arrays) in enumerate(ffn):
            here = refs[at : at + len(arrays)]
            at += len(arrays)
            for place in range(2 * PIECES):
                total = sum(term[first + place].astype(f32) for term in here)
                start = place % PIECES * part
                (up, down)[place // PIECES][number, :, start : start + part] = total
        for number, (first, arrays) in enumerate(attention):
            here = refs[at : at + len(arrays)]
            at += len(arrays)
            for member in range(4):
                total = sum(term[first + member].astype(f32) for term in here)
                if member < 3:
                    qkv[number, member] = total
                else:
                    out[number] = total

    return call(
        "emit", kernel, 1, [whole(term) for term in terms],
        [(shape, f32, spec(shape)) for shape in shapes],
    )


def widen_call(arrays, after=()):
    def kernel(*refs):
        for source, out in zip(refs[: len(arrays)], refs[len(arrays) :]):
            out[...] = source[...].astype(f32)

    rows, width = arrays[0].shape
    block = spec((rows // 4, width), lambda i, *s: (i, 0))
    return call(
        "widen", kernel, 4, [(array, block, True) for array in arrays],
        [((rows, width), f32, block) for _ in arrays], after=after,
    )


def share_call(low, head, ids, class_bins, after):
    high = lax.Precision.HIGHEST

    def kernel(low, head, ids, class_bins, out):
        logits = dot_nt(low[...], head[...])
        expos = jnp.exp(logits - jnp.max(logits, axis=-1, keepdims=True))
        shares = expos / jnp.sum(expos, axis=-1, keepdims=True)
        mask = (ids[...] >= special_ids).astype(f32)
        sums = jnp.dot(mask, shares, precision=high, preferred_element_type=f32)
        bins = lax.broadcasted_iota(jnp.int32, (LANES, class_bins.shape[1]), 0)
        table = (bins == class_bins[...]).astype(f32)
        totals = lax.dot_general(
            jnp.broadcast_to(sums, (8, sums.shape[1])), table, (((1,), (1,)), ((), ())),
            precision=high, preferred_element_type=f32,
        )[0:1]
        lane = lax.broadcasted_iota(jnp.int32, (1, LANES), 1)
        out[...] = jnp.where(lane == BINS, jnp.sum(mask), jnp.where(lane < BINS, totals, 0.0))

    args = (low, head, ids, class_bins)
    return call(
        "share", kernel, 1, [whole(array) for array in args],
        [((1, LANES), f32, spec((1, LANES)))], after=(after,),
    )[0]


def pack_small(layers, bin_row, width):
    count = len(layers)
    part, units = layers[0][3].shape[3], layers[0][4].shape[2]
    folds = units // width
    shared = 6 * count + 1
    total = shared + count * (3 + folds)
    args = [array for layer in layers for array in layer] + [bin_row]

    def kernel(*refs):
        own, other = refs[-1].at[0], refs[-1].at[1]
        own[...] = jnp.zeros((total, width), f32)
        for number in range(count):
            one, two, down, _, _ = refs[5 * number : 5 * number + 5]
            own[6 * number : 6 * number + 2] = one[0:2]
            own[6 * number + 2 : 6 * number + 5] = two[...]
            own[6 * number + 5 : 6 * number + 6] = down[down.shape[0] - 1 :]
        bins = refs[5 * count]
        own[6 * count : 6 * count + 1, : bins.shape[1]] = bins[...]
        other[...] = own[...]
        for number in range(count):
            qkv, up = refs[5 * number + 3 : 5 * number + 5]
            start = shared + number * (3 + folds)
            for side, out in enumerate((own, other)):
                for member in range(3):
                    out[start + member : start + member + 1, :part] = qkv[side, member]
                for fold in range(folds):
                    row = start + 3 + fold
                    out[row : row + 1] = up[side, :, fold * width : (fold + 1) * width]

    shape = (2, total, width)
    return call(
        "pack_small", kernel, 1, [whole(array) for array in args], [(shape, f32, spec(shape))]
    )[0]


def unpack_small(terms, count, part, units):
    width = terms[0].shape[1]
    folds = units // width
    shared = 6 * count + 1

    def kernel(*refs):
        outs = refs[len(terms) :]
        sums = sum(term[...] for term in refs[: len(terms)])
        qkv, up, bins, tokens = outs[6:]
        for number in range(count):
            for member in range(6):
                row = 6 * number + member
                outs[member][number : number + 1] = sums[row : row + 1]
            start = shared + number * (3 + folds)
            for member in range(3):
                row = start + member
                qkv[member, number : number + 1] = sums[row : row + 1, :part]
            for fold in range(folds):
                row = start + 3 + fold
                up[number : number + 1, fold * width : (fold + 1) * width] = sums[row : row + 1]
        row = sums[6 * count : 6 * count + 1, :LANES]
        tally = row[:, BINS : BINS + 1]
        bins[...] = BINS * row / jnp.maximum(tally, 1.0)
        tokens[...] = jnp.broadcast_to(tally, tokens.shape).astype(jnp.int32)

    shapes = [((count, width), f32)] * 6 + [
        ((3, count, part), f32), ((count, units), f32), ((1, LANES), f32), ((1, LANES), jnp.int32)
    ]
    outs = call(
        "unpack_small", kernel, 1, [hot(term) for term in terms],
        [(shape, dtype, spec(shape)) for shape, dtype in shapes],
    )
    return outs[:6], outs[6], outs[7], outs[8], outs[9]


def segment_info(seq_lengths, total):
    ends = jnp.cumsum(seq_lengths)
    places = jnp.arange(total, dtype=jnp.int32)
    labels = jnp.sum((places[:, None] >= ends[None, :-1]).astype(jnp.int32), axis=1)
    starts = ends - seq_lengths
    picks = labels[:, None] == jnp.arange(seq_lengths.shape[0], dtype=jnp.int32)[None, :]
    begin = jnp.sum(jnp.where(picks, starts[None, :], 0), axis=1)
    return (labels, places - begin)


def moves(dp_size, tensor_size):
    def flat(dp, tensor):
        return dp * tensor_size + tensor

    every = [(dp, tensor) for dp in range(dp_size) for tensor in range(tensor_size)]

    def by(target):
        return [(flat(*where), flat(*target(*where))) for where in every]

    return {
        "swap": by(lambda dp, tensor: (dp - dp % 2 + tensor, dp % 2)),
        "y": by(lambda dp, tensor: (dp, 1 - tensor)),
        "z": by(lambda dp, tensor: (dp ^ 12 if dp_size > 8 else dp, tensor)),
        "bits": [
            by(lambda dp, tensor, bit=bit: (dp ^ bit, tensor))
            for bit in (1 << place for place in range(dp_size.bit_length() - 1))
        ],
    }


def per_device(
    x_in,
    lengths,
    token_ids,
    ln1_gain,
    ln1_bias,
    w_qkv,
    b_qkv,
    w_out,
    b_out,
    ln2_gain,
    ln2_bias,
    w_up,
    b_up,
    w_down,
    b_down,
    head,
    class_bins,
    cotangent,
):
    rows, width = x_in.shape
    dp_size = lax.axis_size("dp")
    tensor_size = lax.axis_size("tensor")
    depth = w_qkv.shape[0]
    part = w_qkv.shape[3]
    units = w_up.shape[2]
    total = rows * tensor_size
    dp = lax.axis_index("dp")
    core = dp % 2
    bits = dp_size.bit_length() - 1
    move = moves(dp_size, tensor_size)

    def send(array, name):
        return lax.ppermute(array, AXES, move["bits"][name] if isinstance(name, int) else move[name])

    numbers = send(jnp.concatenate([lengths[0], token_ids]), "swap")
    seq_lengths, ids = numbers[: lengths.shape[1]], numbers[lengths.shape[1] :]
    small_biases = jnp.concatenate([b_qkv.reshape(depth, -1), b_up], axis=1)
    far_biases = send(small_biases, "y")
    w_qkv = jnp.transpose(w_qkv, (0, 2, 1, 3))
    b_qkv = jnp.transpose(b_qkv, (1, 0, 2))
    far_b_qkv = jnp.transpose(far_biases[:, : 3 * part].reshape(depth, 3, part), (1, 0, 2))
    far_b_up = far_biases[:, 3 * part :]

    z_bit = min(2, bits - 1)

    def slots_of(bit):
        own = ((dp >> bit) % 2) * 2 + core
        return jnp.stack([own, own ^ 2, own ^ 1, own ^ 3]).astype(jnp.int32)

    all_slots = (slots_of(1), slots_of(z_bit))

    class Bundle:
        def __init__(self, way, packed):
            self.way, self.packed = way, packed

        def begin(self, *tokens):
            packed = gate(self.packed, tokens) if tokens else self.packed
            self.got = send(packed, "y")
            return packed

        def hop(self, *tokens):
            if tokens:
                self.got = gate(self.got, tokens)
            self.beside = send(self.got, (1, z_bit)[self.way])
            self.across = send(self.got, 0)
            return self.got

        def end(self, *tokens):
            beside = gate(self.beside, tokens) if tokens else self.beside
            pieces = [self.got, beside, self.across, send(beside, 0)]
            self.far = (all_slots[self.way], pieces)
            return beside

    chunk_rows = width // PIECES
    (packed,) = pack_call(0, all_slots, [(0, ((w_qkv, (1, 2)),))])
    key_bundle = Bundle(0, packed)
    key_bundle.begin()
    key_bundle.hop()
    x_low = gate(x_in.astype(bf16), (packed,))
    stream = send(x_low, "swap")
    heads, ups, downs = [], [], []
    for number in range(depth):
        members = (0, 1, 2) if number else (0,)
        arrays = pack_call(
            number, all_slots,
            [(1, ((w_qkv, members), w_out)), (0, (w_up,)), (1, (w_down,))], (packed, x_low),
        )
        for store, way, array in zip((heads, ups, downs), (1, 0, 1), arrays):
            store.append(Bundle(way, array))
    heads[0].begin(key_bundle.got)
    ups[0].begin(heads[0].got)

    def far_heads(number):
        if number:
            return [(*heads[number].far, member) for member in range(3)]
        return [(*heads[0].far, 0), (*key_bundle.far, 0), (*key_bundle.far, 1)]

    def far_out(number):
        return (*heads[number].far, (3 if number else 1) * chunk_rows)

    cotangent_low = cotangent.astype(bf16)

    labels, places = segment_info(seq_lengths, total)
    labels_here = lax.dynamic_slice_in_dim(labels, core * rows, rows, 0)
    labels_far = lax.dynamic_slice_in_dim(labels, (1 - core) * rows, rows, 0)
    places_here = lax.dynamic_slice_in_dim(places, core * rows, rows, 0)
    lane = jnp.arange(LANES, dtype=jnp.int32)[None, :]
    freqs = theta ** (-(lane % HALF).astype(f32) / HALF)
    angles = places_here.astype(f32)[:, None] * freqs
    sine = jnp.sin(angles)
    tables = (jnp.cos(angles), jnp.where(lane % HEAD_DIM < HALF, -sine, sine))
    place = lane % HEAD_DIM
    q_mark = jnp.where(labels_here[:, None] == place, far, 0.0).astype(bf16)

    def key_mark(own):
        other = (own[:, None] != place) & (place < 3)
        return jnp.where(other, 1.0, jnp.where((place >= 3) & (place < 6), -1.0, 0.0)).astype(bf16)

    marks = (q_mark, key_mark(labels_here), key_mark(labels_far))
    chunk = width // dp_size
    order = jnp.arange(width, dtype=jnp.int32)
    block, inside = order // chunk, order % chunk
    home = sum(
        (((block >> (bits - 1 - place)) & 1) << place) for place in range(bits)
    )
    order = (home ^ dp) * chunk + inside
    turn = (order[:, None] == jnp.arange(width, dtype=jnp.int32)[None, :]).astype(bf16)

    def turned(array):
        return lax.dot_general(turn, array, (((1,), (1,)), ((), ())), preferred_element_type=bf16)

    saved = []
    wait = ()
    for number in range(depth):
        more = number + 1 < depth
        normed_attn, n_t_attn, q, kv = qkv_call(
            number, (0, 1, 2), stream, (ln1_gain, ln1_bias, turn), w_qkv, b_qkv, tables,
            after=wait,
        )
        if number == 0:
            key_bundle.end()
            wait = (heads[0].hop(kv), ups[0].hop(kv), downs[0].begin(ups[0].got, kv))
        else:
            wait = ()
        key_far = (*key_bundle.far, 0) if number == 0 else far_heads(number)[1]
        (kv,) = qkv_call(
            number, (1, 2), normed_attn, None, key_far, far_b_qkv, tables, (kv,), wait
        )
        kv_far = send(kv, 0)
        if number == 0:
            heads[0].end(kv)
        (q,) = qkv_call(
            number, (0,), normed_attn, None, far_heads(number)[0], far_b_qkv, tables, (q,), (kv,)
        )
        wait = (downs[number].hop(q),) if number else ()
        if not more:
            low = gate(cotangent_low, (downs[number].got, q))
            grad_stream = send(low, "swap")
            wait += (low,)
        att, logsum = attention_call(q, kv, kv_far, marks, wait)
        if number == 0:
            wait = (ups[0].end(att), downs[0].hop(att))
        else:
            wait = (ups[number].end(att), downs[number].end(att))
        if more:
            wait += (heads[number + 1].begin(downs[number].got, att),)
        middle, normed_ffn, n_t_ffn, active, slope, acc = ffn_call(
            number, stream, att, w_out, far_out(number), (b_out, ln2_gain, ln2_bias, b_down),
            turn, w_up, b_up, w_down, wait,
        )
        wait = (downs[0].end(acc),) if number == 0 else ()
        if more:
            wait += (heads[number + 1].hop(acc), ups[number + 1].begin(heads[number + 1].got, acc))
        up_far, down_far = ups[number].far, downs[number].far
        active_o, slope_o, below, low = ffn_far_call(
            number, normed_ffn, acc, up_far, down_far, far_b_up, wait
        )
        if more:
            wait = (
                heads[number + 1].end(low),
                ups[number + 1].hop(low),
                downs[number + 1].begin(ups[number + 1].got, low),
            )
        saved.append(
            (stream, n_t_attn, (q, kv, kv_far), logsum, att, middle, n_t_ffn,
             (active, slope), (active_o, slope_o))
        )
        stream = below
    out_low = send(low, "swap")
    half = width // 2
    quarter, eighth = half // 2, half // 4

    def pairs(*steps):
        return tuple(array for keep, sent, way in steps for array in (keep, send(sent, way)))

    def join_attention(*arrays):
        shapes = ((2, half, part),) * 2 + ((2, 2, quarter, part),) * 2
        return join_attention_kernel, arrays, shapes

    def join_line(*arrays):
        return join_line_kernel, arrays, ((8, 2, eighth, part),) * 2

    def inner(keep, sent, way):
        members, _, deep, cols = keep.shape
        return inner_kernel, pairs((keep, sent, way)), ((members, 2, deep // 2, cols),) * 2

    def final(keep, sent, way):
        return sum_kernel, pairs((keep, sent, way)), (keep.shape,)

    def cut(keep, sent, way):
        members, _, deep, cols = keep.shape
        return cut_kernel, pairs((keep, sent, way)), ((members, deep, cols),) * 2

    def turn_ways(joined):
        a_keep, a_send, b_keep, b_send = joined
        members, deep, cols = a_keep.shape
        shape_a, shape_b = (members, deep // 2, cols), b_keep.shape[1:]
        arrays = pairs((a_keep, a_send, "y"), (b_keep, b_send, 1))
        return turn_kernel, arrays, (shape_a, shape_a, shape_b, shape_b)

    def merge(*steps):
        members = sum(keep.shape[0] for keep, _, _ in steps)
        _, deep, cols = steps[0][0].shape
        return merge_kernel, pairs(*steps), ((members, deep // 2, cols),) * 2

    def merge_ways(turned):
        a_keep, a_send, b_keep, b_send = turned
        return merge((a_keep, a_send, 1), (b_keep, b_send, "y"))

    def part_sides(keep, sent, way):
        return (
            functools.partial(part_kernel, 0), pairs((keep, sent, way)),
            ((4,) + keep.shape[1:],) * 2,
        )

    def add_small(array, other, way):
        return add_kernel, (array, send(other, way)), (shaped(array.shape, f32),)

    def halves_small(both):
        def kernel(both, got, out):
            out[...] = both[0] + got[...]

        return kernel, (both, send(both[1], "y")), (shaped(both.shape[1:], f32),)

    def plain_sum(keep, got):
        total = plus(keep, got)
        total = plus(total[0], send(total[1], "y"))
        for bit in range(1, bits):
            rows_left = total.shape[-2] // 2
            total = plus(total[..., :rows_left, :], send(total[..., rows_left:, :], bit))
        return total.astype(f32)

    placed = bits == 4 and depth == 2
    pieces = [None] * depth
    plain = [None] * depth
    grad_low = grad_stream
    g_t = turned(grad_low)
    grad_b_down = column_sum(grad_stream.astype(f32))
    for number in reversed(range(depth)):
        stream, n_t_attn, keyed, logsum, att, middle, n_t_ffn, near, distant = saved[number]
        top, last = number == depth - 1, number == 0
        acc, ffn_k, ffn_s, d_b_up = ffn_back_call(
            number, grad_low, n_t_ffn, g_t, near, distant, w_up, w_down,
            ups[number].far, downs[number].far,
        )
        ffn_g = send(ffn_s, 0)
        sides = []
        if placed and not top:
            sides = [turn_ways(joined_ffn), join_line(qkv_k, qkv_g)]
        after = ()
        if last:
            bin_row = share_call(low, jnp.transpose(head), ids[None], class_bins[None], d_b_up)
            after = (bin_row,)
        grad_middle, grad_att, gm_t, smalls_two, *more = middle_back_call(
            number, acc, middle, ln2_gain, grad_stream, w_out, far_out(number), turn,
            sides=sides, after=after,
        )
        if more:
            turned_ffn, lined = more
        after = ()
        if placed and last:
            joined_low = join_ffn_call(ffn_k, ffn_g, (grad_att,))
            after = joined_low[1:2]
        gq, gkv, gkv_s = attention_back_call(
            *keyed, marks, logsum, att, grad_att, tables, after=after
        )
        gkv_g = send(gkv_s, 0)
        after = ()
        if placed and not last:
            joined_ffn = join_ffn_call(ffn_k, ffn_g, (gkv_s,))
            after = joined_ffn[1:2]
        elif placed:
            merged_ffn, lined, turned_low = sums_call(
                "merge_above", merge_ways(turned_ffn), inner(*lined, z_bit), turn_ways(joined_low),
                after=(gkv_s,),
            )
            after = merged_ffn[1:2]
        weights, ending = (w_qkv, far_heads(number)), (stream, ln1_gain, grad_middle, turn)
        if placed and last:
            qkv_k, qkv_s, d_b_qkv = qkv_back_call(
                number, gq, gkv, gkv_g, tables, (n_t_attn, gm_t, att), after=after
            )
            qkv_g = send(qkv_s, 0)
            grad_stream, grad_low, g_t, smalls_one = qkv_back_call(
                number, gq, gkv, gkv_g, tables, None, weights, ending, after=(d_b_qkv,)
            )
        else:
            qkv_k, qkv_s, d_b_qkv, grad_stream, grad_low, g_t, smalls_one = qkv_back_call(
                number, gq, gkv, gkv_g, tables, (n_t_attn, gm_t, att), weights, ending, after=after
            )
            qkv_g = send(qkv_s, 0)
        if not placed:
            plain[number] = (plain_sum(ffn_k, ffn_g), plain_sum(qkv_k, qkv_g))
        pieces[number] = (smalls_one, smalls_two, grad_b_down, d_b_qkv, d_b_up)
        grad_b_down = smalls_one
    grad_x_low = send(grad_low, "swap")
    both = pack_small(pieces, bin_row, width)
    if placed:
        joined_att, merged_low, ended_above, lined = sums_call(
            "tail_one", join_attention(qkv_k, qkv_g), merge_ways(turned_low),
            merge((*merged_ffn, z_bit)), cut(*lined, 3), after=(both,),
        )
        turned_att, ended_low, (both,) = sums_call(
            "tail_two", turn_ways(joined_att), merge((*merged_low, z_bit)),
            add_small(both, both, 0),
        )
        merged_att, (near_1, far_1), (sums,), (ffn_1,) = sums_call(
            "tail_three", merge_ways(turned_att), part_sides(*lined, 1), halves_small(both),
            final(*ended_above, 3),
        )
        ended_att, (ffn_0,), (sums,), (att_1,) = sums_call(
            "tail_four", merge((*merged_att, z_bit)), final(*ended_low, 3),
            add_small(sums, sums, 1), final(near_1, far_1, "y"),
        )
        out_act, grad_x = widen_call((out_low, grad_x_low), ended_att[1:2])
        terms = (sums, send(sums, 2), send(sums, 3), send(sums, "z"))
        ended_ffn = [(0, (ffn_0,)), (0, (ffn_1,))]
        ended_attention = [(0, pairs((*ended_att, 3))), (0, (att_1,))]
        grad_w_up, grad_w_down, grad_w_qkv, grad_w_out = emit_call(ended_ffn, ended_attention)
    else:
        grad_w_up, grad_w_down = (
            jnp.stack([
                jnp.concatenate([ffn[which, place] for place in range(PIECES)], axis=-1)
                for ffn, _ in plain
            ])
            for which in range(2)
        )
        grad_w_qkv = jnp.stack([entry[1][:3] for entry in plain])
        grad_w_out = jnp.stack([entry[1][3] for entry in plain])
        out_act, grad_x = widen_call((out_low, grad_x_low))
        sums = both[0] + send(both[1], "y")
        for bit in range(bits - 1):
            sums = sums + send(sums, bit)
        terms = (sums, send(sums, bits - 1))
    replicated, sharded_qkv, sharded_up, bin_density, count = unpack_small(
        terms, depth, part, units
    )

    return (
        out_act,
        grad_x,
        replicated[0],
        replicated[1],
        jnp.transpose(grad_w_qkv, (0, 2, 1, 3)),
        jnp.transpose(sharded_qkv, (1, 0, 2)),
        jnp.transpose(grad_w_out, (0, 2, 1)),
        replicated[4],
        replicated[2],
        replicated[3],
        grad_w_up,
        sharded_up,
        jnp.transpose(grad_w_down, (0, 2, 1)),
        replicated[5],
        bin_density[0, :BINS],
        count[0, 0],
    )


def solution(mesh):
    placed = (
        P(("dp", "tensor"), None),
        P("dp", None),
        P(("dp", "tensor")),
        P(),
        P(),
        P(None, None, None, "tensor"),
        P(None, None, "tensor"),
        P(None, "tensor", None),
        P(),
        P(),
        P(),
        P(None, None, "tensor"),
        P(None, "tensor"),
        P(None, "tensor", None),
        P(),
        P(),
        P(),
        P(("dp", "tensor"), None),
    )
    return jax.shard_map(
        per_device,
        mesh=mesh,
        in_specs=placed,
        out_specs=(
            P(("dp", "tensor"), None),
            P(("dp", "tensor"), None),
            P(),
            P(),
            P(None, "dp", None, "tensor"),
            P(None, None, "tensor"),
            P(None, "tensor", "dp"),
            P(),
            P(),
            P(),
            P(None, "dp", "tensor"),
            P(None, "tensor"),
            P(None, "tensor", "dp"),
            P(),
            P(),
            P(),
        ),
        check_vma=False,
    )
```

```python
import functools

import jax
import jax.numpy as jnp
from jax import lax
from jax.experimental import pallas as pl
from jax.experimental.pallas import tpu as pltpu
from jax.sharding import PartitionSpec as P

HEAD_DIM = 64
HALF = HEAD_DIM // 2
BINS = 24
LANES = 128
PIECES = 4
VMEM_MIB = {
    "join_ffn": 20, "merge_above": 24, "tail_one": 24, "tail_two": 24, "tail_three": 24, "middle_back": 36
}
COSTS = {}

eps = 1e-05
theta = 10000.0
special_ids = 5
far = -1e30

bf16 = jnp.bfloat16
f32 = jnp.float32
AXES = ("dp", "tensor")


def dot(a, b):
    return jnp.dot(a, b, preferred_element_type=f32)


def dot_nt(a, b):
    return lax.dot_general(a, b, (((1,), (1,)), ((), ())), preferred_element_type=f32)


def normalize(rows):
    centre = rows - jnp.mean(rows, axis=-1, keepdims=True)
    spread = jnp.mean(centre * centre, axis=-1, keepdims=True)
    scale = lax.rsqrt(spread + eps)
    return centre * scale, scale


def norm_backward(rows, gain, grad):
    unit, scale = normalize(rows)
    gained = grad * gain
    mean_grad = jnp.mean(gained, axis=-1, keepdims=True)
    mean_both = jnp.mean(gained * unit, axis=-1, keepdims=True)
    below = scale * (gained - mean_grad - unit * mean_both)
    return below, column_sum(grad * unit), column_sum(grad)


def column_sum(rows):
    return jnp.sum(rows, axis=0, keepdims=True)


def rotate(rows, cosine, sine, sign):
    lane = lax.broadcasted_iota(jnp.int32, cosine.shape, 1)
    low = lane % HEAD_DIM < HALF
    pieces = []
    for start in range(0, rows.shape[1], LANES):
        piece = rows[:, start : start + LANES]
        other = jnp.where(low, pltpu.roll(piece, LANES - HALF, 1), pltpu.roll(piece, HALF, 1))
        pieces.append(piece * cosine + sign * (other * sine))
    return jnp.concatenate(pieces, axis=1)


def gelu_pair(value):
    size = jnp.abs(value) * (2.0**-0.5)
    t = 1.0 / (1.0 + 0.3275911 * size)
    bell = jnp.exp(-0.5 * value * value)
    poly = t * (
        0.5 * 0.254829592
        + t
        * (
            0.5 * -0.284496736
            + t * (0.5 * 1.421413741 + t * (0.5 * -1.453152027 + t * (0.5 * 1.061405429)))
        )
    )
    tail = poly * bell
    share = jnp.where(value < 0, tail, 1.0 - tail)
    return value * share, share + value * bell * 0.3989422804014327


def three_parts(column):
    high = column.astype(bf16).astype(f32)
    rest = column - high
    middle = rest.astype(bf16).astype(f32)
    return high, middle, rest - middle


def spec(shape, index=None):
    zeros = (0,) * len(shape)
    return pl.BlockSpec(shape, index or (lambda i, *s: zeros))


def whole(array):
    return array, spec(array.shape)


def hot(array):
    return array, spec(array.shape), True


def cold(array):
    return pltpu.with_memory_space_constraint(array, pltpu.HBM)


def shaped(shape, dtype):
    return jax.ShapeDtypeStruct(shape, dtype)


def call(
    name, kernel, steps, operands, results, prefetch=(), scratch=(), alias=(), after=(), sides=(),
    token=False,
):
    def side_spec(shape):
        lead = (0,) * (len(shape) - 1)
        return spec(
            tuple(shape[:-1]) + (shape[-1] // 3,), lambda i, *s: (*lead, jnp.minimum(i, 2))
        )

    own_in, own_out = len(operands), len(results) + token
    idle = [array for array, _ in alias] + list(after)
    if token:
        results = [((8, LANES), f32, spec((8, LANES))), *results]
    arrays = [entry[0] if len(entry) > 2 else cold(entry[0]) for entry in operands]
    in_specs = [entry[1] for entry in operands]
    out_specs = [entry[2] for entry in results]
    out_shape = [
        (shaped if len(entry) > 3 else pltpu.HBM)(entry[0], entry[1]) for entry in results
    ]
    for _, side_args, side_shapes in sides:
        in_specs += [side_spec(arg.shape) for arg in side_args]
        out_specs += [side_spec(getattr(shape, "shape", shape)) for shape in side_shapes]
        out_shape += [
            shape
            if hasattr(shape, "dtype")
            else (shaped if name.startswith("tail") else pltpu.HBM)(shape, bf16)
            for shape in side_shapes
        ]
        arrays += side_args
    ahead, count_in, count_out = len(prefetch), len(in_specs), len(out_specs)

    def body(*refs):
        early, refs = refs[:ahead], refs[ahead + len(idle) :]
        ins, outs, rest = (
            refs[:count_in], refs[count_in : count_in + count_out], refs[count_in + count_out :]
        )
        if token:
            outs[0][...] = jnp.zeros((8, LANES), f32)
        if kernel is not None:
            kernel(*early, *ins[:own_in], *outs[token:own_out], *rest)

        def run_sides():
            at_in, at_out = own_in, own_out
            for side_kernel, side_args, side_shapes in sides:
                side_kernel(
                    *ins[at_in : at_in + len(side_args)], *outs[at_out : at_out + len(side_shapes)]
                )
                at_in, at_out = at_in + len(side_args), at_out + len(side_shapes)

        if sides and steps > 3:
            pl.when(pl.program_id(0) < 3)(run_sides)
        else:
            run_sides()

    made = pl.pallas_call(
        body,
        grid_spec=pltpu.PrefetchScalarGridSpec(
            num_scalar_prefetch=ahead,
            grid=(steps,),
            in_specs=[pl.BlockSpec(memory_space=pl.ANY)] * len(idle) + in_specs,
            out_specs=out_specs,
            scratch_shapes=list(scratch),
        ),
        out_shape=out_shape,
        name=name,
        input_output_aliases={
            ahead + place: result for place, (_, result) in enumerate(alias)
        },
        compiler_params=pltpu.CompilerParams(vmem_limit_bytes=VMEM_MIB.get(name, 44) << 20),
        cost_estimate=pl.CostEstimate(
            flops=int(COSTS.get(name, 6e10)), bytes_accessed=int(4e6), transcendentals=0
        ),
    )
    outs = made(*prefetch, *idle, *arrays)
    done, at = list(outs[:own_out]), own_out
    for _, _, side_shapes in sides:
        done.append(outs[at : at + len(side_shapes)])
        at += len(side_shapes)
    return done


def gate(array, after):
    return lax.optimization_barrier((array, *after))[0]


def gather_rows(target, slots, pieces, lane=0):
    count, lanes = pieces[0].shape
    for place, piece in enumerate(pieces):
        start = pl.multiple_of(slots[place] * count, 16)
        target[pl.ds(start, count), lane : lane + lanes] = piece[...]


def qkv_kernel(number, base, members, first, distant, *refs):
    refs = list(refs)
    slots = refs.pop(0) if distant else None
    if first:
        x, gain, bias, turn = refs[:4]
        refs = refs[4:]
    else:
        normed = refs.pop(0)
    pieces, refs = (refs[:PIECES], refs[PIECES:]) if distant else (refs[:1], refs[1:])
    b, cosine, sine, *refs = refs
    if first:
        normed, n_t, *refs = refs
    queries = refs.pop(0) if 0 in members else None
    kv = refs.pop(0) if 1 in members else None
    step = pl.program_id(0)
    if first:

        @pl.when(step == 0)
        def _():
            unit, _ = normalize(x[...].astype(f32))
            normed[...] = (
                unit * gain[number : number + 1] + bias[number : number + 1]
            ).astype(bf16)
            n_t[...] = dot_nt(turn[...], normed[...]).astype(bf16)

    if distant:
        (matrix,) = refs
        gather_rows(matrix, slots, pieces)
        weight = matrix[...]
    else:
        weight = pieces[0][0, 0]
    row = slice(number, number + 1)
    mixed = dot(normed[...], weight) + (b[row] if len(b.shape) == 2 else b[0, row])
    for member in members:

        @pl.when(step == member - base)
        def _(member=member):
            if member == 0:
                turned = rotate(mixed, cosine[...], sine[...], 1.0)
                queries[...] = (turned * HEAD_DIM**-0.5).astype(bf16)
            elif member == 1:
                kv[0] = rotate(mixed, cosine[...], sine[...], 1.0).astype(bf16)
            else:
                kv[0] = mixed.astype(bf16)


def qkv_call(number, members, rows_in, norm, weight, b, tables, prior=(), after=()):
    first, distant = norm is not None, isinstance(weight, tuple)
    rows, width = rows_in.shape
    part = width // 2
    base = members[0]
    operands = [whole(rows_in) if first and number else hot(rows_in)]
    if first:
        operands += [whole(array) for array in norm[:2]] + [hot(norm[2])]
    prefetch, scratch = (), ()
    if distant:
        slots, pieces, lead = weight
        prefetch = (slots,)
        operands += [
            (piece, spec((width // PIECES, part), lambda i, *s: (i + lead, 0)), True)
            for piece in pieces
        ]
        scratch = (pltpu.VMEM((width, part), bf16),)
    else:
        block = spec((1, 1, width, part), lambda i, *s: (number, i + base, 0, 0))
        operands.append((weight, block))
    if distant:
        skip = (b.shape[1] - 3 * part) // part + base
        operands.append((b, spec((b.shape[0], part), lambda i, *s: (0, i + skip))))
    else:
        operands.append((b, spec((1, b.shape[1], part), lambda i, *s: (i + base, 0, 0))))
    operands += [hot(table) for table in tables]
    half = 1 if distant else 0
    results = []
    if first:
        results += [
            ((rows, width), bf16, spec((rows, width)), True),
            ((width, rows), bf16, spec((width, rows))),
        ]
    alias = []
    if 0 in members:
        if prior:
            alias.append((prior[0], len(results)))
        results.append(
            ((rows, 2 * part), bf16, spec((rows, part), lambda i, *s: (0, half)), True)
        )
    if 1 in members:
        if prior:
            alias.append((prior[-1], len(results)))
        block = spec(
            (1, rows, part), lambda i, *s: (jnp.maximum(i + base - 1, 0), 0, half)
        )
        results.append(((2, rows, 2 * part), bf16, block, True))
    return call(
        "qkv",
        functools.partial(qkv_kernel, number, base, members, first, distant),
        len(members),
        operands,
        results,
        prefetch,
        scratch,
        alias,
        after,
    )


def head_lanes(shape, head):
    lane = lax.broadcasted_iota(jnp.int32, shape, 1)
    return (lane < HEAD_DIM) if head == 0 else (lane >= HEAD_DIM)


def attention_kernel(q, kv, kv_far, q_mark, k_mark, k_mark_far, out, logsum):
    rows = q.shape[0]
    queries = q[...]
    scores, values = [], []
    for head in range(2):
        mine = head_lanes((rows, LANES), head)
        marked = jnp.where(mine, queries, q_mark[...])
        for pair, mark in ((kv, k_mark), (kv_far, k_mark_far)):
            scores.append(dot_nt(marked, jnp.where(mine, pair[0], mark[...])))
            values.append(jnp.where(mine, pair[1], jnp.ones_like(pair[1])))
    highest, expos = [], []
    for head in range(2):
        near, distant = scores[2 * head : 2 * head + 2]
        highest.append(
            jnp.maximum(
                jnp.max(near, axis=-1, keepdims=True), jnp.max(distant, axis=-1, keepdims=True)
            )
        )
        expos += [jnp.exp(score - highest[head]).astype(bf16) for score in (near, distant)]
    results, logs = [], []
    for head in range(2):
        total = dot(expos[2 * head], values[2 * head])
        total = total + dot(expos[2 * head + 1], values[2 * head + 1])
        column = HEAD_DIM if head == 0 else 0
        summed = total[:, column : column + 1]
        results.append(total / summed)
        logs.append(highest[head] + jnp.log(summed))
    out[...] = jnp.where(head_lanes((rows, LANES), 0), results[0], results[1]).astype(bf16)
    logsum[...] = jnp.where(head_lanes((rows, LANES), 0), logs[1], logs[0])


def head_specs(rows):
    column = spec((rows, LANES), lambda i, *s: (0, i))
    both = spec((2, rows, LANES), lambda i, *s: (0, 0, i))
    return column, both


def attention_call(q, kv, kv_far, marks, after=(), sides=()):
    rows, width = q.shape
    column, both = head_specs(rows)
    return call(
        "attention",
        attention_kernel,
        width // LANES,
        [(q, column, True), (kv, both, True), (kv_far, both, True)] + [hot(mark) for mark in marks],
        [((rows, width), bf16, column), ((rows, width), f32, column)],
        after=after,
        sides=sides,
    )


def attention_back_kernel(
    q, kv, kv_far, q_mark, k_mark, k_mark_far, logsum, attended, grad, cosine, sine,
    grad_q, grad_kv, grad_kv_far,
):
    rows = q.shape[0]
    queries = q[...]
    grads = grad[...]
    lane = lax.broadcasted_iota(jnp.int32, (rows, LANES), 1) % HEAD_DIM
    logs = three_parts(logsum[...])
    log_mark = sum(
        jnp.where(lane == 3 + place, part, 0.0) for place, part in enumerate(logs)
    ).astype(bf16)
    product = attended[...].astype(f32) * grads.astype(f32)
    value_mark = jnp.where(lane < 3, -1.0, 0.0).astype(bf16)
    dots_t = []
    keys_t = [
        jnp.transpose(pair[0].astype(f32)).astype(bf16) for pair in (kv, kv_far)
    ]
    outs = ([], [])
    for head in range(2):
        mine = head_lanes((rows, LANES), head)
        centre = jnp.sum(jnp.where(mine, product, 0.0), axis=-1, keepdims=True)
        centre_mark = sum(
            jnp.where(lane == place, part, 0.0) for place, part in enumerate(three_parts(centre))
        ).astype(bf16)
        marked = jnp.where(mine, queries, q_mark[...] + log_mark)
        marked_grads = jnp.where(mine, grads, centre_mark)
        turned = 0.0
        for place, (pair, mark) in enumerate(((kv, k_mark), (kv_far, k_mark_far))):
            keys = jnp.where(mine, pair[0], mark[...])
            values = jnp.where(mine, pair[1], value_mark)
            probs = jnp.exp(dot_nt(keys, marked))
            grad_scores = (probs * dot_nt(values, marked_grads)).astype(bf16)
            grad_values = dot(probs.astype(bf16), grads)
            grad_keys = dot(grad_scores, queries)
            turned = turned + dot(
                keys_t[place][head * HEAD_DIM : (head + 1) * HEAD_DIM], grad_scores
            )
            outs[place].append((grad_keys, grad_values))
        dots_t.append(turned)
    grad_queries = jnp.transpose(jnp.concatenate(dots_t, axis=0)) * HEAD_DIM**-0.5
    grad_q[...] = rotate(grad_queries, cosine[...], sine[...], -1.0).astype(bf16)
    mine = head_lanes((rows, LANES), 0)
    for ref, (one, two) in zip((grad_kv, grad_kv_far), outs):
        for member in range(2):
            ref[member] = jnp.where(mine, one[member], two[member]).astype(ref.dtype)


def attention_back_call(q, kv, kv_far, marks, logsum, attended, grad, tables, after=(), sides=()):
    rows, width = q.shape
    column, both = head_specs(rows)
    return call(
        "attention_back",
        attention_back_kernel,
        width // LANES,
        [(q, column), (kv, both), (kv_far, both)]
        + [hot(mark) for mark in marks]
        + [(logsum, column), (attended, column), (grad, column, True)]
        + [hot(table) for table in tables],
        [
            ((rows, width), bf16, column, True),
            ((2, rows, width), bf16, both, True),
            ((2, rows, width), bf16, both, True),
        ],
        after=after,
        sides=sides,
    )


def out_operands(pieces, part, row):
    low = part // PIECES
    return [
        (piece, spec((low, part), lambda i, *s, side=side: (row // low + side, 0)), True)
        for side in range(2)
        for piece in pieces
    ]


def gather_out(target, slots, pieces):
    part = target.shape[0]
    for side in range(2):
        gather_rows(target, slots, pieces[side * PIECES :][:PIECES], side * part)


def ffn_kernel(number, slots, *refs):
    x, att, wo_n = refs[:3]
    wo_pieces, refs = refs[3 : 3 + 2 * PIECES], refs[3 + 2 * PIECES :]
    (b_out, gain, bias, b_down, turn, w_up, b_up, w_down,
     middle, normed, n_t, active, slope, acc, wo_o) = refs
    row = slice(number, number + 1)

    @pl.when(pl.program_id(0) == 0)
    def _():
        part = wo_o.shape[0]
        gather_out(wo_o, slots, wo_pieces)
        mid = (
            x[...].astype(f32)
            + dot(att[:, :part], wo_n[0])
            + dot(att[:, part:], wo_o[...])
            + b_out[row]
        )
        middle[...] = mid
        unit, _ = normalize(mid)
        normed[...] = (unit * gain[row] + bias[row]).astype(bf16)
        n_t[...] = dot_nt(turn[...], normed[...]).astype(bf16)
        acc[...] = mid + b_down[row]

    hidden = dot(normed[...], w_up[0]) + b_up[row]
    value, back = gelu_pair(hidden)
    value = value.astype(bf16)
    active[...] = value
    slope[...] = back.astype(bf16)
    acc[...] += dot(value, w_down[0])


def ffn_call(number, x, att, w_out, heads_far, small, turn, w_up, b_up, w_down, after=()):
    rows, width = x.shape
    units, part = w_up.shape[2], w_out.shape[1]
    slots, pieces, row = heads_far
    b_out, gain, bias, b_down = small
    block = 2 * units // PIECES
    near = (True,) if number else ()
    wide = spec((rows, block), lambda i, *s: (0, i))
    full = spec((rows, width))
    return call(
        "ffn",
        functools.partial(ffn_kernel, number),
        units // block,
        [
            whole(x),
            whole(att),
            (w_out, spec((1, part, width), lambda i, *s: (number, 0, 0))),
            *out_operands(pieces, part, row),
            *[whole(array) for array in (b_out, gain, bias, b_down)],
            hot(turn),
            (w_up, spec((1, width, block), lambda i, *s: (number, 0, i))),
            (b_up, spec((b_up.shape[0], block), lambda i, *s: (0, i))),
            (w_down, spec((1, block, width), lambda i, *s: (number, i, 0))),
        ],
        [
            ((rows, width), f32, full),
            ((rows, width), bf16, full) + near,
            ((width, rows), bf16, spec((width, rows))),
            ((rows, units), bf16, wide),
            ((rows, units), bf16, wide),
            ((rows, width), f32, full) + near,
        ],
        prefetch=(slots,),
        scratch=(pltpu.VMEM((part, width), bf16),),
        after=after,
    )


def far_ffn_operands(up_far, down_far, width, units):
    slots_u, ups = up_far
    slots_d, downs = down_far
    block = 2 * units // PIECES

    def at(i, slots):
        return slots[jnp.clip(i, 0, 1)] // 2

    ups = [
        (piece, spec((width // PIECES, block), lambda i, *s: (0, at(i, s[0]))), True)
        for piece in ups
    ]
    downs = [(piece, spec((units // PIECES, width)), True) for piece in downs]
    return ups, downs, at, (slots_d, slots_u)


def gather_down(target, step, slots, downs):
    for place in range(2):

        @pl.when(step == place)
        def _(place=place):
            for which in (place, place + 2):
                count = downs[which].shape[0]
                start = pl.multiple_of((slots[which] % 2) * count, 16)
                target[pl.ds(start, count), :] = downs[which][...]


def ffn_far_kernel(number, slots_d, slots_u, normed, acc_in, b_up, *refs):
    ups, downs = refs[:PIECES], refs[PIECES : 2 * PIECES]
    active, slope, acc, low, w_up, w_down = refs[2 * PIECES :]
    step = pl.program_id(0)

    @pl.when(step == 0)
    def _():
        acc[...] = acc_in[...]

    gather_rows(w_up, slots_u, ups)
    gather_down(w_down, step, slots_d, downs)
    hidden = dot(normed[...], w_up[...]) + b_up[number : number + 1]
    value, back = gelu_pair(hidden)
    value = value.astype(bf16)
    active[...] = value
    slope[...] = back.astype(bf16)
    acc[...] += dot(value, w_down[...])

    @pl.when(step == pl.num_programs(0) - 1)
    def _():
        low[...] = acc[...].astype(bf16)


def ffn_far_call(number, normed, acc, up_far, down_far, b_up, units, after=()):
    rows, width = normed.shape
    block = 2 * units // PIECES
    ups, downs, at, prefetch = far_ffn_operands(up_far, down_far, width, units)
    wide = spec((rows, block), lambda i, *s: (0, at(i, s[0])))
    full = spec((rows, width))
    return call(
        "ffn_far",
        functools.partial(ffn_far_kernel, number),
        2,
        [
            hot(normed) if number else whole(normed),
            hot(acc) if number else whole(acc),
            (b_up, spec((b_up.shape[0], block), lambda i, *s: (0, at(i, s[0])))),
            *ups,
            *downs,
        ],
        [
            ((rows, units), bf16, wide),
            ((rows, units), bf16, wide),
            ((rows, width), f32, full),
            ((rows, width), bf16, full),
        ],
        prefetch=prefetch,
        scratch=(pltpu.VMEM((width, block), bf16), pltpu.VMEM((block, width), bf16)),
        after=after,
    )


def split_rows(product, keep, send, at):
    half = product.shape[0] // 2
    product = product.astype(bf16)
    keep[at] = product[:half]
    send[at] = product[half:]


def ffn_back_kernel(slots_d, slots_u, *refs):
    (g, n_t, g_t, active_n, slope_n, up_n, down_n, active_o, slope_o) = refs[:9]
    ups, downs = refs[9 : 9 + PIECES], refs[9 + PIECES : 9 + 2 * PIECES]
    acc, keep, send, b_up, up_o, down_o = refs[9 + 2 * PIECES :]
    step = pl.program_id(0)

    @pl.when(step == 0)
    def _():
        acc[...] = jnp.zeros_like(acc)

    def one(active, slope, w_up, w_down):
        grad_active = dot_nt(g[...], w_down)
        grad_hidden = (grad_active * slope[...].astype(f32)).astype(bf16)
        b_up[0] = column_sum(grad_hidden.astype(f32))
        acc[...] += dot_nt(grad_hidden, w_up)
        for which, product in enumerate(
            (dot(n_t[...], grad_hidden), dot(g_t[...], active[...]))
        ):
            block = product.shape[1] // 2
            for place in range(2):
                split_rows(
                    product[:, place * block : (place + 1) * block], keep, send, (0, which, place)
                )

    @pl.when(step < 2)
    def _():
        gather_rows(up_o, slots_u, ups)
        gather_down(down_o, step, slots_d, downs)
        one(active_o, slope_o, up_o[...], down_o[...])

    @pl.when(step >= 2)
    def _():
        one(active_n, slope_n, up_n[0], down_n[0])


def ffn_back_call(
    number, g, n_t, g_t, near, distant, w_up, w_down, up_far, down_far, after=(), sides=()
):
    rows, width = g.shape
    units = w_up.shape[2]
    block = 2 * units // PIECES
    ups, downs, at, prefetch = far_ffn_operands(up_far, down_far, width, units)

    def near_block(i):
        return jnp.maximum(i - 2, 0)

    def result_block(i, s):
        return jnp.where(i < 2, at(i, s[0]), near_block(i))

    def side(i):
        return jnp.where(i < 2, 1, 0)

    near_wide = spec((rows, block), lambda i, *s: (0, near_block(i)))
    far_wide = spec((rows, block), lambda i, *s: (0, at(i, s[0])))
    grads = spec(
        (1, 2, 2, width // 2, block // 2), lambda i, *s: (side(i), 0, result_block(i, s), 0, 0)
    )
    grads_shape = (2, 2, PIECES, width // 2, block // 2)
    return call(
        "ffn_back",
        ffn_back_kernel,
        4,
        [
            hot(g),
            whole(n_t),
            hot(g_t),
            *[(array, near_wide) for array in near],
            (w_up, spec((1, width, block), lambda i, *s: (number, 0, near_block(i)))),
            (w_down, spec((1, block, width), lambda i, *s: (number, near_block(i), 0))),
            *[(array, far_wide) for array in distant],
            *ups,
            *downs,
        ],
        [
            ((rows, width), f32, spec((rows, width)), True),
            (grads_shape, bf16, grads),
            (grads_shape, bf16, grads),
            ((2, 1, units), f32,
             spec((1, 1, block), lambda i, *s: (side(i), 0, result_block(i, s)))),
        ],
        prefetch=prefetch,
        scratch=(pltpu.VMEM((width, block), bf16), pltpu.VMEM((block, width), bf16)),
        after=after,
        sides=sides,
    )


def middle_back_kernel(number, slots, acc, middle, gain, g, wo_n, *refs):
    wo_pieces, refs = refs[: 2 * PIECES], refs[2 * PIECES :]
    turn, grad_middle, grad_att, low_t, smalls, wo_o, low = refs
    step = pl.program_id(0)
    part = wo_o.shape[0]

    @pl.when(step == 0)
    def _():
        below, d_gain, d_bias = norm_backward(middle[...], gain[number : number + 1], acc[...])
        total = below + g[...].astype(f32)
        grad_middle[...] = total
        low[...] = total.astype(bf16)
        smalls[0:1] = d_gain
        smalls[1:2] = d_bias
        smalls[2:3] = column_sum(total)

    @pl.when(step == 1)
    def _():
        gather_out(wo_o, slots, wo_pieces)
        grad_att[:, :part] = dot_nt(low[...], wo_n[0]).astype(bf16)
        grad_att[:, part:] = dot_nt(low[...], wo_o[...]).astype(bf16)

    @pl.when(step == 2)
    def _():
        low_t[...] = dot_nt(turn[...], low[...]).astype(bf16)


def middle_back_call(number, acc, middle, gain, g, w_out, heads_far, turn, after=(), sides=()):
    rows, width = acc.shape
    part = w_out.shape[1]
    slots, pieces, row = heads_far
    return call(
        "middle_back",
        functools.partial(middle_back_kernel, number),
        3,
        [
            hot(acc),
            *[whole(array) for array in (middle, gain, g)],
            (w_out, spec((1, part, width), lambda i, *s: (number, 0, 0))),
            *out_operands(pieces, part, row),
            hot(turn),
        ],
        [
            ((rows, width), f32, spec((rows, width))),
            ((rows, width), bf16, spec((rows, width)), True),
            ((width, rows), bf16, spec((width, rows)), True),
            ((3, width), f32, spec((3, width))),
        ],
        prefetch=(slots,),
        scratch=(pltpu.VMEM((part, width), bf16), pltpu.VMEM((rows, width), bf16)),
        after=after,
        sides=sides,
    )


def qkv_back_kernel(number, weight, rows_grad, *refs):
    refs = list(refs)
    slots = (refs.pop(0), refs.pop(0)) if rows_grad else None
    gq, kv, kv_far, cosine, sine = refs[:5]
    refs = refs[5:]
    if weight:
        n_t, gm_t, att, *refs = refs
    if rows_grad:
        w_n, *refs = refs
        pieces, refs = refs[: 3 * PIECES], refs[3 * PIECES :]
        x, gain, g, *refs = refs
        if number:
            turn, *refs = refs
    if weight:
        keep, send, b, *refs = refs
    if rows_grad:
        acc, low, *refs = refs
        if number:
            low_t, *refs = refs
        smalls, matrix, *refs = refs
    (mixed,) = refs
    step = pl.program_id(0)
    part = gq.shape[1]

    def lanes(member):
        return slice(member * part, (member + 1) * part)

    mixed[:, lanes(0)] = gq[...]
    keys = rotate(
        kv[0].astype(f32) + kv_far[0].astype(f32), cosine[...], sine[...], -1.0
    )
    mixed[:, lanes(1)] = keys.astype(bf16)
    mixed[:, lanes(2)] = plus(kv[1], kv_far[1])
    if weight:
        sums = column_sum(mixed[...].astype(f32))
        product = dot(n_t[...], mixed[...])
        for member in range(3):
            b[0, member] = sums[:, lanes(member)]
            split_rows(product[:, lanes(member)], keep, send, (0, member))
        split_rows(dot(gm_t[...], att[...]), keep, send, (0, 3))
    if rows_grad:

        @pl.when(step == 0)
        def _():
            for member in range(3):
                matrix[:, lanes(member)] = w_n[0, member]
            acc[...] = dot_nt(mixed[...], matrix[...])

        @pl.when(step == 1)
        def _():
            for member in range(3):
                gather_rows(
                    matrix, slots[min(member, 1)], pieces[member * PIECES :][:PIECES],
                    member * part,
                )
            whole_grad = acc[...] + dot_nt(mixed[...], matrix[...])
            below, d_gain, d_bias = norm_backward(
                x[...].astype(f32), gain[number : number + 1], whole_grad
            )
            total = below + g[...]
            acc[...] = total
            low[...] = total.astype(bf16)
            if number:
                low_t[...] = dot_nt(turn[...], low[...]).astype(bf16)
            smalls[0:1] = d_gain
            smalls[1:2] = d_bias
            smalls[2:3] = column_sum(total)


def qkv_back_call(
    number, gq, kv, kv_far, tables, sources=None, weights=None, ending=None, after=()
):
    rows = gq.shape[0]
    part = gq.shape[1] // 2
    width = 2 * part
    column = spec((rows, part), lambda i, *s: (0, i))
    both = spec((2, rows, part), lambda i, *s: (0, 0, i))
    operands = [(gq, column, True), (kv, both, True), (kv_far, both, True), *[hot(table) for table in tables]]
    results, prefetch, scratch = [], (), []
    if sources is not None:
        n_t, gm_t, att = sources
        operands += [whole(n_t), hot(gm_t), (att, column)]
        grads = spec((1, 4, width // 2, part), lambda i, *s: (i, 0, 0, 0))
        results += [((2, 4, width // 2, part), bf16, grads)] * 2
        results.append(
            ((2, 3, 1, part), f32, spec((1, 3, 1, part), lambda i, *s: (i, 0, 0, 0)))
        )
    if weights is not None:
        w_n, members = weights
        prefetch = (members[0][0], members[1][0])
        operands.append((w_n, spec((1, 3, width, part), lambda i, *s: (number, 0, 0, 0))))
        operands += [
            (piece, spec((width // PIECES, part), lambda i, *s, lead=lead: (lead, 0)), True)
            for _, pieces, lead in members
            for piece in pieces
        ]
        x, gain, g, turn = ending
        operands += [whole(x), whole(gain), whole(g)]
        results += [
            ((rows, width), f32, spec((rows, width))),
            ((rows, width), bf16, spec((rows, width)), True),
        ]
        if number:
            operands.append(hot(turn))
            results.append(((width, rows), bf16, spec((width, rows)), True))
        results.append(((3, width), f32, spec((3, width))))
        scratch.append(pltpu.VMEM((width, 3 * part), bf16))
    scratch.append(pltpu.VMEM((rows, 3 * part), bf16))
    return call(
        "qkv_back",
        functools.partial(qkv_back_kernel, number, sources is not None, weights is not None),
        2,
        operands,
        results,
        prefetch=prefetch,
        scratch=scratch,
        after=after,
    )


def pack_call(number, slots, groups, after=()):
    operands, results, entries = [], [], []
    for which, matrices in groups:
        rows, places = 0, []
        matrices = [entry if isinstance(entry, tuple) else (entry, (0,)) for entry in matrices]
        lanes = matrices[0][0].shape[-1]
        for matrix, members in matrices:
            chunk, sides = matrix.shape[-2] // PIECES, matrix.shape[-1] // lanes
            middle = matrix.shape[1:-2]
            zeros = (0,) * len(middle)
            operands.append((
                matrix,
                spec(
                    (1, *middle, chunk, matrix.shape[-1]),
                    lambda i, *s, which=which, zeros=zeros: (number, *zeros, s[which][0], 0),
                ),
            ))
            places.append((rows, members, chunk, sides))
            rows += len(members) * chunk * sides
        results.append(((rows, lanes), bf16, spec((rows, lanes))))
        entries.append((places, lanes))

    def kernel(*refs):
        refs = refs[len(slots) :]
        outs = refs[len(operands) :]
        at = 0
        for out, (places, lanes) in zip(outs, entries):
            for row, members, chunk, sides in places:
                source = refs[at]
                at += 1
                for place, member in enumerate(members):
                    for side in range(sides):
                        cut = slice(side * lanes, (side + 1) * lanes)
                        start = row + (place * sides + side) * chunk
                        if len(source.shape) == 4:
                            piece = source[0, member, :, cut]
                        else:
                            piece = source[0, :, cut]
                        out[start : start + chunk] = piece

    return call("pack", kernel, 1, operands, results, prefetch=slots, after=after)


def plus(a, b):
    return (a.astype(f32) + b.astype(f32)).astype(bf16)


def join_ffn_kernel(keep, got, a_keep, a_send, b_keep, b_send):
    half = b_keep.shape[2]
    for place in range(a_keep.shape[0]):
        a_keep[place] = plus(keep[0, 0, place], got[0, 0, place])
        a_send[place] = plus(keep[1, 0, place], got[1, 0, place])
        for side in range(2):
            b_keep[side, place] = plus(keep[side, 1, place, :half], got[side, 1, place, :half])
            b_send[side, place] = plus(keep[side, 1, place, half:], got[side, 1, place, half:])


def join_ffn_call(keep, got, after=()):
    deep, cols = keep.shape[3:]
    source = spec((2, 2, 1, deep, cols), lambda i, *s: (0, 0, i, 0, 0))
    one = ((PIECES, deep, cols), bf16, spec((1, deep, cols), lambda i, *s: (i, 0, 0)))
    two = (
        (2, PIECES, deep // 2, cols), bf16,
        spec((2, 1, deep // 2, cols), lambda i, *s: (0, i, 0, 0)),
    )
    return call(
        "join_ffn", join_ffn_kernel, PIECES, [(keep, source), (got, source, True)],
        [one, one, two, two], after=after, token=True,
    )


def join_attention_kernel(keep, got, a_keep, a_send, b_keep, b_send):
    half = b_keep.shape[2]
    for member in range(2):
        a_keep[member] = plus(keep[0, member], got[0, member])
        a_send[member] = plus(keep[1, member], got[1, member])
        for side in range(2):
            kept, came = keep.at[side, 2 + member], got.at[side, 2 + member]
            b_keep[side, member] = plus(kept[:half], came[:half])
            b_send[side, member] = plus(kept[half:], came[half:])


def join_line_kernel(keep, got, next_keep, next_send):
    half, quarter = keep.shape[2] // 2, next_keep.shape[2]
    for side in range(2):
        for member in range(4):
            for x in range(2):
                for start, ref in ((x * half, next_keep), (x * half + quarter, next_send)):
                    cut = slice(start, start + quarter)
                    ref[4 * side + member, x] = plus(
                        keep[side, member, cut], got[side, member, cut]
                    )


def cut_kernel(keep, got, next_keep, next_send):
    for member in range(keep.shape[0]):
        next_keep[member] = plus(keep[member, 0], got[member, 0])
        next_send[member] = plus(keep[member, 1], got[member, 1])


def inner_kernel(keep, got, next_keep, next_send):
    half = next_keep.shape[2]
    for member in range(keep.shape[0]):
        for x in range(2):
            next_keep[member, x] = plus(keep[member, x, :half], got[member, x, :half])
            next_send[member, x] = plus(keep[member, x, half:], got[member, x, half:])


def sum_kernel(keep, got, out):
    for member in range(keep.shape[0]):
        out[member] = plus(keep[member], got[member])


def turn_kernel(a_keep, a_got, b_keep, b_got, a_next, a_send, b_next, b_send):
    half = a_next.shape[1]
    for member in range(a_keep.shape[0]):
        a_next[member] = plus(a_keep[member, :half], a_got[member, :half])
        a_send[member] = plus(a_keep[member, half:], a_got[member, half:])
    for member in range(b_keep.shape[1]):
        b_next[member] = plus(b_keep[0, member], b_got[0, member])
        b_send[member] = plus(b_keep[1, member], b_got[1, member])


def merge_kernel(*refs):
    keep, send = refs[-2:]
    half = keep.shape[1]
    place = 0
    for kept, got in zip(refs[:-2:2], refs[1:-2:2]):
        for member in range(kept.shape[0]):
            keep[place] = plus(kept[member, :half], got[member, :half])
            send[place] = plus(kept[member, half:], got[member, half:])
            place += 1


def part_kernel(first, keep, got, near, distant):
    for place in range(4):
        near[place] = plus(keep[first + place], got[first + place])
        distant[place] = plus(keep[first + 4 + place], got[first + 4 + place])


def add_kernel(a, b, out):
    out[...] = a[...] + b[...]


def sums_call(name, *sides, after=(), token=False):
    return call(name, None, 3, [], [], after=after, sides=sides, token=token)


def emit_call(ffn, attention):
    depth = len(ffn)
    terms = [array for _, arrays in ffn + attention for array in arrays]
    chunk, part = terms[0].shape[1:]
    shapes = [
        (depth, chunk, PIECES * part), (depth, chunk, PIECES * part),
        (depth, 3, chunk, part), (depth, chunk, part),
    ]

    def kernel(*refs):
        up, down, qkv, out = refs[len(terms) :]
        at = 0
        for number, (first, arrays) in enumerate(ffn):
            here = refs[at : at + len(arrays)]
            at += len(arrays)
            for place in range(2 * PIECES):
                total = sum(term[first + place].astype(f32) for term in here)
                start = place % PIECES * part
                (up, down)[place // PIECES][number, :, start : start + part] = total
        for number, (first, arrays) in enumerate(attention):
            here = refs[at : at + len(arrays)]
            at += len(arrays)
            for member in range(4):
                total = sum(term[first + member].astype(f32) for term in here)
                if member < 3:
                    qkv[number, member] = total
                else:
                    out[number] = total

    return call(
        "emit", kernel, 1, [whole(term) for term in terms],
        [(shape, f32, spec(shape)) for shape in shapes], token=True,
    )


def widen_call(arrays, after=()):
    def kernel(*refs):
        for source, out in zip(refs[: len(arrays)], refs[len(arrays) :]):
            out[...] = source[...].astype(f32)

    rows, width = arrays[0].shape
    block = spec((rows // 4, width), lambda i, *s: (i, 0))
    return call(
        "widen", kernel, 4, [(array, block, True) for array in arrays],
        [((rows, width), f32, block) for _ in arrays], after=after,
    )


def share_call(low, head, ids, class_bins, after):
    high = lax.Precision.HIGHEST

    def kernel(low, head, ids, class_bins, out):
        logits = dot_nt(low[...], head[...])
        expos = jnp.exp(logits - jnp.max(logits, axis=-1, keepdims=True))
        shares = expos / jnp.sum(expos, axis=-1, keepdims=True)
        mask = (ids[:, : low.shape[0]] >= special_ids).astype(f32)
        sums = jnp.dot(mask, shares, precision=high, preferred_element_type=f32)
        bins = lax.broadcasted_iota(jnp.int32, (LANES, class_bins.shape[1]), 0)
        table = (bins == class_bins[...]).astype(f32)
        totals = lax.dot_general(
            jnp.broadcast_to(sums, (8, sums.shape[1])), table, (((1,), (1,)), ((), ())),
            precision=high, preferred_element_type=f32,
        )[0:1]
        lane = lax.broadcasted_iota(jnp.int32, (1, LANES), 1)
        out[...] = jnp.where(lane == BINS, jnp.sum(mask), jnp.where(lane < BINS, totals, 0.0))

    args = (low, head, ids, class_bins)
    return call(
        "share", kernel, 1, [whole(array) for array in args],
        [((1, LANES), f32, spec((1, LANES)))], after=(after,),
    )[0]


def pack_small(layers, bin_row, width):
    count = len(layers)
    part, units = layers[0][3].shape[3], layers[0][4].shape[2]
    folds = units // width
    shared = 6 * count + 1
    total = shared + count * (3 + folds)
    args = [array for layer in layers for array in layer] + [bin_row]

    def kernel(*refs):
        own, other = refs[-1].at[0], refs[-1].at[1]
        own[...] = jnp.zeros((total, width), f32)
        for number in range(count):
            one, two, down, _, _ = refs[5 * number : 5 * number + 5]
            own[6 * number : 6 * number + 2] = one[0:2]
            own[6 * number + 2 : 6 * number + 5] = two[...]
            own[6 * number + 5 : 6 * number + 6] = down[down.shape[0] - 1 :]
        bins = refs[5 * count]
        own[6 * count : 6 * count + 1, : bins.shape[1]] = bins[...]
        other[...] = own[...]
        for number in range(count):
            qkv, up = refs[5 * number + 3 : 5 * number + 5]
            start = shared + number * (3 + folds)
            for side, out in enumerate((own, other)):
                for member in range(3):
                    out[start + member : start + member + 1, :part] = qkv[side, member]
                for fold in range(folds):
                    row = start + 3 + fold
                    out[row : row + 1] = up[side, :, fold * width : (fold + 1) * width]

    shape = (2, total, width)
    return call(
        "pack_small", kernel, 1, [whole(array) for array in args], [(shape, f32, spec(shape))]
    )[0]


def unpack_small(terms, count, part, units, after=()):
    width = terms[0].shape[1]
    folds = units // width
    shared = 6 * count + 1

    def kernel(*refs):
        outs = refs[len(terms) :]
        sums = sum(term[...] for term in refs[: len(terms)])
        qkv, up, bins, tokens = outs[6:]
        for number in range(count):
            for member in range(6):
                row = 6 * number + member
                outs[member][number : number + 1] = sums[row : row + 1]
            start = shared + number * (3 + folds)
            for member in range(3):
                row = start + member
                qkv[member, number : number + 1] = sums[row : row + 1, :part]
            for fold in range(folds):
                row = start + 3 + fold
                up[number : number + 1, fold * width : (fold + 1) * width] = sums[row : row + 1]
        row = sums[6 * count : 6 * count + 1, :LANES]
        tally = row[:, BINS : BINS + 1]
        bins[...] = BINS * row / jnp.maximum(tally, 1.0)
        tokens[...] = jnp.broadcast_to(tally, tokens.shape).astype(jnp.int32)

    shapes = [((count, width), f32)] * 6 + [
        ((3, count, part), f32), ((count, units), f32), ((1, LANES), f32), ((1, LANES), jnp.int32)
    ]
    outs = call(
        "unpack_small", kernel, 1, [hot(term) for term in terms],
        [(shape, dtype, spec(shape)) for shape, dtype in shapes], after=after,
    )
    return outs[:6], outs[6], outs[7], outs[8], outs[9]


def segment_info(seq_lengths, total):
    ends = jnp.cumsum(seq_lengths)
    places = jnp.arange(total, dtype=jnp.int32)
    labels = jnp.sum((places[:, None] >= ends[None, :-1]).astype(jnp.int32), axis=1)
    starts = ends - seq_lengths
    picks = labels[:, None] == jnp.arange(seq_lengths.shape[0], dtype=jnp.int32)[None, :]
    begin = jnp.sum(jnp.where(picks, starts[None, :], 0), axis=1)
    return (labels, places - begin)


def moves(dp_size, tensor_size):
    def flat(dp, tensor):
        return dp * tensor_size + tensor

    every = [(dp, tensor) for dp in range(dp_size) for tensor in range(tensor_size)]

    def by(target):
        return [(flat(*where), flat(*target(*where))) for where in every]

    return {
        "swap": by(lambda dp, tensor: (dp - dp % 2 + tensor, dp % 2)),
        "y": by(lambda dp, tensor: (dp, 1 - tensor)),
        "z": by(lambda dp, tensor: (dp ^ 12 if dp_size > 8 else dp, tensor)),
        "bits": [
            by(lambda dp, tensor, bit=bit: (dp ^ bit, tensor))
            for bit in (1 << place for place in range(dp_size.bit_length() - 1))
        ],
    }


def per_device(
    x_in,
    lengths,
    token_ids,
    ln1_gain,
    ln1_bias,
    w_qkv,
    b_qkv,
    w_out,
    b_out,
    ln2_gain,
    ln2_bias,
    w_up,
    b_up,
    w_down,
    b_down,
    head,
    class_bins,
    cotangent,
):
    rows, width = x_in.shape
    dp_size = lax.axis_size("dp")
    tensor_size = lax.axis_size("tensor")
    depth = w_qkv.shape[0]
    part = w_qkv.shape[3]
    units = w_up.shape[2]
    total = rows * tensor_size
    dp = lax.axis_index("dp")
    core = dp % 2
    bits = dp_size.bit_length() - 1
    move = moves(dp_size, tensor_size)

    def send(array, name):
        return lax.ppermute(array, AXES, move["bits"][name] if isinstance(name, int) else move[name])

    w_qkv = jnp.transpose(w_qkv, (0, 2, 1, 3))
    z_bit = min(2, bits - 1)

    def slots_of(bit):
        own = ((dp >> bit) % 2) * 2 + core
        return jnp.stack([own, own ^ 2, own ^ 1, own ^ 3]).astype(jnp.int32)

    all_slots = (slots_of(1), slots_of(z_bit))

    class Bundle:
        def __init__(self, way, packed):
            self.way, self.packed = way, packed

        def begin(self, *tokens):
            packed = gate(self.packed, tokens) if tokens else self.packed
            self.got = send(packed, "y")
            return packed

        def hop(self, *tokens):
            if tokens:
                self.got = gate(self.got, tokens)
            self.beside = send(self.got, (1, z_bit)[self.way])
            self.across = send(self.got, 0)
            return self.got

        def end(self, *tokens):
            beside = gate(self.beside, tokens) if tokens else self.beside
            pieces = [self.got, beside, self.across, send(beside, 0)]
            self.far = (all_slots[self.way], pieces)
            return beside

    chunk_rows = width // PIECES
    (packed,) = pack_call(0, all_slots, [(0, ((w_qkv, (1, 2)),))])
    key_bundle = Bundle(0, packed)
    key_bundle.begin()
    key_bundle.hop()
    x_low = gate(x_in.astype(bf16), (packed,))
    stream = send(x_low, "swap")
    numbers = send(gate(jnp.concatenate([token_ids, lengths[0]]), (packed,)), "swap")
    seq_lengths = numbers[rows:]
    far_biases = send(
        gate(jnp.concatenate([b_up, b_qkv.reshape(depth, -1)], axis=1), (packed,)), "y"
    )
    b_qkv = jnp.transpose(b_qkv, (1, 0, 2))
    cotangent_low = cotangent.astype(bf16)
    heads, ups, downs = [], [], []
    for number in range(depth):
        members = (0, 1, 2) if number else (0,)
        arrays = pack_call(
            number, all_slots,
            [(1, ((w_qkv, members), w_out)), (0, (w_up,)), (1, (w_down,))],
            (packed, x_low) if number else (packed, x_low, cotangent_low),
        )
        for store, way, array in zip((heads, ups, downs), (1, 0, 1), arrays):
            store.append(Bundle(way, array))
    heads[0].begin(key_bundle.got)
    ups[0].begin(heads[0].got)

    def far_heads(number):
        if number:
            return [(*heads[number].far, member) for member in range(3)]
        return [(*heads[0].far, 0), (*key_bundle.far, 0), (*key_bundle.far, 1)]

    def far_out(number):
        return (*heads[number].far, (3 if number else 1) * chunk_rows)


    labels, places = segment_info(seq_lengths, total)
    labels_here = lax.dynamic_slice_in_dim(labels, core * rows, rows, 0)
    labels_far = lax.dynamic_slice_in_dim(labels, (1 - core) * rows, rows, 0)
    places_here = lax.dynamic_slice_in_dim(places, core * rows, rows, 0)
    lane = jnp.arange(LANES, dtype=jnp.int32)[None, :]
    freqs = theta ** (-(lane % HALF).astype(f32) / HALF)
    angles = places_here.astype(f32)[:, None] * freqs
    sine = jnp.sin(angles)
    tables = (jnp.cos(angles), jnp.where(lane % HEAD_DIM < HALF, -sine, sine))
    place = lane % HEAD_DIM
    q_mark = jnp.where(labels_here[:, None] == place, far, 0.0).astype(bf16)

    def key_mark(own):
        other = (own[:, None] != place) & (place < 3)
        return jnp.where(other, 1.0, jnp.where((place >= 3) & (place < 6), -1.0, 0.0)).astype(bf16)

    marks = (q_mark, key_mark(labels_here), key_mark(labels_far))
    chunk = width // dp_size
    order = jnp.arange(width, dtype=jnp.int32)
    block, inside = order // chunk, order % chunk
    home = sum(
        (((block >> (bits - 1 - place)) & 1) << place) for place in range(bits)
    )
    order = (home ^ dp) * chunk + inside
    turn = (order[:, None] == jnp.arange(width, dtype=jnp.int32)[None, :]).astype(bf16)

    def turned(array):
        return lax.dot_general(turn, array, (((1,), (1,)), ((), ())), preferred_element_type=bf16)

    saved = []
    wait = ()
    for number in range(depth):
        more = number + 1 < depth
        normed_attn, n_t_attn, q, kv = qkv_call(
            number, (0, 1, 2), stream, (ln1_gain, ln1_bias, turn), w_qkv, b_qkv, tables,
            after=wait,
        )
        if number == 0:
            key_bundle.end()
            wait = (heads[0].hop(kv),)
        else:
            wait = ()
        key_far = (*key_bundle.far, 0) if number == 0 else far_heads(number)[1]
        (kv,) = qkv_call(
            number, (1, 2), normed_attn, None, key_far, far_biases, tables, (kv,), wait
        )
        kv_far = send(kv, 0)
        wait = ()
        if number == 0:
            heads[0].end(kv)
            wait = (ups[0].hop(kv), downs[0].begin(ups[0].got, kv))
        (q,) = qkv_call(
            number, (0,), normed_attn, None, far_heads(number)[0], far_biases, tables, (q,),
            (kv, *wait),
        )
        wait = (downs[number].hop(q),) if number else ()
        if not more:
            late = gate(cotangent_low, (downs[number].got, q))
            pairs_apart = [pair for pair in move["swap"] if pair[0] != pair[1]]
            grad_stream = lax.ppermute(late, AXES, pairs_apart)
            wait += (late,)
        att, logsum = attention_call(q, kv, kv_far, marks, wait)
        if number == 0:
            wait = (ups[0].end(att), downs[0].hop(att))
        else:
            wait = (ups[number].end(att), downs[number].end(att))
        if more:
            wait += (heads[number + 1].begin(downs[number].got, att),)
        middle, normed_ffn, n_t_ffn, active, slope, acc = ffn_call(
            number, stream, att, w_out, far_out(number), (b_out, ln2_gain, ln2_bias, b_down),
            turn, w_up, b_up, w_down, wait,
        )
        wait = (downs[0].end(acc),) if number == 0 else ()
        if more:
            wait += (heads[number + 1].hop(acc), ups[number + 1].begin(heads[number + 1].got, acc))
        up_far, down_far = ups[number].far, downs[number].far
        active_o, slope_o, below, low = ffn_far_call(
            number, normed_ffn, acc, up_far, down_far, far_biases, units, wait
        )
        if more:
            wait = (
                heads[number + 1].end(low),
                ups[number + 1].hop(low),
                downs[number + 1].begin(ups[number + 1].got, low),
            )
        saved.append(
            (stream, n_t_attn, (q, kv, kv_far), logsum, att, middle, n_t_ffn,
             (active, slope), (active_o, slope_o))
        )
        stream = below
    out_low = send(low, "swap")
    stays = core == lax.axis_index("tensor")
    grad_stream = jnp.where(stays, cotangent_low, gate(grad_stream, (low,)))
    half = width // 2
    quarter, eighth = half // 2, half // 4

    def pairs(*steps):
        return tuple(array for keep, sent, way in steps for array in (keep, send(sent, way)))

    def join_attention(*arrays):
        shapes = ((2, half, part),) * 2 + ((2, 2, quarter, part),) * 2
        return join_attention_kernel, arrays, shapes

    def join_line(*arrays):
        return join_line_kernel, arrays, ((8, 2, eighth, part),) * 2

    def inner(keep, sent, way):
        members, _, deep, cols = keep.shape
        return inner_kernel, pairs((keep, sent, way)), ((members, 2, deep // 2, cols),) * 2

    def final(keep, sent, way):
        return sum_kernel, pairs((keep, sent, way)), (keep.shape,)

    def cut(keep, sent, way):
        members, _, deep, cols = keep.shape
        return cut_kernel, pairs((keep, sent, way)), ((members, deep, cols),) * 2

    def turn_ways(joined):
        a_keep, a_send, b_keep, b_send = joined
        members, deep, cols = a_keep.shape
        shape_a, shape_b = (members, deep // 2, cols), b_keep.shape[1:]
        arrays = pairs((a_keep, a_send, "y"), (b_keep, b_send, 1))
        return turn_kernel, arrays, (shape_a, shape_a, shape_b, shape_b)

    def merge(*steps):
        members = sum(keep.shape[0] for keep, _, _ in steps)
        _, deep, cols = steps[0][0].shape
        return merge_kernel, pairs(*steps), ((members, deep // 2, cols),) * 2

    def merge_ways(turned):
        a_keep, a_send, b_keep, b_send = turned
        return merge((a_keep, a_send, 1), (b_keep, b_send, "y"))

    def part_sides(keep, sent, way):
        return (
            functools.partial(part_kernel, 0), pairs((keep, sent, way)),
            ((4,) + keep.shape[1:],) * 2,
        )

    def add_small(array, other, way):
        return add_kernel, (array, send(other, way)), (shaped(array.shape, f32),)

    def halves_small(both):
        def kernel(both, got, out):
            out[...] = both[0] + got[...]

        return kernel, (both, send(both[1], "y")), (shaped(both.shape[1:], f32),)

    def plain_sum(keep, got):
        total = plus(keep, got)
        total = plus(total[0], send(total[1], "y"))
        for bit in range(1, bits):
            rows_left = total.shape[-2] // 2
            total = plus(total[..., :rows_left, :], send(total[..., rows_left:, :], bit))
        return total.astype(f32)

    placed = bits == 4 and depth == 2
    pieces = [None] * depth
    plain = [None] * depth
    grad_low = grad_stream
    g_t = turned(grad_low)
    grad_b_down = column_sum(grad_stream.astype(f32))
    for number in reversed(range(depth)):
        stream, n_t_attn, keyed, logsum, att, middle, n_t_ffn, near, distant = saved[number]
        top, last = number == depth - 1, number == 0
        acc, ffn_k, ffn_s, d_b_up = ffn_back_call(
            number, grad_low, n_t_ffn, g_t, near, distant, w_up, w_down,
            ups[number].far, downs[number].far,
        )
        ffn_g = send(ffn_s, 0)
        sides = []
        if placed and not top:
            sides = [turn_ways(joined_ffn), join_line(qkv_k, qkv_g)]
        after = ()
        if last:
            bin_row = share_call(low, jnp.transpose(head), numbers[None], class_bins[None], d_b_up)
            after = (bin_row,)
        grad_middle, grad_att, gm_t, smalls_two, *more = middle_back_call(
            number, acc, middle, ln2_gain, grad_stream, w_out, far_out(number), turn,
            sides=sides, after=after,
        )
        if more:
            turned_ffn, lined = more
        after = ()
        if placed and last:
            mark, *joined_low = join_ffn_call(ffn_k, ffn_g, (smalls_two,))
            after = (mark,)
        gq, gkv, gkv_s = attention_back_call(
            *keyed, marks, logsum, att, grad_att, tables, after=after
        )
        gkv_g = send(gkv_s, 0)
        after = ()
        if placed and not last:
            mark, *joined_ffn = join_ffn_call(ffn_k, ffn_g, (gkv_s,))
            after = (mark,)
        elif placed:
            mark, merged_ffn, lined, turned_low = sums_call(
                "merge_above", merge_ways(turned_ffn), inner(*lined, z_bit), turn_ways(joined_low),
                after=(gkv_s,), token=True,
            )
            after = (mark,)
        weights, ending = (w_qkv, far_heads(number)), (stream, ln1_gain, grad_middle, turn)
        if placed and last:
            qkv_k, qkv_s, d_b_qkv = qkv_back_call(
                number, gq, gkv, gkv_g, tables, (n_t_attn, gm_t, att), after=after
            )
            qkv_g = send(qkv_s, 0)
            grad_stream, grad_low, smalls_one = qkv_back_call(
                number, gq, gkv, gkv_g, tables, None, weights, ending, after=(d_b_qkv,)
            )
        else:
            qkv_k, qkv_s, d_b_qkv, grad_stream, grad_low, *g_t, smalls_one = qkv_back_call(
                number, gq, gkv, gkv_g, tables, (n_t_attn, gm_t, att), weights, ending, after=after
            )
            g_t = g_t[0] if g_t else None
            qkv_g = send(qkv_s, 0)
        if not placed:
            plain[number] = (plain_sum(ffn_k, ffn_g), plain_sum(qkv_k, qkv_g))
        pieces[number] = (smalls_one, smalls_two, grad_b_down, d_b_qkv, d_b_up)
        grad_b_down = smalls_one
    grad_x_low = send(grad_low, "swap")
    both = pack_small(pieces, bin_row, width)
    if placed:
        joined_att, merged_low, ended_above, lined = sums_call(
            "tail_one", join_attention(qkv_k, qkv_g), merge_ways(turned_low),
            merge((*merged_ffn, z_bit)), cut(*lined, 3), after=(both,),
        )
        turned_att, ended_low, (both,) = sums_call(
            "tail_two", turn_ways(joined_att), merge((*merged_low, z_bit)),
            add_small(both, both, 0),
        )
        merged_att, (near_1, far_1), (sums,), (ffn_1,) = sums_call(
            "tail_three", merge_ways(turned_att), part_sides(*lined, 1), halves_small(both),
            final(*ended_above, 3),
        )
        ended_att, (ffn_0,), (sums,), (att_1,) = sums_call(
            "tail_four", merge((*merged_att, z_bit)), final(*ended_low, 3),
            add_small(sums, sums, 1), final(near_1, far_1, "y"),
        )
        out_act, grad_x = widen_call((out_low, grad_x_low), ended_att[1:2])
        terms = (sums, send(sums, 2), send(sums, 3), send(sums, "z"))
        ended_ffn = [(0, (ffn_0,)), (0, (ffn_1,))]
        ended_attention = [(0, pairs((*ended_att, 3))), (0, (att_1,))]
        mark, grad_w_up, grad_w_down, grad_w_qkv, grad_w_out = emit_call(ended_ffn, ended_attention)
        late = (mark,)
    else:
        grad_w_up, grad_w_down = (
            jnp.stack([
                jnp.concatenate([ffn[which, place] for place in range(PIECES)], axis=-1)
                for ffn, _ in plain
            ])
            for which in range(2)
        )
        grad_w_qkv = jnp.stack([entry[1][:3] for entry in plain])
        grad_w_out = jnp.stack([entry[1][3] for entry in plain])
        out_act, grad_x = widen_call((out_low, grad_x_low))
        sums = both[0] + send(both[1], "y")
        for bit in range(bits - 1):
            sums = sums + send(sums, bit)
        late = ()
        terms = (sums, send(sums, bits - 1))
    replicated, sharded_qkv, sharded_up, bin_density, count = unpack_small(
        terms, depth, part, units, late
    )

    return (
        out_act,
        grad_x,
        replicated[0],
        replicated[1],
        jnp.transpose(grad_w_qkv, (0, 2, 1, 3)),
        jnp.transpose(sharded_qkv, (1, 0, 2)),
        jnp.transpose(grad_w_out, (0, 2, 1)),
        replicated[4],
        replicated[2],
        replicated[3],
        grad_w_up,
        sharded_up,
        jnp.transpose(grad_w_down, (0, 2, 1)),
        replicated[5],
        bin_density[0, :BINS],
        count[0, 0],
    )


def solution(mesh):
    placed = (
        P(("dp", "tensor"), None),
        P("dp", None),
        P(("dp", "tensor")),
        P(),
        P(),
        P(None, None, None, "tensor"),
        P(None, None, "tensor"),
        P(None, "tensor", None),
        P(),
        P(),
        P(),
        P(None, None, "tensor"),
        P(None, "tensor"),
        P(None, "tensor", None),
        P(),
        P(),
        P(),
        P(("dp", "tensor"), None),
    )
    return jax.shard_map(
        per_device,
        mesh=mesh,
        in_specs=placed,
        out_specs=(
            P(("dp", "tensor"), None),
            P(("dp", "tensor"), None),
            P(),
            P(),
            P(None, "dp", None, "tensor"),
            P(None, None, "tensor"),
            P(None, "tensor", "dp"),
            P(),
            P(),
            P(),
            P(None, "dp", "tensor"),
            P(None, "tensor"),
            P(None, "tensor", "dp"),
            P(),
            P(),
            P(),
        ),
        check_vma=False,
    )
```

```python
import functools

import jax
import jax.numpy as jnp
from jax import lax
from jax.experimental import pallas as pl
from jax.experimental.pallas import tpu as pltpu
from jax.sharding import PartitionSpec as P

HEAD_DIM = 64
HALF = HEAD_DIM // 2
BINS = 24
LANES = 128
PIECES = 4
VMEM_MIB = {
    "join_ffn": 20, "merge_above": 24, "tail_one": 24, "tail_two": 24, "tail_three": 24, "middle_back": 36
}
COSTS = {}

eps = 1e-05
theta = 10000.0
special_ids = 5
far = -1e30

bf16 = jnp.bfloat16
f32 = jnp.float32
AXES = ("dp", "tensor")


def dot(a, b):
    return jnp.dot(a, b, preferred_element_type=f32)


def dot_nt(a, b):
    return lax.dot_general(a, b, (((1,), (1,)), ((), ())), preferred_element_type=f32)


def normalize(rows):
    centre = rows - jnp.mean(rows, axis=-1, keepdims=True)
    spread = jnp.mean(centre * centre, axis=-1, keepdims=True)
    scale = lax.rsqrt(spread + eps)
    return centre * scale, scale


def norm_backward(rows, gain, grad):
    unit, scale = normalize(rows)
    gained = grad * gain
    mean_grad = jnp.mean(gained, axis=-1, keepdims=True)
    mean_both = jnp.mean(gained * unit, axis=-1, keepdims=True)
    below = scale * (gained - mean_grad - unit * mean_both)
    return below, column_sum(grad * unit), column_sum(grad)


def column_sum(rows):
    return jnp.sum(rows, axis=0, keepdims=True)


def rotate(rows, cosine, sine, sign):
    lane = lax.broadcasted_iota(jnp.int32, cosine.shape, 1)
    low = lane % HEAD_DIM < HALF
    pieces = []
    for start in range(0, rows.shape[1], LANES):
        piece = rows[:, start : start + LANES]
        other = jnp.where(low, pltpu.roll(piece, LANES - HALF, 1), pltpu.roll(piece, HALF, 1))
        pieces.append(piece * cosine + sign * (other * sine))
    return jnp.concatenate(pieces, axis=1)


def gelu_pair(value):
    size = jnp.abs(value) * (2.0**-0.5)
    t = 1.0 / (1.0 + 0.3275911 * size)
    bell = jnp.exp(-0.5 * value * value)
    poly = t * (
        0.5 * 0.254829592
        + t
        * (
            0.5 * -0.284496736
            + t * (0.5 * 1.421413741 + t * (0.5 * -1.453152027 + t * (0.5 * 1.061405429)))
        )
    )
    tail = poly * bell
    share = jnp.where(value < 0, tail, 1.0 - tail)
    return value * share, share + value * bell * 0.3989422804014327


def three_parts(column):
    high = column.astype(bf16).astype(f32)
    rest = column - high
    middle = rest.astype(bf16).astype(f32)
    return high, middle, rest - middle


def spec(shape, index=None):
    zeros = (0,) * len(shape)
    return pl.BlockSpec(shape, index or (lambda i, *s: zeros))


def whole(array):
    return array, spec(array.shape)


def hot(array):
    return array, spec(array.shape), True


def cold(array):
    return pltpu.with_memory_space_constraint(array, pltpu.HBM)


def shaped(shape, dtype):
    return jax.ShapeDtypeStruct(shape, dtype)


def call(
    name, kernel, steps, operands, results, prefetch=(), scratch=(), alias=(), after=(), sides=(),
    token=False,
):
    def side_spec(shape):
        lead = (0,) * (len(shape) - 1)
        return spec(
            tuple(shape[:-1]) + (shape[-1] // 3,), lambda i, *s: (*lead, jnp.minimum(i, 2))
        )

    own_in, own_out = len(operands), len(results) + token
    idle = [array for array, _ in alias] + list(after)
    if token:
        results = [((8, LANES), f32, spec((8, LANES))), *results]
    arrays = [entry[0] if len(entry) > 2 else cold(entry[0]) for entry in operands]
    in_specs = [entry[1] for entry in operands]
    out_specs = [entry[2] for entry in results]
    out_shape = [
        (shaped if len(entry) > 3 else pltpu.HBM)(entry[0], entry[1]) for entry in results
    ]
    for _, side_args, side_shapes in sides:
        in_specs += [side_spec(arg.shape) for arg in side_args]
        out_specs += [side_spec(getattr(shape, "shape", shape)) for shape in side_shapes]
        out_shape += [
            shape
            if hasattr(shape, "dtype")
            else (shaped if name.startswith("tail") else pltpu.HBM)(shape, bf16)
            for shape in side_shapes
        ]
        arrays += side_args
    ahead, count_in, count_out = len(prefetch), len(in_specs), len(out_specs)

    def body(*refs):
        early, refs = refs[:ahead], refs[ahead + len(idle) :]
        ins, outs, rest = (
            refs[:count_in], refs[count_in : count_in + count_out], refs[count_in + count_out :]
        )
        if token:
            outs[0][...] = jnp.zeros((8, LANES), f32)
        if kernel is not None:
            kernel(*early, *ins[:own_in], *outs[token:own_out], *rest)

        def run_sides():
            at_in, at_out = own_in, own_out
            for side_kernel, side_args, side_shapes in sides:
                side_kernel(
                    *ins[at_in : at_in + len(side_args)], *outs[at_out : at_out + len(side_shapes)]
                )
                at_in, at_out = at_in + len(side_args), at_out + len(side_shapes)

        if sides and steps > 3:
            pl.when(pl.program_id(0) < 3)(run_sides)
        else:
            run_sides()

    made = pl.pallas_call(
        body,
        grid_spec=pltpu.PrefetchScalarGridSpec(
            num_scalar_prefetch=ahead,
            grid=(steps,),
            in_specs=[pl.BlockSpec(memory_space=pl.ANY)] * len(idle) + in_specs,
            out_specs=out_specs,
            scratch_shapes=list(scratch),
        ),
        out_shape=out_shape,
        name=name,
        input_output_aliases={
            ahead + place: result for place, (_, result) in enumerate(alias)
        },
        compiler_params=pltpu.CompilerParams(vmem_limit_bytes=VMEM_MIB.get(name, 44) << 20),
        cost_estimate=pl.CostEstimate(
            flops=int(COSTS.get(name, 6e10)), bytes_accessed=int(4e6), transcendentals=0
        ),
    )
    outs = made(*prefetch, *idle, *arrays)
    done, at = list(outs[:own_out]), own_out
    for _, _, side_shapes in sides:
        done.append(outs[at : at + len(side_shapes)])
        at += len(side_shapes)
    return done


def gate(array, after):
    return lax.optimization_barrier((array, *after))[0]


def gather_rows(target, slots, pieces, lane=0):
    count, lanes = pieces[0].shape
    for place, piece in enumerate(pieces):
        start = pl.multiple_of(slots[place] * count, 16)
        target[pl.ds(start, count), lane : lane + lanes] = piece[...]


def qkv_kernel(number, base, members, first, distant, *refs):
    refs = list(refs)
    slots = refs.pop(0) if distant else None
    if first:
        x, gain, bias, turn = refs[:4]
        refs = refs[4:]
    else:
        normed = refs.pop(0)
    pieces, refs = (refs[:PIECES], refs[PIECES:]) if distant else (refs[:1], refs[1:])
    b, cosine, sine, *refs = refs
    if first:
        normed, n_t, *refs = refs
    queries = refs.pop(0) if 0 in members else None
    kv = refs.pop(0) if 1 in members else None
    step = pl.program_id(0)
    if first:

        @pl.when(step == 0)
        def _():
            unit, _ = normalize(x[...].astype(f32))
            normed[...] = (
                unit * gain[number : number + 1] + bias[number : number + 1]
            ).astype(bf16)
            n_t[...] = dot_nt(turn[...], normed[...]).astype(bf16)

    if distant:
        (matrix,) = refs
        gather_rows(matrix, slots, pieces)
        weight = matrix[...]
    else:
        weight = pieces[0][0, 0]
    row = slice(number, number + 1)
    mixed = dot(normed[...], weight) + (b[row] if len(b.shape) == 2 else b[0, row])
    for member in members:

        @pl.when(step == member - base)
        def _(member=member):
            if member == 0:
                turned = rotate(mixed, cosine[...], sine[...], 1.0)
                queries[...] = (turned * HEAD_DIM**-0.5).astype(bf16)
            elif member == 1:
                kv[0] = rotate(mixed, cosine[...], sine[...], 1.0).astype(bf16)
            else:
                kv[0] = mixed.astype(bf16)


def qkv_call(number, members, rows_in, norm, weight, b, tables, prior=(), after=()):
    first, distant = norm is not None, isinstance(weight, tuple)
    rows, width = rows_in.shape
    part = width // 2
    base = members[0]
    operands = [whole(rows_in) if first and number else hot(rows_in)]
    if first:
        operands += [whole(array) for array in norm[:2]] + [hot(norm[2])]
    prefetch, scratch = (), ()
    if distant:
        slots, pieces, lead = weight
        prefetch = (slots,)
        operands += [
            (piece, spec((width // PIECES, part), lambda i, *s: (i + lead, 0)), True)
            for piece in pieces
        ]
        scratch = (pltpu.VMEM((width, part), bf16),)
    else:
        block = spec((1, 1, width, part), lambda i, *s: (number, i + base, 0, 0))
        operands.append((weight, block))
    if distant:
        skip = (b.shape[1] - 3 * part) // part + base
        operands.append((b, spec((b.shape[0], part), lambda i, *s: (0, i + skip))))
    else:
        operands.append((b, spec((1, b.shape[1], part), lambda i, *s: (i + base, 0, 0))))
    operands += [hot(table) for table in tables]
    half = 1 if distant else 0
    results = []
    if first:
        results += [
            ((rows, width), bf16, spec((rows, width)), True),
            ((width, rows), bf16, spec((width, rows))),
        ]
    alias = []
    if 0 in members:
        if prior:
            alias.append((prior[0], len(results)))
        results.append(
            ((rows, 2 * part), bf16, spec((rows, part), lambda i, *s: (0, half)), True)
        )
    if 1 in members:
        if prior:
            alias.append((prior[-1], len(results)))
        block = spec(
            (1, rows, part), lambda i, *s: (jnp.maximum(i + base - 1, 0), 0, half)
        )
        results.append(((2, rows, 2 * part), bf16, block, True))
    return call(
        "qkv",
        functools.partial(qkv_kernel, number, base, members, first, distant),
        len(members),
        operands,
        results,
        prefetch,
        scratch,
        alias,
        after,
    )


def head_lanes(shape, head):
    lane = lax.broadcasted_iota(jnp.int32, shape, 1)
    return (lane < HEAD_DIM) if head == 0 else (lane >= HEAD_DIM)


def attention_kernel(q, kv, kv_far, q_mark, k_mark, k_mark_far, out, logsum):
    rows = q.shape[0]
    queries = q[...]
    scores, values = [], []
    for head in range(2):
        mine = head_lanes((rows, LANES), head)
        marked = jnp.where(mine, queries, q_mark[...])
        for pair, mark in ((kv, k_mark), (kv_far, k_mark_far)):
            scores.append(dot_nt(marked, jnp.where(mine, pair[0], mark[...])))
            values.append(jnp.where(mine, pair[1], jnp.ones_like(pair[1])))
    highest, expos = [], []
    for head in range(2):
        near, distant = scores[2 * head : 2 * head + 2]
        highest.append(
            jnp.maximum(
                jnp.max(near, axis=-1, keepdims=True), jnp.max(distant, axis=-1, keepdims=True)
            )
        )
        expos += [jnp.exp(score - highest[head]).astype(bf16) for score in (near, distant)]
    results, logs = [], []
    for head in range(2):
        total = dot(expos[2 * head], values[2 * head])
        total = total + dot(expos[2 * head + 1], values[2 * head + 1])
        column = HEAD_DIM if head == 0 else 0
        summed = total[:, column : column + 1]
        results.append(total / summed)
        logs.append(highest[head] + jnp.log(summed))
    out[...] = jnp.where(head_lanes((rows, LANES), 0), results[0], results[1]).astype(bf16)
    logsum[...] = jnp.where(head_lanes((rows, LANES), 0), logs[1], logs[0])


def head_specs(rows):
    column = spec((rows, LANES), lambda i, *s: (0, i))
    both = spec((2, rows, LANES), lambda i, *s: (0, 0, i))
    return column, both


def attention_call(q, kv, kv_far, marks, after=(), sides=()):
    rows, width = q.shape
    column, both = head_specs(rows)
    return call(
        "attention",
        attention_kernel,
        width // LANES,
        [(q, column, True), (kv, both, True), (kv_far, both, True)] + [hot(mark) for mark in marks],
        [((rows, width), bf16, column), ((rows, width), f32, column)],
        after=after,
        sides=sides,
    )


def attention_back_kernel(
    q, kv, kv_far, q_mark, k_mark, k_mark_far, logsum, attended, grad, cosine, sine,
    grad_q, grad_kv, grad_kv_far,
):
    rows = q.shape[0]
    queries = q[...]
    grads = grad[...]
    lane = lax.broadcasted_iota(jnp.int32, (rows, LANES), 1) % HEAD_DIM
    logs = three_parts(logsum[...])
    log_mark = sum(
        jnp.where(lane == 3 + place, part, 0.0) for place, part in enumerate(logs)
    ).astype(bf16)
    product = attended[...].astype(f32) * grads.astype(f32)
    value_mark = jnp.where(lane < 3, -1.0, 0.0).astype(bf16)
    dots_t = []
    keys_t = [
        jnp.transpose(pair[0].astype(f32)).astype(bf16) for pair in (kv, kv_far)
    ]
    outs = ([], [])
    for head in range(2):
        mine = head_lanes((rows, LANES), head)
        centre = jnp.sum(jnp.where(mine, product, 0.0), axis=-1, keepdims=True)
        centre_mark = sum(
            jnp.where(lane == place, part, 0.0) for place, part in enumerate(three_parts(centre))
        ).astype(bf16)
        marked = jnp.where(mine, queries, q_mark[...] + log_mark)
        marked_grads = jnp.where(mine, grads, centre_mark)
        turned = 0.0
        for place, (pair, mark) in enumerate(((kv, k_mark), (kv_far, k_mark_far))):
            keys = jnp.where(mine, pair[0], mark[...])
            values = jnp.where(mine, pair[1], value_mark)
            probs = jnp.exp(dot_nt(keys, marked))
            grad_scores = (probs * dot_nt(values, marked_grads)).astype(bf16)
            grad_values = dot(probs.astype(bf16), grads)
            grad_keys = dot(grad_scores, queries)
            turned = turned + dot(
                keys_t[place][head * HEAD_DIM : (head + 1) * HEAD_DIM], grad_scores
            )
            outs[place].append((grad_keys, grad_values))
        dots_t.append(turned)
    grad_queries = jnp.transpose(jnp.concatenate(dots_t, axis=0)) * HEAD_DIM**-0.5
    grad_q[...] = rotate(grad_queries, cosine[...], sine[...], -1.0).astype(bf16)
    mine = head_lanes((rows, LANES), 0)
    for ref, (one, two) in zip((grad_kv, grad_kv_far), outs):
        for member in range(2):
            ref[member] = jnp.where(mine, one[member], two[member]).astype(ref.dtype)


def attention_back_call(q, kv, kv_far, marks, logsum, attended, grad, tables, after=(), sides=()):
    rows, width = q.shape
    column, both = head_specs(rows)
    return call(
        "attention_back",
        attention_back_kernel,
        width // LANES,
        [(q, column), (kv, both), (kv_far, both)]
        + [hot(mark) for mark in marks]
        + [(logsum, column), (attended, column), (grad, column, True)]
        + [hot(table) for table in tables],
        [
            ((rows, width), bf16, column, True),
            ((2, rows, width), bf16, both, True),
            ((2, rows, width), bf16, both, True),
        ],
        after=after,
        sides=sides,
    )


def out_operands(pieces, part, row):
    low = part // PIECES
    return [
        (piece, spec((low, part), lambda i, *s, side=side: (row // low + side, 0)), True)
        for side in range(2)
        for piece in pieces
    ]


def gather_out(target, slots, pieces):
    part = target.shape[0]
    for side in range(2):
        gather_rows(target, slots, pieces[side * PIECES :][:PIECES], side * part)


def ffn_kernel(number, slots, *refs):
    x, att, wo_n = refs[:3]
    wo_pieces, refs = refs[3 : 3 + 2 * PIECES], refs[3 + 2 * PIECES :]
    (b_out, gain, bias, b_down, turn, w_up, b_up, w_down,
     middle, normed, n_t, active, slope, acc, wo_o) = refs
    row = slice(number, number + 1)

    @pl.when(pl.program_id(0) == 0)
    def _():
        part = wo_o.shape[0]
        gather_out(wo_o, slots, wo_pieces)
        mid = (
            x[...].astype(f32)
            + dot(att[:, :part], wo_n[0])
            + dot(att[:, part:], wo_o[...])
            + b_out[row]
        )
        middle[...] = mid
        unit, _ = normalize(mid)
        normed[...] = (unit * gain[row] + bias[row]).astype(bf16)
        n_t[...] = dot_nt(turn[...], normed[...]).astype(bf16)
        acc[...] = mid + b_down[row]

    hidden = dot(normed[...], w_up[0]) + b_up[row]
    value, back = gelu_pair(hidden)
    value = value.astype(bf16)
    active[...] = value
    slope[...] = back.astype(bf16)
    acc[...] += dot(value, w_down[0])


def ffn_call(number, x, att, w_out, heads_far, small, turn, w_up, b_up, w_down, after=()):
    rows, width = x.shape
    units, part = w_up.shape[2], w_out.shape[1]
    slots, pieces, row = heads_far
    b_out, gain, bias, b_down = small
    block = 2 * units // PIECES
    near = (True,) if number else ()
    wide = spec((rows, block), lambda i, *s: (0, i))
    full = spec((rows, width))
    return call(
        "ffn",
        functools.partial(ffn_kernel, number),
        units // block,
        [
            whole(x),
            whole(att),
            (w_out, spec((1, part, width), lambda i, *s: (number, 0, 0))),
            *out_operands(pieces, part, row),
            *[whole(array) for array in (b_out, gain, bias, b_down)],
            hot(turn),
            (w_up, spec((1, width, block), lambda i, *s: (number, 0, i))),
            (b_up, spec((b_up.shape[0], block), lambda i, *s: (0, i))),
            (w_down, spec((1, block, width), lambda i, *s: (number, i, 0))),
        ],
        [
            ((rows, width), f32, full),
            ((rows, width), bf16, full) + near,
            ((width, rows), bf16, spec((width, rows))),
            ((rows, units), bf16, wide),
            ((rows, units), bf16, wide),
            ((rows, width), f32, full) + near,
        ],
        prefetch=(slots,),
        scratch=(pltpu.VMEM((part, width), bf16),),
        after=after,
    )


def far_ffn_operands(up_far, down_far, width, units):
    slots_u, ups = up_far
    slots_d, downs = down_far
    block = 2 * units // PIECES

    def at(i, slots):
        return slots[jnp.clip(i, 0, 1)] // 2

    ups = [
        (piece, spec((width // PIECES, block), lambda i, *s: (0, at(i, s[0]))), True)
        for piece in ups
    ]
    downs = [(piece, spec((units // PIECES, width)), True) for piece in downs]
    return ups, downs, at, (slots_d, slots_u)


def gather_down(target, step, slots, downs):
    for place in range(2):

        @pl.when(step == place)
        def _(place=place):
            for which in (place, place + 2):
                count = downs[which].shape[0]
                start = pl.multiple_of((slots[which] % 2) * count, 16)
                target[pl.ds(start, count), :] = downs[which][...]


def ffn_far_kernel(number, slots_d, slots_u, normed, acc_in, b_up, *refs):
    ups, downs = refs[:PIECES], refs[PIECES : 2 * PIECES]
    active, slope, acc, low, w_up, w_down = refs[2 * PIECES :]
    step = pl.program_id(0)

    @pl.when(step == 0)
    def _():
        acc[...] = acc_in[...]

    gather_rows(w_up, slots_u, ups)
    gather_down(w_down, step, slots_d, downs)
    hidden = dot(normed[...], w_up[...]) + b_up[number : number + 1]
    value, back = gelu_pair(hidden)
    value = value.astype(bf16)
    active[...] = value
    slope[...] = back.astype(bf16)
    acc[...] += dot(value, w_down[...])

    @pl.when(step == pl.num_programs(0) - 1)
    def _():
        low[...] = acc[...].astype(bf16)


def ffn_far_call(number, normed, acc, up_far, down_far, b_up, units, after=()):
    rows, width = normed.shape
    block = 2 * units // PIECES
    ups, downs, at, prefetch = far_ffn_operands(up_far, down_far, width, units)
    wide = spec((rows, block), lambda i, *s: (0, at(i, s[0])))
    full = spec((rows, width))
    return call(
        "ffn_far",
        functools.partial(ffn_far_kernel, number),
        2,
        [
            hot(normed) if number else whole(normed),
            hot(acc) if number else whole(acc),
            (b_up, spec((b_up.shape[0], block), lambda i, *s: (0, at(i, s[0])))),
            *ups,
            *downs,
        ],
        [
            ((rows, units), bf16, wide),
            ((rows, units), bf16, wide),
            ((rows, width), f32, full),
            ((rows, width), bf16, full),
        ],
        prefetch=prefetch,
        scratch=(pltpu.VMEM((width, block), bf16), pltpu.VMEM((block, width), bf16)),
        after=after,
    )


def split_rows(product, keep, send, at):
    half = product.shape[0] // 2
    product = product.astype(bf16)
    keep[at] = product[:half]
    send[at] = product[half:]


def ffn_back_kernel(slots_d, slots_u, *refs):
    (g, n_t, g_t, active_n, slope_n, up_n, down_n, active_o, slope_o) = refs[:9]
    ups, downs = refs[9 : 9 + PIECES], refs[9 + PIECES : 9 + 2 * PIECES]
    acc, keep, send, b_up, up_o, down_o = refs[9 + 2 * PIECES :]
    step = pl.program_id(0)

    @pl.when(step == 0)
    def _():
        acc[...] = jnp.zeros_like(acc)

    def one(active, slope, w_up, w_down):
        grad_active = dot_nt(g[...], w_down)
        grad_hidden = (grad_active * slope[...].astype(f32)).astype(bf16)
        b_up[0] = column_sum(grad_hidden.astype(f32))
        acc[...] += dot_nt(grad_hidden, w_up)
        for which, product in enumerate(
            (dot(n_t[...], grad_hidden), dot(g_t[...], active[...]))
        ):
            block = product.shape[1] // 2
            for place in range(2):
                split_rows(
                    product[:, place * block : (place + 1) * block], keep, send, (0, which, place)
                )

    @pl.when(step < 2)
    def _():
        gather_rows(up_o, slots_u, ups)
        gather_down(down_o, step, slots_d, downs)
        one(active_o, slope_o, up_o[...], down_o[...])

    @pl.when(step >= 2)
    def _():
        one(active_n, slope_n, up_n[0], down_n[0])


def ffn_back_call(
    number, g, n_t, g_t, near, distant, w_up, w_down, up_far, down_far, after=(), sides=()
):
    rows, width = g.shape
    units = w_up.shape[2]
    block = 2 * units // PIECES
    ups, downs, at, prefetch = far_ffn_operands(up_far, down_far, width, units)

    def near_block(i):
        return jnp.maximum(i - 2, 0)

    def result_block(i, s):
        return jnp.where(i < 2, at(i, s[0]), near_block(i))

    def side(i):
        return jnp.where(i < 2, 1, 0)

    near_wide = spec((rows, block), lambda i, *s: (0, near_block(i)))
    far_wide = spec((rows, block), lambda i, *s: (0, at(i, s[0])))
    grads = spec(
        (1, 2, 2, width // 2, block // 2), lambda i, *s: (side(i), 0, result_block(i, s), 0, 0)
    )
    grads_shape = (2, 2, PIECES, width // 2, block // 2)
    return call(
        "ffn_back",
        ffn_back_kernel,
        4,
        [
            hot(g),
            whole(n_t),
            hot(g_t),
            *[(array, near_wide) for array in near],
            (w_up, spec((1, width, block), lambda i, *s: (number, 0, near_block(i)))),
            (w_down, spec((1, block, width), lambda i, *s: (number, near_block(i), 0))),
            *[(array, far_wide) for array in distant],
            *ups,
            *downs,
        ],
        [
            ((rows, width), f32, spec((rows, width)), True),
            (grads_shape, bf16, grads),
            (grads_shape, bf16, grads),
            ((2, 1, units), f32,
             spec((1, 1, block), lambda i, *s: (side(i), 0, result_block(i, s)))),
        ],
        prefetch=prefetch,
        scratch=(pltpu.VMEM((width, block), bf16), pltpu.VMEM((block, width), bf16)),
        after=after,
        sides=sides,
    )


def middle_back_kernel(number, slots, acc, middle, gain, g, wo_n, *refs):
    wo_pieces, refs = refs[: 2 * PIECES], refs[2 * PIECES :]
    turn, grad_middle, grad_att, low_t, smalls, wo_o, low = refs
    step = pl.program_id(0)
    part = wo_o.shape[0]

    @pl.when(step == 0)
    def _():
        below, d_gain, d_bias = norm_backward(middle[...], gain[number : number + 1], acc[...])
        total = below + g[...].astype(f32)
        grad_middle[...] = total
        low[...] = total.astype(bf16)
        smalls[0:1] = d_gain
        smalls[1:2] = d_bias
        smalls[2:3] = column_sum(total)

    @pl.when(step == 1)
    def _():
        gather_out(wo_o, slots, wo_pieces)
        grad_att[:, :part] = dot_nt(low[...], wo_n[0]).astype(bf16)
        grad_att[:, part:] = dot_nt(low[...], wo_o[...]).astype(bf16)

    @pl.when(step == 2)
    def _():
        low_t[...] = dot_nt(turn[...], low[...]).astype(bf16)


def middle_back_call(number, acc, middle, gain, g, w_out, heads_far, turn, after=(), sides=()):
    rows, width = acc.shape
    part = w_out.shape[1]
    slots, pieces, row = heads_far
    return call(
        "middle_back",
        functools.partial(middle_back_kernel, number),
        3,
        [
            hot(acc),
            *[whole(array) for array in (middle, gain, g)],
            (w_out, spec((1, part, width), lambda i, *s: (number, 0, 0))),
            *out_operands(pieces, part, row),
            hot(turn),
        ],
        [
            ((rows, width), f32, spec((rows, width))),
            ((rows, width), bf16, spec((rows, width)), True),
            ((width, rows), bf16, spec((width, rows)), True),
            ((3, width), f32, spec((3, width))),
        ],
        prefetch=(slots,),
        scratch=(pltpu.VMEM((part, width), bf16), pltpu.VMEM((rows, width), bf16)),
        after=after,
        sides=sides,
    )


def qkv_back_kernel(number, weight, rows_grad, *refs):
    refs = list(refs)
    slots = (refs.pop(0), refs.pop(0)) if rows_grad else None
    gq, kv, kv_far, cosine, sine = refs[:5]
    refs = refs[5:]
    if weight:
        n_t, gm_t, att, *refs = refs
    if rows_grad:
        w_n, *refs = refs
        pieces, refs = refs[: 3 * PIECES], refs[3 * PIECES :]
        x, gain, g, *refs = refs
        if number:
            turn, *refs = refs
    if weight:
        keep, send, b, *refs = refs
    if rows_grad:
        acc, low, *refs = refs
        if number:
            low_t, *refs = refs
        smalls, matrix, *refs = refs
    (mixed,) = refs
    step = pl.program_id(0)
    part = gq.shape[1]

    def lanes(member):
        return slice(member * part, (member + 1) * part)

    mixed[:, lanes(0)] = gq[...]
    keys = rotate(
        kv[0].astype(f32) + kv_far[0].astype(f32), cosine[...], sine[...], -1.0
    )
    mixed[:, lanes(1)] = keys.astype(bf16)
    mixed[:, lanes(2)] = plus(kv[1], kv_far[1])
    if weight:
        sums = column_sum(mixed[...].astype(f32))
        product = dot(n_t[...], mixed[...])
        for member in range(3):
            b[0, member] = sums[:, lanes(member)]
            split_rows(product[:, lanes(member)], keep, send, (0, member))
        split_rows(dot(gm_t[...], att[...]), keep, send, (0, 3))
    if rows_grad:

        @pl.when(step == 0)
        def _():
            for member in range(3):
                matrix[:, lanes(member)] = w_n[0, member]
            acc[...] = dot_nt(mixed[...], matrix[...])

        @pl.when(step == 1)
        def _():
            for member in range(3):
                gather_rows(
                    matrix, slots[min(member, 1)], pieces[member * PIECES :][:PIECES],
                    member * part,
                )
            whole_grad = acc[...] + dot_nt(mixed[...], matrix[...])
            below, d_gain, d_bias = norm_backward(
                x[...].astype(f32), gain[number : number + 1], whole_grad
            )
            total = below + g[...]
            acc[...] = total
            low[...] = total.astype(bf16)
            if number:
                low_t[...] = dot_nt(turn[...], low[...]).astype(bf16)
            smalls[0:1] = d_gain
            smalls[1:2] = d_bias
            smalls[2:3] = column_sum(total)


def qkv_back_call(
    number, gq, kv, kv_far, tables, sources=None, weights=None, ending=None, after=()
):
    rows = gq.shape[0]
    part = gq.shape[1] // 2
    width = 2 * part
    column = spec((rows, part), lambda i, *s: (0, i))
    both = spec((2, rows, part), lambda i, *s: (0, 0, i))
    operands = [(gq, column, True), (kv, both, True), (kv_far, both, True), *[hot(table) for table in tables]]
    results, prefetch, scratch = [], (), []
    if sources is not None:
        n_t, gm_t, att = sources
        operands += [whole(n_t), hot(gm_t), (att, column)]
        grads = spec((1, 4, width // 2, part), lambda i, *s: (i, 0, 0, 0))
        results += [((2, 4, width // 2, part), bf16, grads)] * 2
        results.append(
            ((2, 3, 1, part), f32, spec((1, 3, 1, part), lambda i, *s: (i, 0, 0, 0)))
        )
    if weights is not None:
        w_n, members = weights
        prefetch = (members[0][0], members[1][0])
        operands.append((w_n, spec((1, 3, width, part), lambda i, *s: (number, 0, 0, 0))))
        operands += [
            (piece, spec((width // PIECES, part), lambda i, *s, lead=lead: (lead, 0)), True)
            for _, pieces, lead in members
            for piece in pieces
        ]
        x, gain, g, turn = ending
        operands += [whole(x), whole(gain), whole(g)]
        results += [
            ((rows, width), f32, spec((rows, width))),
            ((rows, width), bf16, spec((rows, width)), True),
        ]
        if number:
            operands.append(hot(turn))
            results.append(((width, rows), bf16, spec((width, rows)), True))
        results.append(((3, width), f32, spec((3, width))))
        scratch.append(pltpu.VMEM((width, 3 * part), bf16))
    scratch.append(pltpu.VMEM((rows, 3 * part), bf16))
    return call(
        "qkv_back",
        functools.partial(qkv_back_kernel, number, sources is not None, weights is not None),
        2,
        operands,
        results,
        prefetch=prefetch,
        scratch=scratch,
        after=after,
    )


def pack_call(number, slots, groups, after=()):
    operands, results, entries = [], [], []
    for which, matrices in groups:
        rows, places = 0, []
        matrices = [entry if isinstance(entry, tuple) else (entry, (0,)) for entry in matrices]
        lanes = matrices[0][0].shape[-1]
        for matrix, members in matrices:
            chunk, sides = matrix.shape[-2] // PIECES, matrix.shape[-1] // lanes
            middle = matrix.shape[1:-2]
            zeros = (0,) * len(middle)
            operands.append((
                matrix,
                spec(
                    (1, *middle, chunk, matrix.shape[-1]),
                    lambda i, *s, which=which, zeros=zeros: (number, *zeros, s[which][0], 0),
                ),
            ))
            places.append((rows, members, chunk, sides))
            rows += len(members) * chunk * sides
        results.append(((rows, lanes), bf16, spec((rows, lanes))))
        entries.append((places, lanes))

    def kernel(*refs):
        refs = refs[len(slots) :]
        outs = refs[len(operands) :]
        at = 0
        for out, (places, lanes) in zip(outs, entries):
            for row, members, chunk, sides in places:
                source = refs[at]
                at += 1
                for place, member in enumerate(members):
                    for side in range(sides):
                        cut = slice(side * lanes, (side + 1) * lanes)
                        start = row + (place * sides + side) * chunk
                        if len(source.shape) == 4:
                            piece = source[0, member, :, cut]
                        else:
                            piece = source[0, :, cut]
                        out[start : start + chunk] = piece

    return call("pack", kernel, 1, operands, results, prefetch=slots, after=after, token=True)


def plus(a, b):
    return (a.astype(f32) + b.astype(f32)).astype(bf16)


def join_ffn_kernel(keep, got, a_keep, a_send, b_keep, b_send):
    half = b_keep.shape[2]
    for place in range(a_keep.shape[0]):
        a_keep[place] = plus(keep[0, 0, place], got[0, 0, place])
        a_send[place] = plus(keep[1, 0, place], got[1, 0, place])
        for side in range(2):
            b_keep[side, place] = plus(keep[side, 1, place, :half], got[side, 1, place, :half])
            b_send[side, place] = plus(keep[side, 1, place, half:], got[side, 1, place, half:])


def join_ffn_call(keep, got, after=()):
    deep, cols = keep.shape[3:]
    source = spec((2, 2, 1, deep, cols), lambda i, *s: (0, 0, i, 0, 0))
    one = ((PIECES, deep, cols), bf16, spec((1, deep, cols), lambda i, *s: (i, 0, 0)))
    two = (
        (2, PIECES, deep // 2, cols), bf16,
        spec((2, 1, deep // 2, cols), lambda i, *s: (0, i, 0, 0)),
    )
    return call(
        "join_ffn", join_ffn_kernel, PIECES, [(keep, source), (got, source, True)],
        [one, one, two, two], after=after, token=True,
    )


def join_attention_kernel(keep, got, a_keep, a_send, b_keep, b_send):
    half = b_keep.shape[2]
    for member in range(2):
        a_keep[member] = plus(keep[0, member], got[0, member])
        a_send[member] = plus(keep[1, member], got[1, member])
        for side in range(2):
            kept, came = keep.at[side, 2 + member], got.at[side, 2 + member]
            b_keep[side, member] = plus(kept[:half], came[:half])
            b_send[side, member] = plus(kept[half:], came[half:])


def join_line_kernel(keep, got, next_keep, next_send):
    half, quarter = keep.shape[2] // 2, next_keep.shape[2]
    for side in range(2):
        for member in range(4):
            for x in range(2):
                for start, ref in ((x * half, next_keep), (x * half + quarter, next_send)):
                    cut = slice(start, start + quarter)
                    ref[4 * side + member, x] = plus(
                        keep[side, member, cut], got[side, member, cut]
                    )


def cut_kernel(keep, got, next_keep, next_send):
    for member in range(keep.shape[0]):
        next_keep[member] = plus(keep[member, 0], got[member, 0])
        next_send[member] = plus(keep[member, 1], got[member, 1])


def inner_kernel(keep, got, next_keep, next_send):
    half = next_keep.shape[2]
    for member in range(keep.shape[0]):
        for x in range(2):
            next_keep[member, x] = plus(keep[member, x, :half], got[member, x, :half])
            next_send[member, x] = plus(keep[member, x, half:], got[member, x, half:])


def sum_kernel(keep, got, out):
    for member in range(keep.shape[0]):
        out[member] = plus(keep[member], got[member])


def turn_kernel(a_keep, a_got, b_keep, b_got, a_next, a_send, b_next, b_send):
    half = a_next.shape[1]
    for member in range(a_keep.shape[0]):
        a_next[member] = plus(a_keep[member, :half], a_got[member, :half])
        a_send[member] = plus(a_keep[member, half:], a_got[member, half:])
    for member in range(b_keep.shape[1]):
        b_next[member] = plus(b_keep[0, member], b_got[0, member])
        b_send[member] = plus(b_keep[1, member], b_got[1, member])


def merge_kernel(*refs):
    keep, send = refs[-2:]
    half = keep.shape[1]
    place = 0
    for kept, got in zip(refs[:-2:2], refs[1:-2:2]):
        for member in range(kept.shape[0]):
            keep[place] = plus(kept[member, :half], got[member, :half])
            send[place] = plus(kept[member, half:], got[member, half:])
            place += 1


def part_kernel(first, keep, got, near, distant):
    for place in range(4):
        near[place] = plus(keep[first + place], got[first + place])
        distant[place] = plus(keep[first + 4 + place], got[first + 4 + place])


def add_kernel(a, b, out):
    out[...] = a[...] + b[...]


def sums_call(name, *sides, after=(), token=False):
    return call(name, None, 3, [], [], after=after, sides=sides, token=token)


def emit_call(ffn, attention):
    depth = len(ffn)
    terms = [array for _, arrays in ffn + attention for array in arrays]
    chunk, part = terms[0].shape[1:]
    shapes = [
        (depth, chunk, PIECES * part), (depth, chunk, PIECES * part),
        (depth, 3, chunk, part), (depth, chunk, part),
    ]

    def kernel(*refs):
        up, down, qkv, out = refs[len(terms) :]
        at = 0
        for number, (first, arrays) in enumerate(ffn):
            here = refs[at : at + len(arrays)]
            at += len(arrays)
            for place in range(2 * PIECES):
                total = sum(term[first + place].astype(f32) for term in here)
                start = place % PIECES * part
                (up, down)[place // PIECES][number, :, start : start + part] = total
        for number, (first, arrays) in enumerate(attention):
            here = refs[at : at + len(arrays)]
            at += len(arrays)
            for member in range(4):
                total = sum(term[first + member].astype(f32) for term in here)
                if member < 3:
                    qkv[number, member] = total
                else:
                    out[number] = total

    return call(
        "emit", kernel, 1, [whole(term) for term in terms],
        [(shape, f32, spec(shape)) for shape in shapes], token=True,
    )


def widen_call(arrays, after=()):
    def kernel(*refs):
        for source, out in zip(refs[: len(arrays)], refs[len(arrays) :]):
            out[...] = source[...].astype(f32)

    rows, width = arrays[0].shape
    block = spec((rows // 4, width), lambda i, *s: (i, 0))
    return call(
        "widen", kernel, 4, [(array, block, True) for array in arrays],
        [((rows, width), f32, block) for _ in arrays], after=after,
    )


def share_call(low, head, ids, class_bins, after):
    high = lax.Precision.HIGHEST

    def kernel(low, head, ids, class_bins, out):
        logits = dot_nt(low[...], head[...])
        expos = jnp.exp(logits - jnp.max(logits, axis=-1, keepdims=True))
        shares = expos / jnp.sum(expos, axis=-1, keepdims=True)
        mask = (ids[:, : low.shape[0]] >= special_ids).astype(f32)
        sums = jnp.dot(mask, shares, precision=high, preferred_element_type=f32)
        bins = lax.broadcasted_iota(jnp.int32, (LANES, class_bins.shape[1]), 0)
        table = (bins == class_bins[...]).astype(f32)
        totals = lax.dot_general(
            jnp.broadcast_to(sums, (8, sums.shape[1])), table, (((1,), (1,)), ((), ())),
            precision=high, preferred_element_type=f32,
        )[0:1]
        lane = lax.broadcasted_iota(jnp.int32, (1, LANES), 1)
        out[...] = jnp.where(lane == BINS, jnp.sum(mask), jnp.where(lane < BINS, totals, 0.0))

    args = (low, head, ids, class_bins)
    return call(
        "share", kernel, 1, [whole(array) for array in args],
        [((1, LANES), f32, spec((1, LANES)))], after=(after,),
    )[0]


def pack_small(layers, bin_row, width):
    count = len(layers)
    part, units = layers[0][3].shape[3], layers[0][4].shape[2]
    folds = units // width
    shared = 6 * count + 1
    total = shared + count * (3 + folds)
    args = [array for layer in layers for array in layer] + [bin_row]

    def kernel(*refs):
        own, other = refs[-1].at[0], refs[-1].at[1]
        own[...] = jnp.zeros((total, width), f32)
        for number in range(count):
            one, two, down, _, _ = refs[5 * number : 5 * number + 5]
            own[6 * number : 6 * number + 2] = one[0:2]
            own[6 * number + 2 : 6 * number + 5] = two[...]
            own[6 * number + 5 : 6 * number + 6] = down[down.shape[0] - 1 :]
        bins = refs[5 * count]
        own[6 * count : 6 * count + 1, : bins.shape[1]] = bins[...]
        other[...] = own[...]
        for number in range(count):
            qkv, up = refs[5 * number + 3 : 5 * number + 5]
            start = shared + number * (3 + folds)
            for side, out in enumerate((own, other)):
                for member in range(3):
                    out[start + member : start + member + 1, :part] = qkv[side, member]
                for fold in range(folds):
                    row = start + 3 + fold
                    out[row : row + 1] = up[side, :, fold * width : (fold + 1) * width]

    shape = (2, total, width)
    return call(
        "pack_small", kernel, 1, [whole(array) for array in args], [(shape, f32, spec(shape))]
    )[0]


def unpack_small(terms, count, part, units, after=()):
    width = terms[0].shape[1]
    folds = units // width
    shared = 6 * count + 1

    def kernel(*refs):
        outs = refs[len(terms) :]
        sums = sum(term[...] for term in refs[: len(terms)])
        qkv, up, bins, tokens = outs[6:]
        for number in range(count):
            for member in range(6):
                row = 6 * number + member
                outs[member][number : number + 1] = sums[row : row + 1]
            start = shared + number * (3 + folds)
            for member in range(3):
                row = start + member
                qkv[member, number : number + 1] = sums[row : row + 1, :part]
            for fold in range(folds):
                row = start + 3 + fold
                up[number : number + 1, fold * width : (fold + 1) * width] = sums[row : row + 1]
        row = sums[6 * count : 6 * count + 1, :LANES]
        tally = row[:, BINS : BINS + 1]
        bins[...] = (BINS * row / jnp.maximum(tally, 1.0))[:, :BINS]
        tokens[...] = tally.astype(jnp.int32)

    shapes = [((count, width), f32)] * 6 + [
        ((3, count, part), f32), ((count, units), f32), ((1, BINS), f32), ((1, 1), jnp.int32)
    ]
    outs = call(
        "unpack_small", kernel, 1, [hot(term) for term in terms],
        [(shape, dtype, spec(shape)) for shape, dtype in shapes], after=after,
    )
    return outs[:6], outs[6], outs[7], outs[8], outs[9]


def segment_info(seq_lengths, total):
    ends = jnp.cumsum(seq_lengths)
    places = jnp.arange(total, dtype=jnp.int32)
    labels = jnp.sum((places[:, None] >= ends[None, :-1]).astype(jnp.int32), axis=1)
    starts = ends - seq_lengths
    picks = labels[:, None] == jnp.arange(seq_lengths.shape[0], dtype=jnp.int32)[None, :]
    begin = jnp.sum(jnp.where(picks, starts[None, :], 0), axis=1)
    return (labels, places - begin)


def moves(dp_size, tensor_size):
    def flat(dp, tensor):
        return dp * tensor_size + tensor

    every = [(dp, tensor) for dp in range(dp_size) for tensor in range(tensor_size)]

    def by(target):
        return [(flat(*where), flat(*target(*where))) for where in every]

    return {
        "swap": by(lambda dp, tensor: (dp - dp % 2 + tensor, dp % 2)),
        "y": by(lambda dp, tensor: (dp, 1 - tensor)),
        "z": by(lambda dp, tensor: (dp ^ 12 if dp_size > 8 else dp, tensor)),
        "bits": [
            by(lambda dp, tensor, bit=bit: (dp ^ bit, tensor))
            for bit in (1 << place for place in range(dp_size.bit_length() - 1))
        ],
    }


def per_device(
    x_in,
    lengths,
    token_ids,
    ln1_gain,
    ln1_bias,
    w_qkv,
    b_qkv,
    w_out,
    b_out,
    ln2_gain,
    ln2_bias,
    w_up,
    b_up,
    w_down,
    b_down,
    head,
    class_bins,
    cotangent,
):
    rows, width = x_in.shape
    dp_size = lax.axis_size("dp")
    tensor_size = lax.axis_size("tensor")
    depth = w_qkv.shape[0]
    part = w_qkv.shape[3]
    units = w_up.shape[2]
    total = rows * tensor_size
    dp = lax.axis_index("dp")
    core = dp % 2
    bits = dp_size.bit_length() - 1
    move = moves(dp_size, tensor_size)

    def send(array, name):
        return lax.ppermute(array, AXES, move["bits"][name] if isinstance(name, int) else move[name])

    w_qkv = jnp.transpose(w_qkv, (0, 2, 1, 3))
    z_bit = min(2, bits - 1)

    def slots_of(bit):
        own = ((dp >> bit) % 2) * 2 + core
        return jnp.stack([own, own ^ 2, own ^ 1, own ^ 3]).astype(jnp.int32)

    all_slots = (slots_of(1), slots_of(z_bit))

    class Bundle:
        def __init__(self, way, packed):
            self.way, self.packed = way, packed

        def begin(self, *tokens):
            packed = gate(self.packed, tokens) if tokens else self.packed
            self.got = send(packed, "y")
            return packed

        def hop(self, *tokens):
            if tokens:
                self.got = gate(self.got, tokens)
            self.beside = send(self.got, (1, z_bit)[self.way])
            self.across = send(self.got, 0)
            return self.got

        def end(self, *tokens):
            beside = gate(self.beside, tokens) if tokens else self.beside
            pieces = [self.got, beside, self.across, send(beside, 0)]
            self.far = (all_slots[self.way], pieces)
            return beside

    chunk_rows = width // PIECES
    _, packed = pack_call(0, all_slots, [(0, ((w_qkv, (1, 2)),))])
    key_bundle = Bundle(0, packed)
    key_bundle.begin()
    key_bundle.hop()
    x_low = gate(x_in.astype(bf16), (packed,))
    stream = send(x_low, "swap")
    numbers = send(gate(jnp.concatenate([token_ids, lengths[0]]), (packed,)), "swap")
    seq_lengths = numbers[rows:]
    far_biases = send(
        gate(jnp.concatenate([b_up, b_qkv.reshape(depth, -1)], axis=1), (packed,)), "y"
    )
    b_qkv = jnp.transpose(b_qkv, (1, 0, 2))
    cotangent_low = cotangent.astype(bf16)
    heads, ups, downs = [], [], []

    def pack_layer(number, after):
        members = (0, 1, 2) if number else (0,)
        mark, *arrays = pack_call(
            number, all_slots,
            [(1, ((w_qkv, members), w_out)), (0, (w_up,)), (1, (w_down,))], after,
        )
        for store, way, array in zip((heads, ups, downs), (1, 0, 1), arrays):
            store.append(Bundle(way, array))
        return mark

    pack_layer(0, (packed, x_low, cotangent_low))
    wait = tuple(pack_layer(number, (key_bundle.got,)) for number in range(1, depth))
    heads[0].begin(key_bundle.got)
    ups[0].begin(heads[0].got)

    def far_heads(number):
        if number:
            return [(*heads[number].far, member) for member in range(3)]
        return [(*heads[0].far, 0), (*key_bundle.far, 0), (*key_bundle.far, 1)]

    def far_out(number):
        return (*heads[number].far, (3 if number else 1) * chunk_rows)


    labels, places = segment_info(seq_lengths, total)
    labels_here = lax.dynamic_slice_in_dim(labels, core * rows, rows, 0)
    labels_far = lax.dynamic_slice_in_dim(labels, (1 - core) * rows, rows, 0)
    places_here = lax.dynamic_slice_in_dim(places, core * rows, rows, 0)
    lane = jnp.arange(LANES, dtype=jnp.int32)[None, :]
    freqs = theta ** (-(lane % HALF).astype(f32) / HALF)
    angles = places_here.astype(f32)[:, None] * freqs
    sine = jnp.sin(angles)
    tables = (jnp.cos(angles), jnp.where(lane % HEAD_DIM < HALF, -sine, sine))
    place = lane % HEAD_DIM
    q_mark = jnp.where(labels_here[:, None] == place, far, 0.0).astype(bf16)

    def key_mark(own):
        other = (own[:, None] != place) & (place < 3)
        return jnp.where(other, 1.0, jnp.where((place >= 3) & (place < 6), -1.0, 0.0)).astype(bf16)

    marks = (q_mark, key_mark(labels_here), key_mark(labels_far))
    chunk = width // dp_size
    order = jnp.arange(width, dtype=jnp.int32)
    block, inside = order // chunk, order % chunk
    home = sum(
        (((block >> (bits - 1 - place)) & 1) << place) for place in range(bits)
    )
    order = (home ^ dp) * chunk + inside
    turn = (order[:, None] == jnp.arange(width, dtype=jnp.int32)[None, :]).astype(bf16)

    def turned(array):
        return lax.dot_general(turn, array, (((1,), (1,)), ((), ())), preferred_element_type=bf16)

    saved = []
    for number in range(depth):
        more = number + 1 < depth
        normed_attn, n_t_attn, q, kv = qkv_call(
            number, (0, 1, 2), stream, (ln1_gain, ln1_bias, turn), w_qkv, b_qkv, tables,
            after=wait,
        )
        if number == 0:
            key_bundle.end()
            wait = (heads[0].hop(kv),)
        else:
            wait = ()
        key_far = (*key_bundle.far, 0) if number == 0 else far_heads(number)[1]
        (kv,) = qkv_call(
            number, (1, 2), normed_attn, None, key_far, far_biases, tables, (kv,), wait
        )
        kv_far = send(kv, 0)
        wait = ()
        if number == 0:
            heads[0].end(kv)
            wait = (ups[0].hop(kv), downs[0].begin(ups[0].got, kv))
        (q,) = qkv_call(
            number, (0,), normed_attn, None, far_heads(number)[0], far_biases, tables, (q,),
            (kv, *wait),
        )
        wait = (downs[number].hop(q),) if number else ()
        if not more:
            late = gate(cotangent_low, (downs[number].got, q))
            pairs_apart = [pair for pair in move["swap"] if pair[0] != pair[1]]
            grad_stream = lax.ppermute(late, AXES, pairs_apart)
            wait += (late,)
        att, logsum = attention_call(q, kv, kv_far, marks, wait)
        if number == 0:
            wait = (ups[0].end(att), downs[0].hop(att))
        else:
            wait = (ups[number].end(att), downs[number].end(att))
        if more:
            wait += (heads[number + 1].begin(downs[number].got, att),)
        middle, normed_ffn, n_t_ffn, active, slope, acc = ffn_call(
            number, stream, att, w_out, far_out(number), (b_out, ln2_gain, ln2_bias, b_down),
            turn, w_up, b_up, w_down, wait,
        )
        wait = (downs[0].end(acc),) if number == 0 else ()
        if more:
            wait += (heads[number + 1].hop(acc), ups[number + 1].begin(heads[number + 1].got, acc))
        up_far, down_far = ups[number].far, downs[number].far
        active_o, slope_o, below, low = ffn_far_call(
            number, normed_ffn, acc, up_far, down_far, far_biases, units, wait
        )
        if more:
            wait = (
                heads[number + 1].end(low),
                ups[number + 1].hop(low),
                downs[number + 1].begin(ups[number + 1].got, low),
            )
        saved.append(
            (stream, n_t_attn, (q, kv, kv_far), logsum, att, middle, n_t_ffn,
             (active, slope), (active_o, slope_o))
        )
        stream = below
    out_low = send(low, "swap")
    stays = core == lax.axis_index("tensor")
    grad_stream = jnp.where(stays, cotangent_low, gate(grad_stream, (low,)))
    half = width // 2
    quarter, eighth = half // 2, half // 4

    def pairs(*steps):
        return tuple(array for keep, sent, way in steps for array in (keep, send(sent, way)))

    def join_attention(*arrays):
        shapes = ((2, half, part),) * 2 + ((2, 2, quarter, part),) * 2
        return join_attention_kernel, arrays, shapes

    def join_line(*arrays):
        return join_line_kernel, arrays, ((8, 2, eighth, part),) * 2

    def inner(keep, sent, way):
        members, _, deep, cols = keep.shape
        return inner_kernel, pairs((keep, sent, way)), ((members, 2, deep // 2, cols),) * 2

    def final(keep, sent, way):
        return sum_kernel, pairs((keep, sent, way)), (keep.shape,)

    def cut(keep, sent, way):
        members, _, deep, cols = keep.shape
        return cut_kernel, pairs((keep, sent, way)), ((members, deep, cols),) * 2

    def turn_ways(joined):
        a_keep, a_send, b_keep, b_send = joined
        members, deep, cols = a_keep.shape
        shape_a, shape_b = (members, deep // 2, cols), b_keep.shape[1:]
        arrays = pairs((a_keep, a_send, "y"), (b_keep, b_send, 1))
        return turn_kernel, arrays, (shape_a, shape_a, shape_b, shape_b)

    def merge(*steps):
        members = sum(keep.shape[0] for keep, _, _ in steps)
        _, deep, cols = steps[0][0].shape
        return merge_kernel, pairs(*steps), ((members, deep // 2, cols),) * 2

    def merge_ways(turned):
        a_keep, a_send, b_keep, b_send = turned
        return merge((a_keep, a_send, 1), (b_keep, b_send, "y"))

    def part_sides(keep, sent, way):
        return (
            functools.partial(part_kernel, 0), pairs((keep, sent, way)),
            ((4,) + keep.shape[1:],) * 2,
        )

    def add_small(array, other, way):
        return add_kernel, (array, send(other, way)), (shaped(array.shape, f32),)

    def halves_small(both):
        def kernel(both, got, out):
            out[...] = both[0] + got[...]

        return kernel, (both, send(both[1], "y")), (shaped(both.shape[1:], f32),)

    def plain_sum(keep, got):
        total = plus(keep, got)
        total = plus(total[0], send(total[1], "y"))
        for bit in range(1, bits):
            rows_left = total.shape[-2] // 2
            total = plus(total[..., :rows_left, :], send(total[..., rows_left:, :], bit))
        return total.astype(f32)

    placed = bits == 4 and depth == 2
    pieces = [None] * depth
    plain = [None] * depth
    grad_low = grad_stream
    g_t = turned(grad_low)
    grad_b_down = column_sum(grad_stream.astype(f32))
    for number in reversed(range(depth)):
        stream, n_t_attn, keyed, logsum, att, middle, n_t_ffn, near, distant = saved[number]
        top, last = number == depth - 1, number == 0
        acc, ffn_k, ffn_s, d_b_up = ffn_back_call(
            number, grad_low, n_t_ffn, g_t, near, distant, w_up, w_down,
            ups[number].far, downs[number].far,
        )
        ffn_g = send(ffn_s, 0)
        sides = []
        if placed and not top:
            sides = [turn_ways(joined_ffn), join_line(qkv_k, qkv_g)]
        after = ()
        if last:
            bin_row = share_call(low, jnp.transpose(head), numbers[None], class_bins[None], d_b_up)
            after = (bin_row,)
        grad_middle, grad_att, gm_t, smalls_two, *more = middle_back_call(
            number, acc, middle, ln2_gain, grad_stream, w_out, far_out(number), turn,
            sides=sides, after=after,
        )
        if more:
            turned_ffn, lined = more
        after = ()
        if placed and last:
            mark, *joined_low = join_ffn_call(ffn_k, ffn_g, (smalls_two,))
            after = (mark,)
        gq, gkv, gkv_s = attention_back_call(
            *keyed, marks, logsum, att, grad_att, tables, after=after
        )
        gkv_g = send(gkv_s, 0)
        after = ()
        if placed and not last:
            mark, *joined_ffn = join_ffn_call(ffn_k, ffn_g, (gkv_s,))
            after = (mark,)
        elif placed:
            mark, merged_ffn, lined, turned_low = sums_call(
                "merge_above", merge_ways(turned_ffn), inner(*lined, z_bit), turn_ways(joined_low),
                after=(gkv_s,), token=True,
            )
            after = (mark,)
        weights, ending = (w_qkv, far_heads(number)), (stream, ln1_gain, grad_middle, turn)
        if placed and last:
            qkv_k, qkv_s, d_b_qkv = qkv_back_call(
                number, gq, gkv, gkv_g, tables, (n_t_attn, gm_t, att), after=after
            )
            qkv_g = send(qkv_s, 0)
            grad_stream, grad_low, smalls_one = qkv_back_call(
                number, gq, gkv, gkv_g, tables, None, weights, ending, after=(d_b_qkv,)
            )
        else:
            qkv_k, qkv_s, d_b_qkv, grad_stream, grad_low, *g_t, smalls_one = qkv_back_call(
                number, gq, gkv, gkv_g, tables, (n_t_attn, gm_t, att), weights, ending, after=after
            )
            g_t = g_t[0] if g_t else None
            qkv_g = send(qkv_s, 0)
        if not placed:
            plain[number] = (plain_sum(ffn_k, ffn_g), plain_sum(qkv_k, qkv_g))
        pieces[number] = (smalls_one, smalls_two, grad_b_down, d_b_qkv, d_b_up)
        grad_b_down = smalls_one
    grad_x_low = send(grad_low, "swap")
    both = pack_small(pieces, bin_row, width)
    if placed:
        joined_att, merged_low, ended_above, lined = sums_call(
            "tail_one", join_attention(qkv_k, qkv_g), merge_ways(turned_low),
            merge((*merged_ffn, z_bit)), cut(*lined, 3), after=(both,),
        )
        turned_att, ended_low, (both,) = sums_call(
            "tail_two", turn_ways(joined_att), merge((*merged_low, z_bit)),
            add_small(both, both, 0),
        )
        merged_att, (near_1, far_1), (sums,), (ffn_1,) = sums_call(
            "tail_three", merge_ways(turned_att), part_sides(*lined, 1), halves_small(both),
            final(*ended_above, 3),
        )
        ended_att, (ffn_0,), (sums,), (att_1,) = sums_call(
            "tail_four", merge((*merged_att, z_bit)), final(*ended_low, 3),
            add_small(sums, sums, 1), final(near_1, far_1, "y"),
        )
        out_act, grad_x = widen_call((out_low, grad_x_low), ended_att[1:2])
        terms = (sums, send(sums, 2), send(sums, 3), send(sums, "z"))
        ended_ffn = [(0, (ffn_0,)), (0, (ffn_1,))]
        ended_attention = [(0, pairs((*ended_att, 3))), (0, (att_1,))]
        mark, grad_w_up, grad_w_down, grad_w_qkv, grad_w_out = emit_call(ended_ffn, ended_attention)
        late = (mark,)
    else:
        grad_w_up, grad_w_down = (
            jnp.stack([
                jnp.concatenate([ffn[which, place] for place in range(PIECES)], axis=-1)
                for ffn, _ in plain
            ])
            for which in range(2)
        )
        grad_w_qkv = jnp.stack([entry[1][:3] for entry in plain])
        grad_w_out = jnp.stack([entry[1][3] for entry in plain])
        out_act, grad_x = widen_call((out_low, grad_x_low))
        sums = both[0] + send(both[1], "y")
        for bit in range(bits - 1):
            sums = sums + send(sums, bit)
        late = ()
        terms = (sums, send(sums, bits - 1))
    replicated, sharded_qkv, sharded_up, bin_density, count = unpack_small(
        terms, depth, part, units, late
    )

    return (
        out_act,
        grad_x,
        replicated[0],
        replicated[1],
        jnp.transpose(grad_w_qkv, (0, 2, 1, 3)),
        jnp.transpose(sharded_qkv, (1, 0, 2)),
        jnp.transpose(grad_w_out, (0, 2, 1)),
        replicated[4],
        replicated[2],
        replicated[3],
        grad_w_up,
        sharded_up,
        jnp.transpose(grad_w_down, (0, 2, 1)),
        replicated[5],
        bin_density.reshape(BINS),
        count.reshape(()),
    )


def solution(mesh):
    placed = (
        P(("dp", "tensor"), None),
        P("dp", None),
        P(("dp", "tensor")),
        P(),
        P(),
        P(None, None, None, "tensor"),
        P(None, None, "tensor"),
        P(None, "tensor", None),
        P(),
        P(),
        P(),
        P(None, None, "tensor"),
        P(None, "tensor"),
        P(None, "tensor", None),
        P(),
        P(),
        P(),
        P(("dp", "tensor"), None),
    )
    return jax.shard_map(
        per_device,
        mesh=mesh,
        in_specs=placed,
        out_specs=(
            P(("dp", "tensor"), None),
            P(("dp", "tensor"), None),
            P(),
            P(),
            P(None, "dp", None, "tensor"),
            P(None, None, "tensor"),
            P(None, "tensor", "dp"),
            P(),
            P(),
            P(),
            P(None, "dp", "tensor"),
            P(None, "tensor"),
            P(None, "tensor", "dp"),
            P(),
            P(),
            P(),
        ),
        check_vma=False,
    )
```
